32 devices in a mesh: fsdp: 2 (over x), cp: 16 (over z, y, core).
Axes of the slice: x: 2, y: 2, z: 4, core: 2. Of those that a mesh axis runs over, the one named last changes fastest.
Arguments:
- tokens: bfloat16 [4, 1024, 2048], P('fsdp', 'cp'), may hold values from -6 to 6
- cotangent: bfloat16 [4, 1024, 2048], P('fsdp', 'cp'), may hold values from -6 to 6
- attn_gain: bfloat16 [2048], P(('fsdp', 'cp')), may hold values from 0.5 to 1.5
- q_weight: bfloat16 [2048, 2048], P(('fsdp', 'cp')), may hold values from -0.125 to 0.125
- k_weight: bfloat16 [2048, 512], P(('fsdp', 'cp')), may hold values from -0.125 to 0.125
- v_weight: bfloat16 [2048, 512], P(('fsdp', 'cp')), may hold values from -0.125 to 0.125
- o_weight: bfloat16 [2048, 2048], P(('fsdp', 'cp')), may hold values from -2 to 2
- ffn_gain: bfloat16 [2048], P(('fsdp', 'cp')), may hold values from 0.5 to 1.5
- gate_weight: bfloat16 [2048, 8192], P(('fsdp', 'cp')), may hold values from -0.125 to 0.125
- up_weight: bfloat16 [2048, 8192], P(('fsdp', 'cp')), may hold values from -0.125 to 0.125
- down_weight: bfloat16 [2048, 8192], P(('fsdp', 'cp')), may hold values from -0.0625 to 0.0625
Outputs:
- block_out: bfloat16 [4, 1024, 2048], P('fsdp', 'cp')
- input_grad: bfloat16 [4, 1024, 2048], P('fsdp', 'cp')
- attn_gain_grad: float32 [2048], P(('fsdp', 'cp'))
- q_weight_grad: float32 [2048, 2048], P(('fsdp', 'cp'))
- k_weight_grad: float32 [2048, 512], P(('fsdp', 'cp'))
- v_weight_grad: float32 [2048, 512], P(('fsdp', 'cp'))
- o_weight_grad: float32 [2048, 2048], P(('fsdp', 'cp'))
- ffn_gain_grad: float32 [2048], P(('fsdp', 'cp'))
- gate_weight_grad: float32 [2048, 8192], P(('fsdp', 'cp'))
- up_weight_grad: float32 [2048, 8192], P(('fsdp', 'cp'))
- down_weight_grad: float32 [2048, 8192], P(('fsdp', 'cp'))
The draws below stay inside these ranges and needn't reach their ends.
All inputs are finite; a program needn't handle non-finite values.
Results may differ from the reference program's by a relative error of at most 0.014.
Values may be sent and summed in bfloat16 or wider, within the bound.
A program may use at most 960 MiB of HBM per device.

```python
import jax
import jax.numpy as jnp
from jax import lax

D = 2048
HEADS = 32
KV_HEADS = 8
HEAD_DIM = 64
FF = 8192
BLK = 32
SEQ_LEN = 1024
SEQS = 4
KV_WIDTH = 512
N_CP = 16


def steps_of(stream_key, shape, cuts, least, largest):
    gain = 1.0
    for dim, shards_of in cuts:
        heights = jax.random.uniform(jax.random.fold_in(jax.random.fold_in(stream_key, 6), dim), (shards_of,), jnp.float32, least / len(cuts), largest / len(cuts))
        gain = gain * jnp.repeat(jnp.exp(heights), shape[dim] // shards_of).reshape((-1,) + (1,) * (len(shape) - 1 - dim))
    return gain


def noise(key, extent, scale, bound, shards=(), kind=jnp.bfloat16):
    entries = scale * jax.random.normal(key, extent, jnp.float32)
    if shards:
        entries = entries * steps_of(key, extent, shards, -0.22, 0.18)
    return jnp.clip(entries, -bound, bound).astype(kind)


def setup_inputs(seed: int = 0) -> dict:
    key_list = jax.random.split(jax.random.key(seed), 12)
    tokens = noise(key_list[0], (SEQS, SEQ_LEN, D), 1.0, 6.0, ((0, 2), (1, 16)))
    cotangent = noise(key_list[1], (SEQS, SEQ_LEN, D), 1.0, 6.0, ((0, 2), (1, 16)))
    attn_gain = jnp.clip(1.0 + 0.1 * jax.random.normal(key_list[2], (D,), jnp.float32), 0.5, 1.5).astype(jnp.bfloat16)
    q_weight = noise(key_list[3], (D, D), D ** -0.5, 0.125, ((0, 32),))
    k_weight = noise(key_list[4], (D, KV_WIDTH), D ** -0.5, 0.125, ((0, 32),))
    v_weight = noise(key_list[5], (D, KV_WIDTH), D ** -0.5, 0.125, ((0, 32),))
    o_weight = noise(key_list[6], (D, D), (max(1, 5 * D // SEQ_LEN)) ** -0.5, 2.0, ((0, 32),))
    ffn_gain = jnp.clip(1.0 + 0.1 * jax.random.normal(key_list[7], (D,), jnp.float32), 0.5, 1.5).astype(jnp.bfloat16)
    gate_weight = noise(key_list[8], (D, FF), D ** -0.5, 0.125, ((0, 32),))
    up_weight = noise(key_list[9], (D, FF), D ** -0.5, 0.125, ((0, 32),))
    down_weight = noise(key_list[10], (D, FF), FF ** -0.5, 0.0625, ((0, 32),))
    return {"tokens": tokens, "cotangent": cotangent, "attn_gain": attn_gain, "q_weight": q_weight, "k_weight": k_weight, "v_weight": v_weight, "o_weight": o_weight, "ffn_gain": ffn_gain, "gate_weight": gate_weight, "up_weight": up_weight, "down_weight": down_weight}


NORM_EPS = 1e-05
ROPE_BASE = 500000.0
HIGHEST_PREC = lax.Precision.HIGHEST

@jax.custom_vjp
def low(v):
    return lax.optimization_barrier(v.astype(jnp.bfloat16)).astype(jnp.float32)

@jax.custom_vjp
def low_back(v):
    return v

def low_keep(v):
    return (low(v), None)

def low_pass(kept, grad):
    return (grad,)

def back_keep(v):
    return (v, None)

def back_low(kept, grad):
    return (low(grad),)
low.defvjp(low_keep, low_pass)
low_back.defvjp(back_keep, back_low)

def dealt_positions(row_ids, block_len, cp_size):
    owner = row_ids // (2 * block_len)
    within = row_ids % (2 * block_len)
    return jnp.where(within < block_len, owner * block_len + within, (2 * cp_size - 1 - owner) * block_len + within - block_len)

def rotary_tables(positions, head_width):
    half_width = head_width // 2
    freq_index = jnp.arange(half_width, dtype=jnp.float32)
    inverse = ROPE_BASE ** (-(2.0 * freq_index) / head_width)
    angle = positions.astype(jnp.float32)[:, None] * inverse[None, :]
    return (jnp.cos(angle), jnp.sin(angle))

def rotate(vector, cosine, sine):
    half_width = vector.shape[-1] // 2
    first = vector[..., :half_width]
    second = vector[..., half_width:]
    cos_wide = cosine[:, None, :]
    sin_wide = sine[:, None, :]
    return jnp.concatenate([first * cos_wide - second * sin_wide, second * cos_wide + first * sin_wide], axis=-1)

def layer(x_seq, attn_gain, q_weight, k_weight, v_weight, o_weight, ffn_gain, gate_weight, up_weight, down_weight, positions, cosine, sine):
    seq_len = x_seq.shape[0]
    group_size = HEADS // KV_HEADS
    score_scale = HEAD_DIM ** (-0.5)
    inv_one = lax.rsqrt(lax.optimization_barrier(jnp.mean(x_seq * x_seq, axis=-1, keepdims=True)) + NORM_EPS)
    attn_in = low(x_seq * inv_one * attn_gain)
    q_proj = low_back(jnp.dot(attn_in, q_weight, precision=HIGHEST_PREC))
    k_proj = low_back(jnp.dot(attn_in, k_weight, precision=HIGHEST_PREC))
    v_proj = low_back(jnp.dot(attn_in, v_weight, precision=HIGHEST_PREC))
    q_rot = low(rotate(q_proj.reshape(seq_len, HEADS, HEAD_DIM), cosine, sine)).reshape(seq_len, KV_HEADS, group_size, HEAD_DIM)
    k_rot = low(rotate(k_proj.reshape(seq_len, KV_HEADS, HEAD_DIM), cosine, sine))
    v_low = low(v_proj).reshape(seq_len, KV_HEADS, HEAD_DIM)
    query_block = 16 * BLK

    def attend(start):
        queries = lax.dynamic_slice_in_dim(q_rot, start, query_block, 0)
        places = lax.dynamic_slice_in_dim(positions, start, query_block, 0)
        raw = low_back(score_scale * jnp.einsum('qkgd,tkd->kgqt', queries, k_rot, precision=HIGHEST_PREC))
        scores = jnp.where(places[:, None] >= positions[None, :], raw, -1e+30)
        peak = lax.optimization_barrier(jnp.max(scores, axis=-1, keepdims=True))
        expo = jnp.exp(scores - peak)
        probs = low(expo / lax.optimization_barrier(jnp.sum(expo, axis=-1, keepdims=True)))
        return jnp.einsum('kgqt,tkd->qkgd', probs, v_low, precision=HIGHEST_PREC)
    starts = jnp.arange(seq_len // query_block, dtype=jnp.int32) * query_block
    mixed = lax.map(jax.checkpoint(attend), starts).reshape(seq_len, HEADS * HEAD_DIM)
    attn_mix = low(low_back(mixed))
    resid = x_seq + low_back(jnp.dot(attn_mix, o_weight, precision=HIGHEST_PREC))
    inv_two = lax.rsqrt(lax.optimization_barrier(jnp.mean(resid * resid, axis=-1, keepdims=True)) + NORM_EPS)
    ffn_in = low(resid * inv_two * ffn_gain)
    gate = low_back(jnp.dot(ffn_in, gate_weight, precision=HIGHEST_PREC))
    up_val = low_back(jnp.dot(ffn_in, up_weight, precision=HIGHEST_PREC))
    hidden = low(jax.nn.silu(gate) * up_val)
    return resid + jnp.dot(hidden, down_weight.T, precision=HIGHEST_PREC)

def reference(tokens, cotangent, attn_gain, q_weight, k_weight, v_weight, o_weight, ffn_gain, gate_weight, up_weight, down_weight):
    positions = dealt_positions(jnp.arange(SEQ_LEN, dtype=jnp.int32), BLK, N_CP)
    cosine, sine = rotary_tables(positions, HEAD_DIM)
    weights = tuple((matrix.astype(jnp.float32) for matrix in (attn_gain, q_weight, k_weight, v_weight, o_weight, ffn_gain, gate_weight, up_weight, down_weight)))

    def forward(x_all, *params):

        def one_sequence(x_seq):
            return layer(x_seq, *params, positions, cosine, sine)
        return lax.map(one_sequence, x_all)
    block_out, pullback = jax.vjp(forward, tokens.astype(jnp.float32), *weights)
    grads = pullback(cotangent.astype(jnp.float32))
    return (block_out.astype(jnp.bfloat16), grads[0].astype(jnp.bfloat16), grads[1], grads[2], grads[3], grads[4], grads[5], grads[6], grads[7], grads[8], grads[9])
```

```python
import functools

import jax
import jax.numpy as jnp
from jax import lax
from jax.experimental import pallas as pl
from jax.experimental.pallas import tpu as pltpu
from jax.sharding import PartitionSpec as P

HEADS = 32
KV_HEADS = 8
HEAD_DIM = 64
HALF = HEAD_DIM // 2
NORM_EPS = 1e-05
ROPE_BASE = 500000.0
BOTH = ("fsdp", "cp")
F32 = jnp.float32
BF16 = jnp.bfloat16


def dot(left, right):
    return jnp.dot(left, right, preferred_element_type=F32)


def contract_rows(left, right):
    return lax.dot_general(left, right, (((0,), (0,)), ((), ())), preferred_element_type=F32)


def contract_cols(left, right):
    return lax.dot_general(left, right, (((1,), (1,)), ((), ())), preferred_element_type=F32)


def swap_halves(wide):
    pieces = []
    for start in range(0, wide.shape[-1], HEAD_DIM):
        pieces.append(wide[:, start + HALF : start + HEAD_DIM])
        pieces.append(wide[:, start : start + HALF])
    return jnp.concatenate(pieces, axis=-1)


def diagonal_mask(rows_of, cols_of, team, block_len, later):
    def place(index):
        owner, within = index // block_len, index % block_len
        return (team - 1 - owner) * block_len + within if later else index

    return place(rows_of) >= place(cols_of)


QUARTER_OF = (0, 3, 1, 2)


def attention_forward(team, block_len, q_width, t_ref, proj_ref, cos_ref, sin_ref, mix_ref, rot_ref, wide_ref):
    t = t_ref[0]
    quarter = team * block_len
    heads = q_width // HEAD_DIM

    def place_chunk(owner, carry):
        diff = owner ^ t
        spot = diff // 2 + (diff % 2) * (team // 2)
        rows = pl.ds(pl.multiple_of(owner * block_len, block_len), block_len)
        for slot in range(4):
            wide_ref[QUARTER_OF[slot], rows, :] = proj_ref[spot, slot * block_len : (slot + 1) * block_len, :]
        return carry

    lax.fori_loop(0, team, place_chunk, 0)
    for part in range(4):
        wide = wide_ref[part]
        cosine, sine = cos_ref[part], sin_ref[part]
        qk = wide[:, : q_width + HEAD_DIM]
        turned = qk * cosine + swap_halves(qk) * sine
        rot_ref[part] = jnp.concatenate([turned, wide[:, q_width + HEAD_DIM :]], axis=-1).astype(BF16)

    for part in range(4):
        span = (part + 1) * quarter
        keys = rot_ref[: part + 1, :, q_width : q_width + HEAD_DIM].reshape(span, HEAD_DIM)
        values = rot_ref[: part + 1, :, q_width + HEAD_DIM :].reshape(span, HEAD_DIM)
        row = lax.broadcasted_iota(jnp.int32, (quarter, quarter), 0)
        col = lax.broadcasted_iota(jnp.int32, (quarter, quarter), 1)
        allowed = diagonal_mask(row, col, team, block_len, part >= 2)
        outs = []
        for head in range(heads):
            query = rot_ref[part, :, head * HEAD_DIM : (head + 1) * HEAD_DIM]
            scores = contract_cols(query, keys)
            last = jnp.where(allowed, scores[:, part * quarter :], -1e30)
            scores = jnp.concatenate([scores[:, : part * quarter], last], axis=-1) if part else last
            peak = jnp.max(scores, axis=-1, keepdims=True)
            expo = jnp.exp(scores - peak)
            total = jnp.sum(expo, axis=-1, keepdims=True)
            outs.append(dot(expo.astype(BF16), values) / total)
        mixed = jnp.concatenate(outs, axis=-1).astype(BF16)
        slot = QUARTER_OF.index(part)
        for owner in range(team):
            mix_ref[owner, slot * block_len : (slot + 1) * block_len, :] = mixed[
                owner * block_len : (owner + 1) * block_len, :
            ]


def attention_backward(
    team, block_len, q_width, t_ref, rot_ref, grad_ref, cos_ref, sin_ref, out_ref, wide_ref, dq_ref, dkv_ref
):
    t = t_ref[0]
    quarter = team * block_len
    heads = q_width // HEAD_DIM
    dkv_ref[...] = jnp.zeros_like(dkv_ref)
    for owner in range(team):
        for slot in range(4):
            wide_ref[QUARTER_OF[slot], owner * block_len : (owner + 1) * block_len, :] = grad_ref[
                owner, slot * block_len : (slot + 1) * block_len, :
            ]

    for part in range(4):
        span = (part + 1) * quarter
        keys = rot_ref[: part + 1, :, q_width : q_width + HEAD_DIM].reshape(span, HEAD_DIM)
        values = rot_ref[: part + 1, :, q_width + HEAD_DIM :].reshape(span, HEAD_DIM)
        row = lax.broadcasted_iota(jnp.int32, (quarter, quarter), 0)
        col = lax.broadcasted_iota(jnp.int32, (quarter, quarter), 1)
        allowed = diagonal_mask(row, col, team, block_len, part >= 2)
        for head in range(heads):
            cols = slice(head * HEAD_DIM, (head + 1) * HEAD_DIM)
            query = rot_ref[part, :, cols]
            grad = wide_ref[part, :, cols]
            scores = contract_cols(query, keys)
            last = jnp.where(allowed, scores[:, part * quarter :], -1e30)
            scores = jnp.concatenate([scores[:, : part * quarter], last], axis=-1) if part else last
            peak = jnp.max(scores, axis=-1, keepdims=True)
            expo = jnp.exp(scores - peak)
            probs = expo / jnp.sum(expo, axis=-1, keepdims=True)
            dprob = contract_cols(grad, values)
            delta = jnp.sum(probs * dprob, axis=-1, keepdims=True)
            score_grad = (probs * (dprob - delta)).astype(BF16)
            dq_ref[part, :, cols] = dot(score_grad, keys)
            dk = contract_rows(score_grad, query)
            dv = contract_rows(probs.astype(BF16), grad)
            both = jnp.concatenate([dk, dv], axis=-1).reshape(part + 1, quarter, 2 * HEAD_DIM)
            dkv_ref[: part + 1] += both

    for part in range(4):
        qk = jnp.concatenate([dq_ref[part], dkv_ref[part][:, :HEAD_DIM]], axis=-1)
        turned = qk * cos_ref[part] - swap_halves(qk) * sin_ref[part]
        dq_ref[part] = turned[:, :q_width]
        dkv_ref[part] = jnp.concatenate([turned[:, q_width:], dkv_ref[part][:, HEAD_DIM:]], axis=-1)

    def place_chunk(owner, carry):
        diff = owner ^ t
        spot = diff // 2 + (diff % 2) * (team // 2)
        rows = pl.ds(pl.multiple_of(owner * block_len, block_len), block_len)
        for slot in range(4):
            piece = jnp.concatenate([dq_ref[QUARTER_OF[slot], rows, :], dkv_ref[QUARTER_OF[slot], rows, :]], axis=-1)
            out_ref[spot, slot * block_len : (slot + 1) * block_len, :] = piece.astype(BF16)
        return carry

    lax.fori_loop(0, team, place_chunk, 0)


def vmem():
    return pl.BlockSpec(memory_space=pltpu.VMEM)


def smem():
    return pl.BlockSpec(memory_space=pltpu.SMEM)


def body(
    tokens,
    cotangent,
    attn_gain,
    q_weight,
    k_weight,
    v_weight,
    o_weight,
    ffn_gain,
    gate_weight,
    up_weight,
    down_weight,
):
    fsdp_size, cp_size = lax.axis_size("fsdp"), lax.axis_size("cp")
    devices = fsdp_size * cp_size
    teams, row_count, width = tokens.shape
    team = cp_size // teams
    block_len = row_count // 2
    chunk = teams * row_count
    token_count = team * chunk
    quarter = team * block_len
    f = lax.axis_index("fsdp")
    c = lax.axis_index("cp")
    side, t = c // team, c % team
    q_width = HEADS // team * HEAD_DIM
    copies = team // KV_HEADS
    qkv_width = q_width + 2 * HEAD_DIM
    team_groups = [[k * team + i for i in range(team)] for k in range(teams)]

    def swap(value, mask):
        return lax.ppermute(value, BOTH, [(i, i ^ mask) for i in range(devices)])

    def to_team(value):
        return lax.all_to_all(value, "cp", 0, 0, axis_index_groups=team_groups, tiled=True)

    def reorder(value):
        blocks = value.reshape(-1, fsdp_size, teams, width // (fsdp_size * teams))
        blocks = jnp.where(f == 1, blocks[:, ::-1], blocks)
        blocks = jnp.where(side == 1, blocks[:, :, ::-1], blocks)
        return blocks.reshape(value.shape)

    def own_rows(value):
        mine = jnp.where(side == 0, value[0], value[1])
        other = jnp.where(side == 0, value[1], value[0])
        theirs = swap(other, team)
        return jnp.concatenate([jnp.where(side == 0, mine, theirs), jnp.where(side == 0, theirs, mine)], axis=0)

    def give_rows(value):
        first, second = value[:row_count], value[row_count:]
        mine = jnp.where(side == 0, first, second)
        theirs = swap(jnp.where(side == 0, second, first), team)
        return jnp.stack([jnp.where(side == 0, mine, theirs), jnp.where(side == 0, theirs, mine)], axis=0)

    def team_gather(value):
        evens = jnp.concatenate([value] + [swap(value, m) for m in range(2, team, 2)], axis=0)
        return jnp.concatenate([evens, swap(evens, 1)], axis=0)

    def team_reduce(make):
        half = token_count // 2
        theirs = swap(make(1), 1)
        evens = (make(0).astype(F32) + theirs.astype(F32)).astype(BF16).reshape(team // 2, chunk, width)
        total = evens[0].astype(F32)
        for m in range(2, team, 2):
            total = total + swap(evens[m // 2], m).astype(F32)
        return total

    def gather_small(value):
        for bit in range(devices.bit_length() - 1):
            mask = 1 << bit
            index = (f * cp_size + c) & mask
            theirs = swap(value, mask)
            value = jnp.where(
                index == 0, jnp.concatenate([value, theirs], -1), jnp.concatenate([theirs, value], -1)
            )
        return value

    def scatter_small(value):
        for bit in reversed(range(devices.bit_length() - 1)):
            mask = 1 << bit
            index = (f * cp_size + c) & mask
            half = value.shape[-1] // 2
            low, high = value[..., :half], value[..., half:]
            theirs = swap(jnp.where(index == 0, high, low), mask)
            value = jnp.where(index == 0, low, high) + theirs
        return value

    def spread(pieces):
        own = to_team(pieces).reshape(team * pieces.shape[1], pieces.shape[2])
        beside = swap(own, team)
        return jnp.concatenate([own, beside, swap(own, cp_size), swap(beside, cp_size)], axis=0)

    def collect(value):
        cols = value.shape[1]
        blocks = value.reshape(fsdp_size, teams, -1, cols)
        theirs = swap(blocks[1], cp_size)
        blocks = (blocks[0].astype(F32) + theirs.astype(F32)).astype(BF16)
        theirs = swap(blocks[1], team)
        own = (blocks[0].astype(F32) + theirs.astype(F32)).astype(BF16)
        return to_team(own.reshape(team, -1, cols))

    def cut(weight):
        rows = weight.shape[0]
        return weight.reshape(rows, team, -1).transpose(1, 0, 2)

    def join(pieces):
        return pieces.transpose(1, 0, 2).reshape(pieces.shape[1], -1).astype(F32)

    def repeat_heads(weight):
        heads = weight.reshape(weight.shape[0], KV_HEADS, HEAD_DIM)
        return jnp.repeat(heads, copies, axis=1).reshape(weight.shape[0], -1)

    def sum_heads(pieces):
        grouped = pieces.astype(F32).reshape(KV_HEADS, copies, -1, HEAD_DIM).sum(axis=1)
        return grouped.transpose(1, 0, 2).reshape(grouped.shape[1], -1)

    x_float = own_rows(tokens).astype(F32)
    gains = gather_small(jnp.stack([attn_gain, ffn_gain]))
    gain_one, gain_two = gains[0:1].astype(F32), gains[1:2].astype(F32)
    qkv_team = spread(
        jnp.concatenate([cut(q_weight), cut(repeat_heads(k_weight)), cut(repeat_heads(v_weight))], axis=-1)
    )
    dy_low = own_rows(cotangent)
    o_full = lax.all_gather(o_weight, BOTH, axis=0, tiled=True)
    gate_team = spread(cut(gate_weight))
    up_team = spread(cut(up_weight))
    down_team = spread(cut(down_weight))

    inv_one = lax.rsqrt(jnp.mean(x_float * x_float, axis=-1, keepdims=True) + NORM_EPS)
    normed_one = x_float * inv_one
    attn_in = team_gather(reorder((normed_one * gain_one).astype(BF16)))
    proj = dot(attn_in, qkv_team)

    spots = jnp.arange(quarter, dtype=jnp.int32)
    owner, within = spots // block_len, spots % block_len
    flipped = (team - 1 - owner) * block_len + within
    places = jnp.stack([spots, quarter + spots, 2 * quarter + flipped, 3 * quarter + flipped])
    inverse = ROPE_BASE ** (-(2.0 * jnp.arange(HALF, dtype=F32)) / HEAD_DIM)
    angle = places.astype(F32)[:, :, None] * inverse
    cosine, sine = jnp.cos(angle), jnp.sin(angle)
    turn_heads = q_width // HEAD_DIM + 1
    scale = HEAD_DIM ** (-0.5)
    scales = jnp.concatenate([jnp.full((q_width,), scale, F32), jnp.ones((HEAD_DIM,), F32)])
    cos_table = jnp.tile(jnp.concatenate([cosine, cosine], -1), (1, 1, turn_heads)) * scales
    sin_table = jnp.tile(jnp.concatenate([-sine, sine], -1), (1, 1, turn_heads)) * scales
    t_scalar = t.astype(jnp.int32).reshape(1)

    mix_parts, rot = pl.pallas_call(
        functools.partial(attention_forward, team, block_len, q_width),
        out_shape=(
            jax.ShapeDtypeStruct((team, chunk, q_width), BF16),
            jax.ShapeDtypeStruct((4, quarter, qkv_width), BF16),
        ),
        in_specs=[smem(), vmem(), vmem(), vmem()],
        out_specs=(vmem(), vmem()),
        scratch_shapes=[pltpu.VMEM((4, quarter, qkv_width), F32)],
        compiler_params=pltpu.CompilerParams(vmem_limit_bytes=60 << 20),
        name="attention_forward",
    )(t_scalar, proj.reshape(team, chunk, qkv_width), cos_table, sin_table)

    attn_mix = to_team(mix_parts).transpose(1, 0, 2).reshape(chunk, width)
    resid = x_float + dot(attn_mix, o_full)
    inv_two = lax.rsqrt(jnp.mean(resid * resid, axis=-1, keepdims=True) + NORM_EPS)
    normed_two = resid * inv_two
    ffn_in = team_gather(reorder((normed_two * gain_two).astype(BF16)))
    dy_team = team_gather(reorder(dy_low))

    gate = dot(ffn_in, gate_team)
    up_val = dot(ffn_in, up_team)
    sigma = jax.nn.sigmoid(gate)
    silu_val = gate * sigma
    hidden = (silu_val * up_val).astype(BF16)
    hidden_grad = dot(dy_team, down_team)
    gate_grad = (hidden_grad * up_val * (sigma + gate * sigma * (1.0 - sigma))).astype(BF16)
    up_grad = (hidden_grad * silu_val).astype(BF16)

    half = token_count // 2

    def half_of(value, odd):
        return value[half * odd : half * (odd + 1)]

    ffn_in_grad = reorder(
        team_reduce(
            lambda odd: (
                contract_cols(half_of(gate_grad, odd), gate_team) + contract_cols(half_of(up_grad, odd), up_team)
            ).astype(BF16)
        )
    )
    down_sum = reorder(team_reduce(lambda odd: contract_cols(half_of(hidden, odd), down_team).astype(BF16)))
    block_out = give_rows((resid + down_sum).astype(BF16))

    ffn_gain_grad = scatter_small(jnp.sum(ffn_in_grad * normed_two, axis=0))
    scaled_two = ffn_in_grad * gain_two
    resid_grad = dy_low.astype(F32) + inv_two * (
        scaled_two - normed_two * jnp.mean(scaled_two * normed_two, axis=-1, keepdims=True)
    )
    branch_grad = resid_grad.astype(BF16)
    mix_grad = contract_cols(branch_grad, o_full).astype(BF16)
    mix_grad = to_team(mix_grad.reshape(chunk, team, q_width).transpose(1, 0, 2))
    o_weight_grad = lax.psum_scatter(
        contract_rows(attn_mix, branch_grad).astype(BF16), BOTH, scatter_dimension=0, tiled=True
    ).astype(F32)

    down_weight_grad = join(collect(contract_rows(dy_team, hidden).astype(BF16)))
    gate_weight_grad = join(collect(contract_rows(ffn_in, gate_grad).astype(BF16)))
    up_weight_grad = join(collect(contract_rows(ffn_in, up_grad).astype(BF16)))

    proj_grad = pl.pallas_call(
        functools.partial(attention_backward, team, block_len, q_width),
        out_shape=jax.ShapeDtypeStruct((team, chunk, qkv_width), BF16),
        in_specs=[smem(), vmem(), vmem(), vmem(), vmem()],
        out_specs=vmem(),
        scratch_shapes=[
            pltpu.VMEM((4, quarter, q_width), BF16),
            pltpu.VMEM((4, quarter, q_width), F32),
            pltpu.VMEM((4, quarter, 2 * HEAD_DIM), F32),
        ],
        compiler_params=pltpu.CompilerParams(vmem_limit_bytes=60 << 20),
        name="attention_backward",
    )(t_scalar, rot, mix_grad, cos_table, sin_table).reshape(token_count, qkv_width)

    attn_in_grad = reorder(
        team_reduce(lambda odd: contract_cols(half_of(proj_grad, odd), qkv_team).astype(BF16))
    )
    attn_gain_grad = scatter_small(jnp.sum(attn_in_grad * normed_one, axis=0))
    scaled_one = attn_in_grad * gain_one
    input_grad = resid_grad + inv_one * (
        scaled_one - normed_one * jnp.mean(scaled_one * normed_one, axis=-1, keepdims=True)
    )
    input_grad = give_rows(input_grad.astype(BF16))

    qkv_grad = collect(contract_rows(attn_in, proj_grad).astype(BF16))
    q_weight_grad = join(qkv_grad[:, :, :q_width])
    k_weight_grad = sum_heads(qkv_grad[:, :, q_width : q_width + HEAD_DIM])
    v_weight_grad = sum_heads(qkv_grad[:, :, q_width + HEAD_DIM :])

    return (
        block_out,
        input_grad,
        attn_gain_grad,
        q_weight_grad,
        k_weight_grad,
        v_weight_grad,
        o_weight_grad,
        ffn_gain_grad,
        gate_weight_grad,
        up_weight_grad,
        down_weight_grad,
    )


def solution(mesh):
    rows = P(BOTH, None)
    placed = P("fsdp", "cp", None)
    gain = P(BOTH)
    return jax.shard_map(
        body,
        mesh=mesh,
        in_specs=(placed, placed, gain, rows, rows, rows, rows, gain, rows, rows, rows),
        out_specs=(placed, placed, gain, rows, rows, rows, rows, gain, rows, rows, rows),
        check_vma=False,
    )
```

```python
import functools

import jax
import jax.numpy as jnp
from jax import lax
from jax.experimental import pallas as pl
from jax.experimental.pallas import tpu as pltpu
from jax.sharding import PartitionSpec as P

HEADS = 32
KV_HEADS = 8
HEAD_DIM = 64
HALF = HEAD_DIM // 2
NORM_EPS = 1e-05
ROPE_BASE = 500000.0
BOTH = ("fsdp", "cp")
F32 = jnp.float32
BF16 = jnp.bfloat16
MESH = pl.DeviceIdType.MESH
VMEM_BYTES = 60 << 20


def dot(left, right):
    return jnp.dot(left, right, preferred_element_type=F32)


def contract_rows(left, right):
    return lax.dot_general(left, right, (((0,), (0,)), ((), ())), preferred_element_type=F32)


def contract_cols(left, right):
    return lax.dot_general(left, right, (((1,), (1,)), ((), ())), preferred_element_type=F32)


def flip(index, mask):
    bit = 1
    out = index
    while bit <= mask:
        if mask & bit:
            out = out + bit - 2 * bit * ((index // bit) % 2)
        bit *= 2
    return out


def spot_of(diff, team):
    return diff // 2 + (diff % 2) * (team // 2)


def chunk_blocks(member, team):
    second = team + flip(member, team // 2)
    last = 4 * team - 1
    return member, last - member, second, last - second


def natural_unit(mine, index):
    block = flip(mine, index // 2)
    turned = block % 2
    return block * 2 + (index % 2) + turned * (1 - 2 * (index % 2))


def swap_halves(wide):
    pieces = []
    for start in range(0, wide.shape[-1], HEAD_DIM):
        pieces.append(wide[:, start + HALF : start + HEAD_DIM])
        pieces.append(wide[:, start : start + HALF])
    return jnp.concatenate(pieces, axis=-1)


def over_row_blocks(token_count, step):
    quarter = token_count // 4
    rows = min(256, (1 << 18) // token_count)
    for first in range(0, token_count, quarter):
        if rows == quarter:
            step(first, first + quarter, first, rows)
        else:

            def block(index, carry, first=first):
                step(first, first + quarter, pl.multiple_of(first + index * rows, rows), rows)
                return carry

            lax.fori_loop(0, quarter // rows, block, 0)


def masked_scores(query, keys, first, start):
    rows, span = query.shape[0], keys.shape[0] - first
    scores = contract_cols(query, keys)
    row = lax.broadcasted_iota(jnp.int32, (rows, span), 0) + (start - first)
    col = lax.broadcasted_iota(jnp.int32, (rows, span), 1)
    last = jnp.where(row >= col, scores[:, first:], -1e30)
    return jnp.concatenate([scores[:, :first], last], axis=-1) if first else last


def differ(left, right, size):
    out = 0
    bit = 1
    while bit < size:
        out = out + ((left // bit + right // bit) % 2) * bit
        bit *= 2
    return out


class Links:
    def __init__(self, cp_size, send, recv, local):
        self.f, self.c = lax.axis_index("fsdp"), lax.axis_index("cp")
        self.cp_size, self.send, self.recv, self.local = cp_size, send, recv, local
        self.used = self.used_local = 0

    def device(self, mask):
        return (flip(self.f, mask // self.cp_size), flip(self.c, mask % self.cp_size))

    def barrier(self, masks):
        sem = pltpu.get_barrier_semaphore()
        for mask in masks:
            pl.semaphore_signal(sem, inc=1, device_id=self.device(mask), device_id_type=MESH)
        pl.semaphore_wait(sem, len(masks))

    def copy(self, src, dst, mask):
        index = self.used
        self.used += 1
        return pltpu.make_async_remote_copy(
            src_ref=src,
            dst_ref=dst,
            send_sem=self.send.at[index],
            recv_sem=self.recv.at[index],
            device_id=self.device(mask),
            device_id_type=MESH,
        )

    def inside(self, src, dst):
        index = self.used_local
        self.used_local += 1
        return pltpu.make_async_copy(src, dst, self.local.at[index])


class TeamGather:
    def __init__(self, links, team, src, dst):
        self.evens = range(2, team, 2)
        self.dst, self.team = dst, team
        self.sends = [links.copy(src, dst.at[spot_of(m, team)], m) for m in self.evens]
        self.passes = [links.copy(src, dst.at[spot_of(1, team)], 1)]
        for m in self.evens:
            self.passes.append(links.copy(dst.at[spot_of(m, team)], dst.at[spot_of(m + 1, team)], 1))
        self.own = links.inside(src, dst.at[0])

    def start(self):
        for send in self.sends:
            send.start()
        self.passes[0].start()
        self.own.start()

    def forward(self, index):
        self.sends[index].wait_recv()
        self.passes[index + 1].start()

    def finish(self):
        for passed in self.passes:
            passed.wait_recv()
        for send in self.sends + self.passes:
            send.wait_send()
        self.own.wait()


class Spread:
    def __init__(self, links, team, t, inner, pieces, full, above, below):
        self.inner, self.team = inner, team
        near, mirror = team // 2, team + team // 2
        across = links.cp_size
        self.own = links.inside(pieces(0), full.at[0, t])
        self.cuts = [links.copy(pieces(m), full.at[0, t], m) for m in range(1, team)]
        self.far = [links.copy(full.at[0], full.at[2], across), links.copy(full.at[1], full.at[3], across)]
        self.straight = links.copy(full.at[0], full.at[1], mirror)
        self.up = links.copy(full.at[0], above, near)
        self.over = links.copy(above, below, mirror)
        self.down = links.copy(below, full.at[1], near)

    def cut(self):
        self.own.start()
        for piece in self.cuts:
            piece.start()

    def leave(self):
        self.own.wait()
        for piece in self.cuts:
            piece.wait_recv()
        self.far[0].start()

        @pl.when(self.inner)
        def _():
            self.straight.start()

        @pl.when(jnp.logical_not(self.inner))
        def _():
            self.up.start()

    def relay(self):
        @pl.when(self.inner)
        def _():
            self.up.wait_recv()
            self.over.start()

    def arrive(self):
        @pl.when(self.inner)
        def _():
            self.straight.wait_recv()
            self.far[1].start()
            self.over.wait_recv()
            self.down.start()

        @pl.when(jnp.logical_not(self.inner))
        def _():
            self.down.wait_recv()
            self.far[1].start()

    def finish(self):
        for copy in self.far:
            copy.wait_recv()
        for copy in self.cuts + self.far:
            copy.wait_send()

        @pl.when(self.inner)
        def _():
            self.straight.wait_send()
            self.over.wait_send()
            self.down.wait_send()

        @pl.when(jnp.logical_not(self.inner))
        def _():
            self.up.wait_send()


def entry_kernel(
    fsdp_size,
    cp_size,
    tokens,
    cotangent,
    gains_in,
    qkv_cut,
    o_cut,
    gate_in,
    up_in,
    down_in,
    cos_ref,
    sin_ref,
    x_ref,
    gains_ref,
    attn_in_ref,
    qkv_full,
    o_wide,
    rot_ref,
    mix_ref,
    resid_ref,
    ffn_in_ref,
    dy_ref,
    gate_full,
    up_full,
    down_full,
    o_full,
    *rest,
):
    relays, scratch = rest[:10], rest[10:]
    (send, recv, local, swapped, dy_swapped, slots, chunk_ref, dy_chunk, acts, wqkv, mixed, o_pieces, taken, parts) = scratch
    links = Links(cp_size, send, recv, local)
    f, c = links.f, links.c
    team = cp_size // 2
    near, mirror = team // 2, team + team // 2
    side = c // team
    t = c % team + side * (flip(c, near) - c)
    inner = t // near == 1
    row_count, width = tokens.shape[1], tokens.shape[2]
    block_len = row_count // 2
    unit = width // 8
    token_count, q_width = mixed.shape
    heads = q_width // HEAD_DIM
    cols = gate_full.shape[-1]
    mine = f * 2 + side

    links.barrier(list(range(1, team)) + [mirror, cp_size])
    swap = links.copy(tokens.at[1 - side], swapped, mirror)
    swap.start()
    slots[0] = gains_in[...]
    stages = []
    size = 1
    for mask in [1 << k for k in range(team.bit_length() - 1)] + [mirror, cp_size]:
        stages.append(links.copy(slots.at[pl.ds(0, size)], slots.at[pl.ds(size, size)], mask))
        size *= 2

    def columns_of(weight):
        return lambda m: weight.at[:, pl.ds(pl.multiple_of(flip(t, m) * cols, cols), cols)]

    def spread(pieces, full, index):
        return Spread(links, team, t, inner, pieces, full, relays[2 * index], relays[2 * index + 1])

    qkv_spread = spread(lambda m: qkv_cut.at[flip(t, m)], qkv_full, 0)
    o_spread = spread(lambda m: o_cut.at[flip(t, m)], o_full, 1)
    gate_spread = spread(columns_of(gate_in), gate_full, 2)
    up_spread = spread(columns_of(up_in), up_full, 3)
    down_spread = spread(columns_of(down_in), down_full, 4)

    stages[0].start()
    qkv_spread.cut()
    o_spread.cut()
    for step in range(1, len(stages)):
        stages[step - 1].wait_recv()
        stages[step].start()
    gate_spread.cut()

    def fill(dst, source, theirs):
        here = pl.ds(pl.multiple_of(side * row_count, row_count), row_count)
        there = pl.ds(pl.multiple_of((1 - side) * row_count, row_count), row_count)
        for index in range(8):
            cols = slice(index * unit, (index + 1) * unit)
            natural = pl.ds(pl.multiple_of(natural_unit(mine, index) * unit, unit), unit)
            dst[here, cols] = source[side, :, natural].astype(dst.dtype)
            dst[there, cols] = theirs[:, natural].astype(dst.dtype)

    stages[-1].wait_recv()
    pieces = []
    for b in range(4):
        for member in range(team):
            pieces.append(slots[b * team + flip(t, member)][:8, : width // (4 * team)])
    gains = jnp.concatenate(pieces, axis=-1).astype(F32)
    gains_ref[...] = gains
    swap.wait_recv()
    fill(x_ref, tokens, swapped)
    x = x_ref[...]
    inv_one = lax.rsqrt(jnp.mean(x * x, axis=-1, keepdims=True) + NORM_EPS)
    chunk_ref[...] = (x * inv_one * gains[0:1]).astype(BF16)
    gather_one = TeamGather(links, team, chunk_ref, acts)
    gather_one.start()
    dy_swap = links.copy(cotangent.at[1 - side], dy_swapped, mirror)
    dy_swap.start()
    qkv_spread.leave()
    o_spread.leave()
    up_spread.cut()
    down_spread.cut()
    for index in range(len(gather_one.sends) - 1):
        gather_one.forward(index)
    qkv_spread.relay()
    o_spread.relay()
    gather_one.forward(len(gather_one.sends) - 1)
    gate_spread.leave()
    qkv_spread.arrive()
    o_spread.arrive()
    gate_spread.relay()
    qkv_spread.finish()
    load = links.inside(qkv_full, wqkv)
    load.start()
    gather_one.finish()
    attn_out = links.inside(acts, attn_in_ref)
    attn_out.start()
    o_spread.finish()

    o_rows = o_full.shape[2]

    def o_source(m):
        count = q_width // o_rows
        first = flip(t, m) * count
        owners, start = first // team, first % team
        block = ((owners // 2 + mine // 2) % 2) * 2 + (owners + mine) % 2
        return o_full.at[block, pl.ds(start + (owners % 2) * (flip(start, near) - start), count)]

    o_own = links.inside(o_source(0), o_pieces.at[t])
    o_sends = [links.copy(o_source(m), o_pieces.at[t], m) for m in range(1, team)]
    o_own.start()
    for copy in o_sends:
        copy.start()
    up_spread.leave()

    load.wait()
    weights = wqkv[...].reshape(width, wqkv.shape[-1])

    def project(m, carry):
        proj = dot(acts[spot_of(m, team)], weights)
        qk = proj[:, : q_width + HEAD_DIM]
        qk_swapped = swap_halves(qk)
        blocks = chunk_blocks(differ(t, m, team), team)
        for slot in range(4):
            piece = slice(slot * block_len, (slot + 1) * block_len)
            rows = pl.ds(pl.multiple_of(blocks[slot] * block_len, block_len), block_len)
            turned = qk[piece] * cos_ref[rows, :] + qk_swapped[piece] * sin_ref[rows, :]
            rot_ref[rows, :] = jnp.concatenate([turned, proj[piece, q_width + HEAD_DIM :]], axis=-1).astype(BF16)
        return carry

    lax.fori_loop(0, team, project, 0)
    gate_spread.arrive()

    dy_swap.wait_recv()
    fill(dy_chunk, cotangent, dy_swapped)
    gather_dy = TeamGather(links, team, dy_chunk, dy_ref)
    gather_dy.start()
    up_spread.relay()

    def attend(first, span, start, rows):
        keys = rot_ref[:span, q_width : q_width + HEAD_DIM]
        values = rot_ref[:span, q_width + HEAD_DIM :]
        outs = []
        for head in range(heads):
            query = rot_ref[pl.ds(start, rows), head * HEAD_DIM : (head + 1) * HEAD_DIM]
            scores = masked_scores(query, keys, first, start)
            peak = jnp.max(scores, axis=-1, keepdims=True)
            expo = jnp.exp(scores - peak)
            total = jnp.sum(expo, axis=-1, keepdims=True)
            outs.append(dot(expo.astype(BF16), values) / total)
        mixed[pl.ds(start, rows), :] = jnp.concatenate(outs, axis=-1).astype(BF16)

    over_row_blocks(token_count, attend)
    gather_dy.forward(0)

    def collect_mix(m, carry):
        blocks = chunk_blocks(differ(t, m, team), team)
        for slot in range(4):
            where = pl.ds(pl.multiple_of(blocks[slot] * block_len, block_len), block_len)
            mix_ref[spot_of(m, team), slot * block_len : (slot + 1) * block_len, :] = mixed[where, :]
        return carry

    lax.fori_loop(0, team, collect_mix, 0)
    for copy in o_sends:
        copy.wait_recv()
    o_own.wait()
    span = width // team
    for index in range(8):
        for piece in range(team // 8):
            start = index * unit + piece * span
            source = natural_unit(mine, index) * (team // 8) + piece
            o_wide[:, start : start + span] = o_pieces[source].reshape(q_width, span)

    attn_out.wait()
    half = team // 2
    crossed = []
    for spot in range(half, team):
        acts[spot] = dot(mix_ref[spot], o_wide[...]).astype(BF16)
        copy = links.copy(acts.at[spot], taken.at[spot - half], 1)
        copy.start()
        crossed.append(copy)
    for index in range(1, len(gather_dy.sends)):
        gather_dy.forward(index)
    down_spread.leave()
    given = []
    for spot in list(range(1, half)) + [0]:
        part = dot(mix_ref[spot], o_wide[...])
        crossed[spot].wait_recv()
        if spot:
            acts[spot] = (part + taken[spot].astype(F32)).astype(BF16)
            copy = links.copy(acts.at[spot], parts.at[spot - 1], 2 * spot)
            copy.start()
            given.append(copy)
        else:
            resid_ref[...] = x_ref[...] + part + taken[0].astype(F32)
    up_spread.arrive()
    down_spread.relay()
    for index, copy in enumerate(given):
        copy.wait_recv()
        resid_ref[...] += parts[index].astype(F32)
    resid = resid_ref[...]
    inv_two = lax.rsqrt(jnp.mean(resid * resid, axis=-1, keepdims=True) + NORM_EPS)
    chunk_ref[...] = (resid * inv_two * gains_ref[1:2]).astype(BF16)
    gather_two = TeamGather(links, team, chunk_ref, ffn_in_ref)
    gather_two.start()
    gather_dy.finish()
    for index in range(len(gather_two.sends)):
        gather_two.forward(index)
    gate_spread.finish()
    down_spread.arrive()
    gather_two.finish()
    up_spread.finish()
    down_spread.finish()
    swap.wait_send()
    dy_swap.wait_send()
    for copy in stages + o_sends + crossed + given:
        copy.wait_send()


def attention_backward(
    team, block_len, q_width, where_ref, rot_ref, grad_ref, cos_ref, sin_ref, out_ref, wide_ref, dq_ref, dkv_ref
):
    t = where_ref[0]
    token_count = wide_ref.shape[0]
    heads = q_width // HEAD_DIM
    dkv_ref[...] = jnp.zeros_like(dkv_ref)

    def place_grad(m, carry):
        blocks = chunk_blocks(differ(t, m, team), team)
        for slot in range(4):
            where = pl.ds(pl.multiple_of(blocks[slot] * block_len, block_len), block_len)
            wide_ref[where, :] = grad_ref[spot_of(m, team), slot * block_len : (slot + 1) * block_len, :]
        return carry

    lax.fori_loop(0, team, place_grad, 0)

    def attend(first, span, start, count):
        rows = pl.ds(start, count)
        keys = rot_ref[:span, q_width : q_width + HEAD_DIM]
        values = rot_ref[:span, q_width + HEAD_DIM :]
        for head in range(heads):
            cols = slice(head * HEAD_DIM, (head + 1) * HEAD_DIM)
            query = rot_ref[rows, cols]
            grad = wide_ref[rows, cols]
            scores = masked_scores(query, keys, first, start)
            peak = jnp.max(scores, axis=-1, keepdims=True)
            expo = jnp.exp(scores - peak)
            probs = expo / jnp.sum(expo, axis=-1, keepdims=True)
            dprob = contract_cols(grad, values)
            delta = jnp.sum(probs * dprob, axis=-1, keepdims=True)
            score_grad = (probs * (dprob - delta)).astype(BF16)
            dq_ref[rows, cols] = dot(score_grad, keys)
            dk = contract_rows(score_grad, query)
            dv = contract_rows(probs.astype(BF16), grad)
            dkv_ref[:span, :] += jnp.concatenate([dk, dv], axis=-1)

    over_row_blocks(token_count, attend)

    for start in range(0, token_count, token_count // 4):
        rows = slice(start, start + token_count // 4)
        qk = jnp.concatenate([dq_ref[rows, :], dkv_ref[rows, :HEAD_DIM]], axis=-1)
        turned = qk * cos_ref[rows, :] - swap_halves(qk) * sin_ref[rows, :]
        dq_ref[rows, :] = turned[:, :q_width]
        dkv_ref[rows, :] = jnp.concatenate([turned[:, q_width:], dkv_ref[rows, HEAD_DIM:]], axis=-1)

    def give_chunk(m, carry):
        blocks = chunk_blocks(differ(t, m, team), team)
        for slot in range(4):
            rows = pl.ds(pl.multiple_of(blocks[slot] * block_len, block_len), block_len)
            piece = jnp.concatenate([dq_ref[rows, :], dkv_ref[rows, :]], axis=-1)
            out_ref[spot_of(m, team), slot * block_len : (slot + 1) * block_len, :] = piece.astype(BF16)
        return carry

    lax.fori_loop(0, team, give_chunk, 0)


def vmem():
    return pl.BlockSpec(memory_space=pltpu.VMEM)


def smem():
    return pl.BlockSpec(memory_space=pltpu.SMEM)


def anywhere():
    return pl.BlockSpec(memory_space=pl.ANY)


def body(
    tokens,
    cotangent,
    attn_gain,
    q_weight,
    k_weight,
    v_weight,
    o_weight,
    ffn_gain,
    gate_weight,
    up_weight,
    down_weight,
):
    fsdp_size, cp_size = lax.axis_size("fsdp"), lax.axis_size("cp")
    devices = fsdp_size * cp_size
    teams, row_count, width = tokens.shape
    team = cp_size // teams
    mirror = team + team // 2
    block_len = row_count // 2
    chunk = teams * row_count
    token_count = team * chunk
    f = lax.axis_index("fsdp")
    c = lax.axis_index("cp")
    side = c // team
    t = c % team ^ (team // 2 * side)
    q_width = HEADS // team * HEAD_DIM
    copies = team // KV_HEADS
    qkv_width = q_width + 2 * HEAD_DIM
    weight_rows = q_weight.shape[0]
    hidden_cols = gate_weight.shape[1] // team
    team_groups = [[k * team + i for i in range(team)] for k in range(teams)]

    def swap(value, mask):
        return lax.ppermute(value, BOTH, [(i, i ^ mask) for i in range(devices)])

    def turn(value):
        half = team // 2
        return jnp.where(side == 1, jnp.concatenate([value[half:], value[:half]], axis=0), value)

    def to_team(value):
        return turn(lax.all_to_all(turn(value), "cp", 0, 0, axis_index_groups=team_groups, tiled=True))

    def swap_blocks(blocks):
        blocks = jnp.where(f == 1, blocks[:, ::-1], blocks)
        return jnp.where(side == 1, blocks[:, :, ::-1], blocks)

    def turn_second(blocks):
        return jnp.concatenate([blocks[:, :, :1], blocks[:, :, 1:, ::-1]], axis=2)

    def reorder_rows(value):
        blocks = value.reshape(1, 2, 2, 2, width // 8, -1)
        return swap_blocks(turn_second(blocks)).reshape(value.shape)

    def restore(value):
        blocks = value.reshape(-1, 2, 2, 2, width // 8)
        return turn_second(swap_blocks(blocks)).reshape(value.shape)

    def give_rows(value):
        first, second = value[:row_count], value[row_count:]
        mine = jnp.where(side == 0, first, second)
        theirs = swap(jnp.where(side == 0, second, first), mirror)
        return jnp.stack([jnp.where(side == 0, mine, theirs), jnp.where(side == 0, theirs, mine)], axis=0)

    def team_gather(value):
        evens = jnp.concatenate([value] + [swap(value, m) for m in range(2, team, 2)], axis=0)
        return jnp.concatenate([evens, swap(evens, 1)], axis=0)

    def team_reduce(make):
        theirs = swap(make(1), 1)
        evens = (make(0).astype(F32) + theirs.astype(F32)).astype(BF16).reshape(team // 2, chunk, width)
        total = evens[0].astype(F32)
        for m in range(2, team, 2):
            total = total + swap(evens[m // 2], m).astype(F32)
        return total

    def scatter_small(value):
        for bit in reversed(range(devices.bit_length() - 1)):
            mask = 1 << bit
            index = (f * cp_size + c) & mask
            half = value.shape[-1] // 2
            low, high = value[..., :half], value[..., half:]
            theirs = swap(jnp.where(index == 0, high, low), mask)
            value = jnp.where(index == 0, low, high) + theirs
        return value

    def collect(value):
        cols = value.shape[-1]
        blocks = value.reshape(fsdp_size, teams, -1, cols)
        theirs = swap(blocks[1], cp_size)
        blocks = (blocks[0].astype(F32) + theirs.astype(F32)).astype(BF16)
        theirs = swap(blocks[1], mirror)
        own = (blocks[0].astype(F32) + theirs.astype(F32)).astype(BF16)
        return to_team(own.reshape(team, -1, cols))

    def cut(weight):
        return weight.reshape(weight_rows, team, -1).transpose(1, 0, 2)

    def join(pieces):
        return pieces.transpose(1, 0, 2).reshape(pieces.shape[1], -1).astype(F32)

    def repeat_heads(weight):
        heads = weight.reshape(weight_rows, KV_HEADS, HEAD_DIM)
        return jnp.repeat(heads, copies, axis=1).reshape(weight_rows, -1)

    def sum_heads(pieces):
        grouped = pieces.astype(F32).reshape(KV_HEADS, copies, -1, HEAD_DIM).sum(axis=1)
        return grouped.transpose(1, 0, 2).reshape(grouped.shape[1], -1)

    inverse = ROPE_BASE ** (-(2.0 * jnp.arange(HALF, dtype=F32)) / HEAD_DIM)
    angle = jnp.arange(token_count, dtype=jnp.int32).astype(F32)[:, None] * inverse[None, :]
    cosine, sine = jnp.cos(angle), jnp.sin(angle)
    turn_heads = q_width // HEAD_DIM + 1
    scale = HEAD_DIM ** (-0.5)
    scales = jnp.concatenate([jnp.full((q_width,), scale, F32), jnp.ones((HEAD_DIM,), F32)])
    cos_table = jnp.tile(jnp.concatenate([cosine, cosine], -1), (1, turn_heads)) * scales
    sin_table = jnp.tile(jnp.concatenate([-sine, sine], -1), (1, turn_heads)) * scales

    qkv_cut = jnp.concatenate([cut(q_weight), cut(repeat_heads(k_weight)), cut(repeat_heads(v_weight))], axis=-1)
    o_cut = cut(o_weight)
    gains_in = jnp.pad(jnp.stack([attn_gain, ffn_gain]), ((0, 14), (0, 128 - weight_rows)))

    def hbm(*shape):
        return jax.ShapeDtypeStruct(shape, BF16)

    out_shape = (
        jax.ShapeDtypeStruct((chunk, width), F32),
        jax.ShapeDtypeStruct((8, width), F32),
        hbm(team, chunk, width),
        hbm(4, team, weight_rows, qkv_width),
        hbm(q_width, width),
        hbm(token_count, qkv_width),
        hbm(team, chunk, q_width),
        jax.ShapeDtypeStruct((chunk, width), F32),
        hbm(team, chunk, width),
        hbm(team, chunk, width),
        hbm(4, team, weight_rows, hidden_cols),
        hbm(4, team, weight_rows, hidden_cols),
        hbm(4, team, weight_rows, hidden_cols),
        hbm(4, team, weight_rows, width // team),
    )
    relay_cols = (qkv_width, width // team, hidden_cols, hidden_cols, hidden_cols)
    relays = tuple(hbm(team, weight_rows, cols) for cols in relay_cols for _ in range(2))
    spaces = [vmem(), vmem(), anywhere(), anywhere(), vmem(), vmem(), vmem(), vmem()] + [anywhere()] * 16
    outs = pl.pallas_call(
        functools.partial(entry_kernel, fsdp_size, cp_size),
        out_shape=out_shape + relays,
        in_specs=[vmem(), vmem(), vmem()] + [anywhere()] * 5 + [vmem()] * 2,
        out_specs=tuple(spaces),
        scratch_shapes=[
            pltpu.SemaphoreType.DMA((10 * team + 48,)),
            pltpu.SemaphoreType.DMA((10 * team + 48,)),
            pltpu.SemaphoreType.DMA((16,)),
            pltpu.VMEM((row_count, width), BF16),
            pltpu.VMEM((row_count, width), BF16),
            pltpu.VMEM((devices, 16, 128), BF16),
            pltpu.VMEM((chunk, width), BF16),
            pltpu.VMEM((chunk, width), BF16),
            pltpu.VMEM((team, chunk, width), BF16),
            pltpu.VMEM((4, team, weight_rows, qkv_width), BF16),
            pltpu.VMEM((token_count, q_width), BF16),
            pltpu.VMEM((team, q_width // weight_rows, weight_rows, width // team), BF16),
            pltpu.VMEM((team // 2, chunk, width), BF16),
            pltpu.VMEM((team // 2 - 1, chunk, width), BF16),
        ],
        compiler_params=pltpu.CompilerParams(
            collective_id=0, has_side_effects=True, vmem_limit_bytes=VMEM_BYTES
        ),
        name="entry",
    )(tokens, cotangent, gains_in, qkv_cut, o_cut, gate_weight, up_weight, down_weight, cos_table, sin_table)
    x_float, gains, attn_in, qkv_team, o_team, rot, mix, resid, ffn_in, dy_team, gate_team, up_team, down_team = outs[:13]
    gain_one, gain_two = gains[0:1], gains[1:2]
    attn_in = attn_in.reshape(token_count, width)
    ffn_in = ffn_in.reshape(token_count, width)
    dy_low = dy_team[0]
    dy_team = dy_team.reshape(token_count, width)
    qkv_team = qkv_team.reshape(width, qkv_width)
    gate_team, up_team, down_team = (w.reshape(width, hidden_cols) for w in (gate_team, up_team, down_team))
    mix = mix.reshape(token_count, q_width)

    inv_one = lax.rsqrt(jnp.mean(x_float * x_float, axis=-1, keepdims=True) + NORM_EPS)
    normed_one = x_float * inv_one
    inv_two = lax.rsqrt(jnp.mean(resid * resid, axis=-1, keepdims=True) + NORM_EPS)
    normed_two = resid * inv_two

    gate = dot(ffn_in, gate_team)
    up_val = dot(ffn_in, up_team)
    sigma = jax.nn.sigmoid(gate)
    silu_val = gate * sigma
    hidden = (silu_val * up_val).astype(BF16)
    hidden_grad = dot(dy_team, down_team)
    gate_grad = (hidden_grad * up_val * (sigma + gate * sigma * (1.0 - sigma))).astype(BF16)
    up_grad = (hidden_grad * silu_val).astype(BF16)

    half = token_count // 2

    def half_of(value, odd):
        return value[half * odd : half * (odd + 1)]

    ffn_in_grad = team_reduce(
        lambda odd: (
            contract_cols(half_of(gate_grad, odd), gate_team) + contract_cols(half_of(up_grad, odd), up_team)
        ).astype(BF16)
    )
    down_sum = team_reduce(lambda odd: contract_cols(half_of(hidden, odd), down_team).astype(BF16))
    block_out = give_rows(restore((resid + down_sum).astype(BF16)))

    ffn_gain_grad = scatter_small(restore(jnp.sum(ffn_in_grad * normed_two, axis=0)))
    scaled_two = ffn_in_grad * gain_two
    resid_grad = dy_low.astype(F32) + inv_two * (
        scaled_two - normed_two * jnp.mean(scaled_two * normed_two, axis=-1, keepdims=True)
    )
    branch_grad = team_gather(resid_grad.astype(BF16))
    mix_grad = contract_cols(branch_grad, o_team).astype(BF16).reshape(team, chunk, q_width)

    down_weight_grad = join(collect(contract_rows(dy_team, hidden).astype(BF16)))
    gate_weight_grad = join(collect(contract_rows(ffn_in, gate_grad).astype(BF16)))
    up_weight_grad = join(collect(contract_rows(ffn_in, up_grad).astype(BF16)))

    proj_grad = pl.pallas_call(
        functools.partial(attention_backward, team, block_len, q_width),
        out_shape=jax.ShapeDtypeStruct((team, chunk, qkv_width), BF16),
        in_specs=[smem(), vmem(), vmem(), vmem(), vmem()],
        out_specs=vmem(),
        scratch_shapes=[
            pltpu.VMEM((token_count, q_width), BF16),
            pltpu.VMEM((token_count, q_width), F32),
            pltpu.VMEM((token_count, 2 * HEAD_DIM), F32),
        ],
        compiler_params=pltpu.CompilerParams(vmem_limit_bytes=VMEM_BYTES),
        name="attention_backward",
    )(t.astype(jnp.int32).reshape(1), rot, mix_grad, cos_table, sin_table).reshape(token_count, qkv_width)

    attn_in_grad = team_reduce(lambda odd: contract_cols(half_of(proj_grad, odd), qkv_team).astype(BF16))
    attn_gain_grad = scatter_small(restore(jnp.sum(attn_in_grad * normed_one, axis=0)))
    scaled_one = attn_in_grad * gain_one
    input_grad = resid_grad + inv_one * (
        scaled_one - normed_one * jnp.mean(scaled_one * normed_one, axis=-1, keepdims=True)
    )
    input_grad = give_rows(restore(input_grad.astype(BF16)))

    qkv_grad = collect(contract_rows(attn_in, proj_grad).astype(BF16))
    q_weight_grad = join(qkv_grad[:, :, :q_width])
    k_weight_grad = sum_heads(qkv_grad[:, :, q_width : q_width + HEAD_DIM])
    v_weight_grad = sum_heads(qkv_grad[:, :, q_width + HEAD_DIM :])

    o_grad = restore(contract_rows(mix, branch_grad)).astype(BF16)
    o_grad = to_team(o_grad.reshape(q_width, team, -1).transpose(1, 0, 2)).reshape(width, -1)
    o_weight_grad = join(collect(reorder_rows(o_grad)))

    return (
        block_out,
        input_grad,
        attn_gain_grad,
        q_weight_grad,
        k_weight_grad,
        v_weight_grad,
        o_weight_grad,
        ffn_gain_grad,
        gate_weight_grad,
        up_weight_grad,
        down_weight_grad,
    )


def solution(mesh):
    rows = P(BOTH, None)
    placed = P("fsdp", "cp", None)
    gain = P(BOTH)
    return jax.shard_map(
        body,
        mesh=mesh,
        in_specs=(placed, placed, gain, rows, rows, rows, rows, gain, rows, rows, rows),
        out_specs=(placed, placed, gain, rows, rows, rows, rows, gain, rows, rows, rows),
        check_vma=False,
    )
```

```python
import functools

import jax
import jax.numpy as jnp
from jax import lax
from jax.experimental import pallas as pl
from jax.experimental.pallas import tpu as pltpu
from jax.sharding import PartitionSpec as P

HEADS = 32
KV_HEADS = 8
HEAD_DIM = 64
HALF = HEAD_DIM // 2
NORM_EPS = 1e-05
ROPE_BASE = 500000.0
BOTH = ("fsdp", "cp")
F32 = jnp.float32
BF16 = jnp.bfloat16
MESH = pl.DeviceIdType.MESH
VMEM_BYTES = 60 << 20


def dot(left, right):
    return jnp.dot(left, right, preferred_element_type=F32)


def contract_rows(left, right):
    return lax.dot_general(left, right, (((0,), (0,)), ((), ())), preferred_element_type=F32)


def contract_cols(left, right):
    return lax.dot_general(left, right, (((1,), (1,)), ((), ())), preferred_element_type=F32)


def flip(index, mask):
    bit = 1
    out = index
    while bit <= mask:
        if mask & bit:
            out = out + bit - 2 * bit * ((index // bit) % 2)
        bit *= 2
    return out


def spot_of(diff, team):
    return diff // 2 + (diff % 2) * (team // 2)


def chunk_blocks(member, team):
    second = team + flip(member, team // 2)
    last = 4 * team - 1
    return member, last - member, second, last - second


def natural_unit(mine, index):
    block = flip(mine, index // 2)
    turned = block % 2
    return block * 2 + (index % 2) + turned * (1 - 2 * (index % 2))


def swap_halves(wide):
    pieces = []
    for start in range(0, wide.shape[-1], HEAD_DIM):
        pieces.append(wide[:, start + HALF : start + HEAD_DIM])
        pieces.append(wide[:, start : start + HALF])
    return jnp.concatenate(pieces, axis=-1)


def over_row_blocks(token_count, most, step):
    quarter = token_count // 4
    rows = min(most, (1 << 18) // token_count)
    for first in range(0, token_count, quarter):
        if rows == quarter:
            step(first, first + quarter, first, rows)
        else:

            def block(index, carry, first=first):
                step(first, first + quarter, pl.multiple_of(first + index * rows, rows), rows)
                return carry

            lax.fori_loop(0, quarter // rows, block, 0)


def turn_by(wide, cosine, sine):
    swapped = swap_halves(wide)
    pieces = []
    for start in range(0, wide.shape[-1], 2 * HEAD_DIM):
        piece = slice(start, start + 2 * HEAD_DIM)
        span = wide[:, piece].shape[-1]
        pieces.append(wide[:, piece] * cosine[:, :span] + swapped[:, piece] * sine[:, :span])
    return jnp.concatenate(pieces, axis=-1)


def masked_scores(query, keys, first, start):
    rows, span = query.shape[0], keys.shape[0] - first
    scores = contract_cols(query, keys)
    row = lax.broadcasted_iota(jnp.int32, (rows, span), 0) + (start - first)
    col = lax.broadcasted_iota(jnp.int32, (rows, span), 1)
    last = jnp.where(row >= col, scores[:, first:], -1e30)
    return jnp.concatenate([scores[:, :first], last], axis=-1) if first else last


def differ(left, right, size):
    out = 0
    bit = 1
    while bit < size:
        out = out + ((left // bit + right // bit) % 2) * bit
        bit *= 2
    return out


class Links:
    def __init__(self, cp_size, send, recv, local):
        self.f, self.c = lax.axis_index("fsdp"), lax.axis_index("cp")
        self.cp_size, self.send, self.recv, self.local = cp_size, send, recv, local
        self.used = self.used_local = 0

    def device(self, mask):
        return (flip(self.f, mask // self.cp_size), flip(self.c, mask % self.cp_size))

    def barrier(self, masks):
        sem = pltpu.get_barrier_semaphore()
        for mask in masks:
            pl.semaphore_signal(sem, inc=1, device_id=self.device(mask), device_id_type=MESH)
        pl.semaphore_wait(sem, len(masks))

    def copy(self, src, dst, mask):
        index = self.used
        self.used += 1
        return pltpu.make_async_remote_copy(
            src_ref=src,
            dst_ref=dst,
            send_sem=self.send.at[index],
            recv_sem=self.recv.at[index],
            device_id=self.device(mask),
            device_id_type=MESH,
        )

    def inside(self, src, dst):
        index = self.used_local
        self.used_local += 1
        return pltpu.make_async_copy(src, dst, self.local.at[index])


class TeamGather:
    def __init__(self, links, team, src, dst):
        near = team // 2
        row = range(2, near, 2)

        def place(mask):
            return dst.at[spot_of(mask, team)]

        self.to_near = links.copy(src, place(near), near)
        self.to_row = [links.copy(src, place(m), m) for m in row]
        self.on = [links.copy(place(near), place(near + m), m) for m in row]
        self.to_core = links.copy(src, place(1), 1)
        self.near_core = links.copy(place(near), place(near + 1), 1)
        self.row_core = [links.copy(place(m), place(m + 1), 1) for m in row]
        self.on_core = [links.copy(place(near + m), place(near + m + 1), 1) for m in row]
        self.own = links.inside(src, dst.at[0])

    def start(self):
        self.to_near.start()
        for copy in self.to_row:
            copy.start()
        self.to_core.start()
        self.own.start()

    def pass_near(self):
        self.to_near.wait_recv()
        for copy in self.on:
            copy.start()
        self.near_core.start()

    def pass_row(self):
        for copy, core in zip(self.to_row, self.row_core):
            copy.wait_recv()
            core.start()

    def pass_on(self):
        for copy, core in zip(self.on, self.on_core):
            copy.wait_recv()
            core.start()

    def finish(self):
        core = [self.to_core, self.near_core] + self.row_core + self.on_core
        for copy in core:
            copy.wait_recv()
        for copy in [self.to_near] + self.to_row + self.on + core:
            copy.wait_send()
        self.own.wait()


class TeamSum:
    def __init__(self, links, team, parts, taken, row_in, near_in):
        self.team, self.parts, self.taken, self.row_in, self.near_in = team, parts, taken, row_in, near_in
        near = team // 2
        self.row = list(range(2, near, 2))
        half = team // 2
        self.cross = [links.copy(parts.at[half + e], taken.at[e], 1) for e in range(half)]
        self.far = [links.copy(parts.at[(near + m) // 2], row_in.at[0, i], m) for i, m in enumerate(self.row)]
        self.here = [links.copy(parts.at[m // 2], row_in.at[1, i], m) for i, m in enumerate(self.row)]
        self.last = links.copy(parts.at[near // 2], near_in, near)

    def start(self, make, near_sum, own_sum):
        half, rows, width = self.taken.shape
        pieces = [slice(start, start + 512) for start in range(0, width, 512)]
        for low in range(half - 2, -1, -2):
            for cols in pieces:
                value = make(pl.ds((half + low) * rows, 2 * rows), cols).astype(BF16)
                for k in range(2):
                    self.parts[half + low + k, :, cols] = value[k * rows : (k + 1) * rows]
            self.cross[low + 1].start()
            self.cross[low].start()
        for low in range(half - 2, -1, -2):
            self.cross[low + 1].wait_recv()
            self.cross[low].wait_recv()
            for cols in pieces:
                value = make(pl.ds(low * rows, 2 * rows), cols)
                for k in range(2):
                    spot = low + k
                    part = value[k * rows : (k + 1) * rows] + self.taken[spot, :, cols].astype(F32)
                    if spot == half // 2:
                        near_sum[:, cols] = part
                    elif spot == 0:
                        own_sum[:, cols] = part
                    else:
                        self.parts[spot, :, cols] = part.astype(BF16)
            for spot in (low + 1, low):
                if spot > half // 2:
                    self.far[spot - half // 2 - 1].start()
                elif 0 < spot < half // 2:
                    self.here[spot - 1].start()

    def pass_near(self, value):
        for index, copy in enumerate(self.far):
            copy.wait_recv()
            value = value + self.row_in[0, index].astype(F32)
        self.parts[self.team // 4] = value.astype(BF16)
        self.last.start()

    def total(self, value):
        for index, copy in enumerate(self.here):
            copy.wait_recv()
            value = value + self.row_in[1, index].astype(F32)
        self.last.wait_recv()
        return value + self.near_in[...].astype(F32)

    def finish(self):
        for copy in self.cross + self.far + self.here + [self.last]:
            copy.wait_send()


class Spread:
    def __init__(self, links, team, t, pieces, full):
        self.own = links.inside(pieces(0), full.at[0, t])
        self.cuts = [links.copy(pieces(m), full.at[0, t], m) for m in range(1, team)]
        self.far = [links.copy(full.at[b], full.at[b + 2], links.cp_size) for b in range(2)]
        self.side = links.copy(full.at[0], full.at[1], team + team // 2)

    def cut(self):
        self.own.start()
        for piece in self.cuts:
            piece.start()

    def leave(self):
        self.own.wait()
        for piece in self.cuts:
            piece.wait_recv()
        self.far[0].start()
        self.side.start()

    def arrive(self):
        self.side.wait_recv()
        self.far[1].start()

    def finish(self):
        for copy in self.far:
            copy.wait_recv()
        for copy in self.cuts + self.far + [self.side]:
            copy.wait_send()


class Collect:
    def __init__(self, links, team, t, grad, far_in, side_in, final, out):
        self.grad, self.far_in, self.side_in, self.final = grad, far_in, side_in, final
        self.far = links.copy(grad.at[pl.ds(2, 2)], far_in, links.cp_size)
        self.side = links.copy(grad.at[1], side_in, team + team // 2)
        self.own = links.inside(final.at[t], out.at[t])
        self.cuts = [links.copy(final.at[flip(t, m)], out.at[t], m) for m in range(1, team)]

    def cut(self):
        self.own.start()
        for piece in self.cuts:
            piece.start()

    def finish(self):
        self.own.wait()
        self.far.wait_send()
        self.side.wait_send()
        for piece in self.cuts:
            piece.wait()


def entry_kernel(
    fsdp_size,
    cp_size,
    tokens,
    cotangent,
    gains_in,
    qkv_cut,
    o_cut,
    gate_in,
    up_in,
    down_in,
    cos_ref,
    sin_ref,
    x_ref,
    gains_ref,
    attn_in_ref,
    qkv_full,
    o_wide,
    rot_ref,
    mix_ref,
    resid_ref,
    ffn_in_ref,
    dy_ref,
    gate_full,
    up_full,
    down_full,
    o_full,
    send,
    recv,
    local,
    swapped,
    dy_swapped,
    slots,
    chunk_ref,
    dy_chunk,
    acts,
    wqkv,
    mixed,
    o_pieces,
    taken,
    row_in,
    near_in,
    near_sum,
):
    links = Links(cp_size, send, recv, local)
    f, c = links.f, links.c
    team = cp_size // 2
    near, mirror = team // 2, team + team // 2
    side = c // team
    t = c % team + side * (flip(c, near) - c)
    row_count, width = tokens.shape[1], tokens.shape[2]
    block_len = row_count // 2
    unit = width // 8
    token_count, q_width = mixed.shape
    heads = q_width // HEAD_DIM
    cols = gate_full.shape[-1]
    mine = f * 2 + side

    links.barrier(list(range(1, team)) + [mirror, cp_size])
    swap = links.copy(tokens.at[1 - side], swapped, mirror)
    swap.start()
    slots[0] = gains_in[...]
    stages = []
    size = 1
    for mask in [1 << k for k in range(team.bit_length() - 1)] + [mirror, cp_size]:
        stages.append(links.copy(slots.at[pl.ds(0, size)], slots.at[pl.ds(size, size)], mask))
        size *= 2

    def columns_of(weight):
        return lambda m: weight.at[:, pl.ds(pl.multiple_of(flip(t, m) * cols, cols), cols)]

    def spread(pieces, full):
        return Spread(links, team, t, pieces, full)

    qkv_spread = spread(lambda m: qkv_cut.at[flip(t, m)], qkv_full)
    o_spread = spread(lambda m: o_cut.at[flip(t, m)], o_full)
    gate_spread = spread(columns_of(gate_in), gate_full)
    up_spread = spread(columns_of(up_in), up_full)
    down_spread = spread(columns_of(down_in), down_full)

    stages[0].start()
    qkv_spread.cut()
    o_spread.cut()
    for step in range(1, len(stages)):
        stages[step - 1].wait_recv()
        stages[step].start()
    gate_spread.cut()

    def fill(dst, source, theirs):
        here = pl.ds(pl.multiple_of(side * row_count, row_count), row_count)
        there = pl.ds(pl.multiple_of((1 - side) * row_count, row_count), row_count)
        for index in range(8):
            cols = slice(index * unit, (index + 1) * unit)
            natural = pl.ds(pl.multiple_of(natural_unit(mine, index) * unit, unit), unit)
            dst[here, cols] = source[side, :, natural].astype(dst.dtype)
            dst[there, cols] = theirs[:, natural].astype(dst.dtype)

    stages[-1].wait_recv()
    pieces = []
    for b in range(4):
        for member in range(team):
            pieces.append(slots[b * team + flip(t, member)][:8, : width // (4 * team)])
    gains = jnp.concatenate(pieces, axis=-1).astype(F32)
    gains_ref[...] = gains
    swap.wait_recv()
    fill(x_ref, tokens, swapped)
    x = x_ref[...]
    inv_one = lax.rsqrt(jnp.mean(x * x, axis=-1, keepdims=True) + NORM_EPS)
    chunk_ref[...] = (x * inv_one * gains[0:1]).astype(BF16)
    gather_one = TeamGather(links, team, chunk_ref, acts)
    gather_one.start()
    dy_swap = links.copy(cotangent.at[1 - side], dy_swapped, mirror)
    dy_swap.start()
    qkv_spread.leave()
    o_spread.leave()
    gather_one.pass_near()
    gather_one.pass_row()
    gate_spread.leave()
    gather_one.pass_on()
    up_spread.cut()
    down_spread.cut()
    qkv_spread.arrive()
    o_spread.arrive()
    up_spread.leave()
    qkv_spread.finish()
    load = links.inside(qkv_full, wqkv)
    load.start()
    gather_one.finish()
    attn_out = links.inside(acts, attn_in_ref)
    attn_out.start()
    o_spread.finish()

    o_rows = o_full.shape[2]

    def o_source(m):
        count = q_width // o_rows
        first = flip(t, m) * count
        owners, start = first // team, first % team
        block = ((owners // 2 + mine // 2) % 2) * 2 + (owners + mine) % 2
        return o_full.at[block, pl.ds(start + (owners % 2) * (flip(start, near) - start), count)]

    o_own = links.inside(o_source(0), o_pieces.at[t])
    o_sends = [links.copy(o_source(m), o_pieces.at[t], m) for m in range(1, team)]
    o_own.start()
    for copy in o_sends:
        copy.start()

    load.wait()
    weights = wqkv[...].reshape(width, wqkv.shape[-1])

    def project(m, carry):
        proj = dot(acts[spot_of(m, team)], weights)
        keys = proj[:, q_width : q_width + HEAD_DIM]
        qk = jnp.concatenate([proj[:, :q_width] * HEAD_DIM ** (-0.5), keys], axis=-1)
        blocks = chunk_blocks(differ(t, m, team), team)
        for slot in range(4):
            piece = slice(slot * block_len, (slot + 1) * block_len)
            rows = pl.ds(pl.multiple_of(blocks[slot] * block_len, block_len), block_len)
            turned = turn_by(qk[piece], cos_ref[rows, :], sin_ref[rows, :])
            rot_ref[rows, :] = jnp.concatenate([turned, proj[piece, q_width + HEAD_DIM :]], axis=-1).astype(BF16)
        return carry

    lax.fori_loop(0, team, project, 0)

    dy_swap.wait_recv()
    fill(dy_chunk, cotangent, dy_swapped)
    gather_dy = TeamGather(links, team, dy_chunk, dy_ref)
    gather_dy.start()
    down_spread.leave()

    def attend(first, span, start, rows):
        keys = rot_ref[:span, q_width : q_width + HEAD_DIM]
        values = rot_ref[:span, q_width + HEAD_DIM :]
        outs = []
        for head in range(heads):
            query = rot_ref[pl.ds(start, rows), head * HEAD_DIM : (head + 1) * HEAD_DIM]
            scores = masked_scores(query, keys, first, start)
            peak = jnp.max(scores, axis=-1, keepdims=True)
            expo = jnp.exp(scores - peak)
            total = jnp.sum(expo, axis=-1, keepdims=True)
            outs.append(dot(expo.astype(BF16), values) / total)
        mixed[pl.ds(start, rows), :] = jnp.concatenate(outs, axis=-1).astype(BF16)

    over_row_blocks(token_count, 256, attend)
    gather_dy.pass_near()

    def collect_mix(m, carry):
        blocks = chunk_blocks(differ(t, m, team), team)
        for slot in range(4):
            where = pl.ds(pl.multiple_of(blocks[slot] * block_len, block_len), block_len)
            mix_ref[spot_of(m, team), slot * block_len : (slot + 1) * block_len, :] = mixed[where, :]
        return carry

    lax.fori_loop(0, team, collect_mix, 0)
    for copy in o_sends:
        copy.wait_recv()
    o_own.wait()
    span = width // team
    for index in range(8):
        for piece in range(team // 8):
            start = index * unit + piece * span
            source = natural_unit(mine, index) * (team // 8) + piece
            o_wide[:, start : start + span] = o_pieces[source].reshape(q_width, span)

    attn_out.wait()
    summed = TeamSum(links, team, acts, taken, row_in, near_in)
    row_pair = 2 * row_count
    gather_dy.pass_row()

    def mix_out(place, cols):
        spots = pl.ds(place.start // row_pair, 2)
        return dot(mix_ref[spots].reshape(2 * row_pair, q_width), o_wide[:, cols])

    summed.start(mix_out, near_sum, resid_ref)
    summed.pass_near(near_sum[...])
    gather_dy.pass_on()
    resid_ref[...] = x_ref[...] + summed.total(resid_ref[...])
    resid = resid_ref[...]
    inv_two = lax.rsqrt(jnp.mean(resid * resid, axis=-1, keepdims=True) + NORM_EPS)
    chunk_ref[...] = (resid * inv_two * gains_ref[1:2]).astype(BF16)
    gather_two = TeamGather(links, team, chunk_ref, ffn_in_ref)
    gather_two.start()
    gather_dy.finish()
    gate_spread.arrive()
    gather_two.pass_near()
    gather_two.pass_row()
    gather_two.pass_on()
    up_spread.arrive()
    gate_spread.finish()
    down_spread.arrive()
    gather_two.finish()
    up_spread.finish()
    down_spread.finish()
    swap.wait_send()
    dy_swap.wait_send()
    summed.finish()
    for copy in stages + o_sends:
        copy.wait_send()


def backward_heads(token_count, q_width, rot_ref, wide_ref, cos_ref, sin_ref, dq_ref, dkv_ref):
    heads = q_width // HEAD_DIM
    dkv_ref[...] = jnp.zeros_like(dkv_ref)

    def attend(first, span, start, count):
        rows = pl.ds(start, count)
        keys = rot_ref[:span, q_width : q_width + HEAD_DIM]
        values = rot_ref[:span, q_width + HEAD_DIM :]
        for head in range(heads):
            cols = slice(head * HEAD_DIM, (head + 1) * HEAD_DIM)
            query = rot_ref[rows, cols]
            grad = wide_ref[rows, cols]
            scores = masked_scores(query, keys, first, start)
            peak = jnp.max(scores, axis=-1, keepdims=True)
            expo = jnp.exp(scores - peak)
            probs = expo / jnp.sum(expo, axis=-1, keepdims=True)
            dprob = contract_cols(grad, values)
            delta = jnp.sum(probs * dprob, axis=-1, keepdims=True)
            score_grad = (probs * (dprob - delta)).astype(BF16)
            dq_ref[rows, cols] = dot(score_grad, keys)
            dk = contract_rows(score_grad, query)
            dv = contract_rows(probs.astype(BF16), grad)
            dkv_ref[:span, :] += jnp.concatenate([dk, dv], axis=-1)

    over_row_blocks(token_count, 128, attend)

    for start in range(0, token_count, token_count // 4):
        rows = slice(start, start + token_count // 4)
        qk = jnp.concatenate([dq_ref[rows, :], dkv_ref[rows, :HEAD_DIM]], axis=-1)
        turned = turn_by(qk, cos_ref[rows, :], -sin_ref[rows, :])
        dq_ref[rows, :] = turned[:, :q_width] * HEAD_DIM ** (-0.5)
        dkv_ref[rows, :] = jnp.concatenate([turned[:, q_width:], dkv_ref[rows, HEAD_DIM:]], axis=-1)


def scatter_chunk(t, m, team, block_len, wide_ref, value):
    blocks = chunk_blocks(differ(t, m, team), team)
    for slot in range(4):
        where = pl.ds(pl.multiple_of(blocks[slot] * block_len, block_len), block_len)
        wide_ref[where, :] = value[slot * block_len : (slot + 1) * block_len, :]


def gather_chunk(t, m, team, block_len, out_ref, *sources):
    blocks = chunk_blocks(differ(t, m, team), team)
    for slot in range(4):
        rows = pl.ds(pl.multiple_of(blocks[slot] * block_len, block_len), block_len)
        place = pl.ds(pl.multiple_of((spot_of(m, team) * 4 + slot) * block_len, block_len), block_len)
        piece = jnp.concatenate([source[rows, :] for source in sources], axis=-1)
        out_ref[place, :] = piece.astype(BF16)


def attention_backward(
    team, block_len, q_width, where_ref, rot_ref, grad_ref, cos_ref, sin_ref, out_ref, wide_ref, dq_ref, dkv_ref
):
    t = where_ref[0]

    def place_grad(m, carry):
        scatter_chunk(t, m, team, block_len, wide_ref, grad_ref[spot_of(m, team)])
        return carry

    lax.fori_loop(0, team, place_grad, 0)
    backward_heads(wide_ref.shape[0], q_width, rot_ref, wide_ref, cos_ref, sin_ref, dq_ref, dkv_ref)

    def give_chunk(m, carry):
        gather_chunk(t, m, team, block_len, out_ref, dq_ref, dkv_ref)
        return carry

    lax.fori_loop(0, team, give_chunk, 0)


def exit_kernel(
    cp_size,
    x_ref,
    resid_ref,
    gains_ref,
    rot_ref,
    mix_ref,
    o_wide,
    cos_ref,
    sin_ref,
    attn_in,
    ffn_in,
    dy,
    gate_in,
    up_in,
    down_in,
    qkv_in,
    block_out,
    input_grad,
    gain_grads,
    gate_out,
    up_out,
    down_out,
    qkv_out,
    o_out,
    branch,
    gate_grad,
    gate_far,
    gate_side,
    gate_final,
    up_grad,
    up_far,
    up_side,
    up_final,
    down_grad,
    down_far,
    down_side,
    down_final,
    qkv_grad,
    qkv_far,
    qkv_side,
    qkv_final,
    send,
    recv,
    local,
    store_sem,
    load_sem,
    first,
    second,
    gate_w,
    up_w,
    down_w,
    qkv_w,
    parts,
    hidden,
    both,
    stage_out,
    stage_in,
    taken_one,
    row_one,
    near_one,
    taken_two,
    row_two,
    near_two,
    resid_grad,
    near_sum,
    own_sum,
    chunk_ref,
    grad_rows,
    wide,
    dq_ref,
    dkv_ref,
    proj_grad,
    o_far,
    o_two,
    o_side,
    o_final,
    gain_slots,
    gain_in,
):
    links = Links(cp_size, send, recv, local)
    f, c = links.f, links.c
    team = cp_size // 2
    near, mirror = team // 2, team + team // 2
    side = c // team
    t = c % team + side * (flip(c, near) - c)
    mine = f * 2 + side
    half = team // 2
    token_count, width = first.shape
    rows = token_count // team
    row_count = rows // 2
    block_len = row_count // 2
    unit = width // 8
    cols = hidden.shape[1]
    q_width = wide.shape[1]
    weight_rows = gate_grad.shape[2]

    links.barrier(list(range(1, team)) + [mirror, cp_size])
    loads = [
        links.inside(source, target)
        for source, target in (
            (ffn_in, first),
            (gate_in, gate_w),
            (up_in, up_w),
            (dy, second),
            (down_in, down_w),
            (qkv_in, qkv_w),
        )
    ]
    for load in loads:
        load.start()
    for load in loads[:3]:
        load.wait()

    steps = token_count // 256

    def forward(index, carry):
        place = pl.ds(pl.multiple_of(index * 256, 256), 256)
        spots = pl.ds(index * (256 // rows), 256 // rows)
        block = first[place, :]
        for start in range(0, cols, 256):
            cut = slice(start, start + 256)
            later = slice(cols + start, cols + start + 256)
            gate = dot(block, gate_w[:, cut])
            up_val = dot(block, up_w[:, cut])
            sigma = jax.nn.sigmoid(gate)
            silu_val = gate * sigma
            hidden[place, cut] = (silu_val * up_val).astype(BF16)
            factor = up_val * (sigma + silu_val * (1.0 - sigma))
            parts[spots, :, cut] = silu_val.astype(BF16).reshape(256 // rows, rows, 256)
            parts[spots, :, later] = factor.astype(BF16).reshape(256 // rows, rows, 256)
        return carry

    lax.fori_loop(0, steps, forward, 0)

    def produce(left, right, widths, start, count, targets, adds):
        def one(index, carry):
            place = start + index
            slot = index % 2
            block, part = place // 2, pl.ds((place % 2) * half, half)
            waits = []
            for a, sources in enumerate(adds):
                for k, source in enumerate(sources):
                    load = pltpu.make_async_copy(
                        source(block, part), stage_in.at[a, k, :, :, : widths[k]], load_sem.at[a, k]
                    )
                    load.start()
                    waits.append(load)
            stores = [
                pltpu.make_async_copy(
                    stage_out.at[slot, k, :, :, : widths[k]], target(block, part), store_sem.at[slot, k]
                )
                for k, target in enumerate(targets)
            ]

            @pl.when(index >= 2)
            def _():
                for store in stores:
                    store.wait()

            turned = left[:, pl.ds(pl.multiple_of(place * unit, unit), unit)].T
            offset = 0
            for k, span in enumerate(widths):
                value = dot(turned, right[:, offset : offset + span]).reshape(half, weight_rows, span)
                for a in range(len(adds)):
                    waits[a * len(widths) + k].wait()
                    value = value + stage_in[a, k, :, :, :span].astype(F32)
                stage_out[slot, k, :, :, :span] = value.astype(BF16)
                stores[k].start()
                offset += span
            return carry

        lax.fori_loop(0, count, one, 0)
        for index in range(max(0, count - 2), count):
            for k, target in enumerate(targets):
                pltpu.make_async_copy(
                    stage_out.at[index % 2, k, :, :, : widths[k]], target(0, pl.ds(0, half)), store_sem.at[index % 2, k]
                ).wait()

    def in_block(ref):
        return lambda block, part: ref.at[block, part]

    def in_side(ref):
        return lambda block, part: ref.at[part]

    def give_far(left, right, widths, collects):
        produce(left, right, widths, 4, 4, [in_block(k.grad) for k in collects], [])
        for collect in collects:
            collect.far.start()

    def give_side(left, right, widths, collects):
        for collect in collects:
            collect.far.wait_recv()
        produce(
            left, right, widths, 2, 2, [in_block(k.grad) for k in collects], [[in_block(k.far_in) for k in collects]]
        )
        for collect in collects:
            collect.side.start()

    def give_final(left, right, widths, collects):
        for collect in collects:
            collect.side.wait_recv()
        produce(
            left,
            right,
            widths,
            0,
            2,
            [in_side(k.final) for k in collects],
            [[in_block(k.far_in) for k in collects], [in_side(k.side_in) for k in collects]],
        )
        for collect in collects:
            collect.cut()

    gate_sum = Collect(links, team, t, gate_grad, gate_far, gate_side, gate_final, gate_out)
    up_sum = Collect(links, team, t, up_grad, up_far, up_side, up_final, up_out)
    down_sum = Collect(links, team, t, down_grad, down_far, down_side, down_final, down_out)
    qkv_sum = Collect(links, team, t, qkv_grad, qkv_far, qkv_side, qkv_final, qkv_out)

    loads[3].wait()
    give_far(second, hidden, [cols], [down_sum])
    loads[4].wait()

    def backward(index, carry):
        place = pl.ds(pl.multiple_of(index * 256, 256), 256)
        spots = pl.ds(index * (256 // rows), 256 // rows)
        block = second[place, :]
        for start in range(0, cols, 256):
            cut = slice(start, start + 256)
            later = slice(cols + start, cols + start + 256)
            hidden_grad = dot(block, down_w[:, cut])
            silu_val = parts[spots, :, cut].reshape(256, 256).astype(F32)
            factor = parts[spots, :, later].reshape(256, 256).astype(F32)
            both[place, cut] = (hidden_grad * factor).astype(BF16)
            both[place, later] = (hidden_grad * silu_val).astype(BF16)
        return carry

    lax.fori_loop(0, steps, backward, 0)

    def team_sum(taken, row_in, near_in, make):
        summed = TeamSum(links, team, parts, taken, row_in, near_in)
        summed.start(make, near_sum, own_sum)
        return summed

    def finish_sum(summed):
        summed.pass_near(near_sum[...])
        value = summed.total(own_sum[...])
        summed.finish()
        return value

    ffn_sum = team_sum(
        taken_one,
        row_one,
        near_one,
        lambda place, cut: contract_cols(both[place, :cols], gate_w[cut, :]) + contract_cols(both[place, cols:], up_w[cut, :]),
    )
    ffn_sum.pass_near(near_sum[...])
    give_far(first, both, [cols, cols], [gate_sum, up_sum])
    ffn_in_grad = ffn_sum.total(own_sum[...])
    ffn_sum.finish()

    def place_gain(row, value):
        share = width // (4 * team)
        for b in range(4):
            for member in range(team):
                start = (b * team + member) * share
                gain_slots[b * team + flip(t, member), row : row + 1, :share] = value[:, start : start + share]

    gain_slots[...] = jnp.zeros_like(gain_slots)
    resid = resid_ref[...]
    inv_two = lax.rsqrt(jnp.mean(resid * resid, axis=-1, keepdims=True) + NORM_EPS)
    normed = resid * inv_two
    place_gain(1, jnp.sum(ffn_in_grad * normed, axis=0, keepdims=True))
    scaled = ffn_in_grad * gains_ref[1:2]
    value = second[:rows, :].astype(F32) + inv_two * (
        scaled - normed * jnp.mean(scaled * normed, axis=-1, keepdims=True)
    )
    resid_grad[...] = value
    chunk_ref[...] = value.astype(BF16)
    gather = TeamGather(links, team, chunk_ref, branch)
    gather.start()
    give_side(second, hidden, [cols], [down_sum])
    gather.pass_near()
    gather.pass_row()
    gather.pass_on()
    gather.finish()
    load = links.inside(branch, parts)
    load.start()
    load.wait()

    for low in range(0, team, 2):
        value = contract_cols(parts[low : low + 2].reshape(2 * rows, width), o_wide[...]).astype(BF16)
        for spot in range(2):
            m = 2 * (low + spot) if low + spot < half else 2 * (low + spot - half) + 1
            scatter_chunk(t, m, team, block_len, wide, value[spot * rows : (spot + 1) * rows])

    def head_rows(member):
        return pl.ds(pl.multiple_of(member * q_width, q_width), q_width)

    span = width // team
    turned = mix_ref[...].reshape(token_count, q_width).T
    for index in range(8):
        value = dot(turned, parts[:, :, index * unit : (index + 1) * unit].reshape(token_count, unit)).astype(BF16)
        for piece in range(team // 8):
            target = natural_unit(mine, index) * (team // 8) + piece
            gate_w[head_rows(target), span : 2 * span] = value[:, piece * span : (piece + 1) * span]
    quarter = width // 4
    o_place = gate_w.at[head_rows(t), pl.ds(0, span)]

    def o_part(member):
        return gate_w.at[head_rows(member), pl.ds(span, span)]

    def o_land(block):
        return gate_w[pl.ds(pl.multiple_of(block * quarter, quarter), quarter), :span].astype(F32)

    o_own = links.inside(o_part(t), o_place)
    o_sends = [links.copy(o_part(flip(t, m)), o_place, m) for m in range(1, team)]
    o_own.start()
    for copy in o_sends:
        copy.start()

    out_sum = team_sum(taken_two, row_two, near_two, lambda place, cut: contract_cols(hidden[place, :], down_w[cut, :]))
    backward_heads(token_count, q_width, rot_ref, wide, cos_ref, sin_ref, dq_ref, dkv_ref)

    def give_chunk(m, carry):
        gather_chunk(t, m, team, block_len, proj_grad, dq_ref, dkv_ref)
        return carry

    lax.fori_loop(0, team, give_chunk, 0)

    def give_rows(value, target, out):
        for index in range(8):
            natural = pl.ds(pl.multiple_of(natural_unit(mine, index) * unit, unit), unit)
            target[:, natural] = value[:, index * unit : (index + 1) * unit].astype(BF16)
        here = pl.ds(pl.multiple_of(side * row_count, row_count), row_count)
        there = pl.ds(pl.multiple_of((1 - side) * row_count, row_count), row_count)
        own = links.inside(target.at[here], out.at[side])
        other = links.copy(target.at[there], out.at[side], mirror)
        own.start()
        other.start()
        return own, other

    out_copies = give_rows(resid_ref[...] + finish_sum(out_sum), chunk_ref, block_out)
    qkv_width = q_width + 2 * HEAD_DIM
    loads[5].wait()
    attn_sum = team_sum(
        taken_one,
        row_one,
        near_one,
        lambda place, cut: contract_cols(proj_grad[place, :], qkv_w[cut, :]),
    )
    attn_load = links.inside(attn_in, second)
    give_final(second, hidden, [cols], [down_sum])
    attn_load.start()
    for copy in o_sends:
        copy.wait_recv()
    o_own.wait()
    other_half = pl.ds(pl.multiple_of((1 - f) * 2 * quarter, 2 * quarter), 2 * quarter)
    o_across = links.copy(gate_w.at[other_half, pl.ds(0, span)], o_far, cp_size)
    o_across.start()
    give_side(first, both, [cols, cols], [gate_sum, up_sum])
    attn_load.wait()
    attn_in_grad = finish_sum(attn_sum)

    x = x_ref[...]
    inv_one = lax.rsqrt(jnp.mean(x * x, axis=-1, keepdims=True) + NORM_EPS)
    normed = x * inv_one
    place_gain(0, jnp.sum(attn_in_grad * normed, axis=0, keepdims=True))
    size = 2 * team
    gain_steps = []
    for mask in [cp_size, mirror] + [1 << k for k in reversed(range(team.bit_length() - 1))]:
        gain_steps.append(links.copy(gain_slots.at[pl.ds(size, size)], gain_in.at[pl.ds(size, size)], mask))
        size //= 2
    gain_steps[0].start()
    scaled = attn_in_grad * gains_ref[0:1]
    value = resid_grad[...] + inv_one * (scaled - normed * jnp.mean(scaled * normed, axis=-1, keepdims=True))
    grad_copies = give_rows(value, grad_rows, input_grad)

    give_far(second, proj_grad, [qkv_width], [qkv_sum])
    o_across.wait_recv()

    def o_came(block):
        return o_far[pl.ds(pl.multiple_of(block * quarter, quarter), quarter), :].astype(F32)

    o_two[...] = (o_land(f * 2 + 1 - side) + o_came(1 - side)).astype(BF16)
    o_cross = links.copy(o_two, o_side, mirror)
    o_cross.start()
    size = 2 * team
    for index, step in enumerate(gain_steps):
        step.wait_recv()
        gain_slots[:size] += gain_in[size : 2 * size]
        size //= 2
        if index + 1 < len(gain_steps):
            gain_steps[index + 1].start()
    gain_grads[...] = gain_slots[0]
    give_side(second, proj_grad, [qkv_width], [qkv_sum])
    o_cross.wait_recv()
    o_final[...] = (o_land(f * 2 + side) + o_came(side) + o_side[...].astype(F32)).astype(BF16)

    def o_rows(member):
        place = member + side * (flip(member, near) - member)
        return o_final.at[pl.ds(pl.multiple_of(place * weight_rows, weight_rows), weight_rows)]

    o_last = links.inside(o_rows(t), o_out.at[t])
    o_gives = [links.copy(o_rows(flip(t, m)), o_out.at[t], m) for m in range(1, team)]
    o_last.start()
    for copy in o_gives:
        copy.start()
    give_final(first, both, [cols, cols], [gate_sum, up_sum])
    give_final(second, proj_grad, [qkv_width], [qkv_sum])
    for own, other in (out_copies, grad_copies):
        own.wait()
        other.wait()
    for copy in o_sends + [o_across, o_cross] + gain_steps:
        copy.wait_send()
    for copy in o_gives:
        copy.wait()
    o_last.wait()
    for collect in (down_sum, gate_sum, up_sum, qkv_sum):
        collect.finish()


def vmem():
    return pl.BlockSpec(memory_space=pltpu.VMEM)


def smem():
    return pl.BlockSpec(memory_space=pltpu.SMEM)


def anywhere():
    return pl.BlockSpec(memory_space=pl.ANY)


def body(
    tokens,
    cotangent,
    attn_gain,
    q_weight,
    k_weight,
    v_weight,
    o_weight,
    ffn_gain,
    gate_weight,
    up_weight,
    down_weight,
):
    fsdp_size, cp_size = lax.axis_size("fsdp"), lax.axis_size("cp")
    devices = fsdp_size * cp_size
    teams, row_count, width = tokens.shape
    team = cp_size // teams
    mirror = team + team // 2
    block_len = row_count // 2
    chunk = teams * row_count
    token_count = team * chunk
    f = lax.axis_index("fsdp")
    c = lax.axis_index("cp")
    side = c // team
    t = c % team ^ (team // 2 * side)
    q_width = HEADS // team * HEAD_DIM
    copies = team // KV_HEADS
    qkv_width = q_width + 2 * HEAD_DIM
    weight_rows = q_weight.shape[0]
    hidden_cols = gate_weight.shape[1] // team
    team_groups = [[k * team + i for i in range(team)] for k in range(teams)]

    def swap(value, mask):
        return lax.ppermute(value, BOTH, [(i, i ^ mask) for i in range(devices)])

    def turn(value):
        half = team // 2
        return jnp.where(side == 1, jnp.concatenate([value[half:], value[:half]], axis=0), value)

    def to_team(value):
        return turn(lax.all_to_all(turn(value), "cp", 0, 0, axis_index_groups=team_groups, tiled=True))

    def swap_blocks(blocks):
        blocks = jnp.where(f == 1, blocks[:, ::-1], blocks)
        return jnp.where(side == 1, blocks[:, :, ::-1], blocks)

    def turn_second(blocks):
        return jnp.concatenate([blocks[:, :, :1], blocks[:, :, 1:, ::-1]], axis=2)

    def reorder_rows(value):
        blocks = value.reshape(1, 2, 2, 2, width // 8, -1)
        return swap_blocks(turn_second(blocks)).reshape(value.shape)

    def restore(value):
        blocks = value.reshape(-1, 2, 2, 2, width // 8)
        return turn_second(swap_blocks(blocks)).reshape(value.shape)

    def give_rows(value):
        first, second = value[:row_count], value[row_count:]
        mine = jnp.where(side == 0, first, second)
        theirs = swap(jnp.where(side == 0, second, first), mirror)
        return jnp.stack([jnp.where(side == 0, mine, theirs), jnp.where(side == 0, theirs, mine)], axis=0)

    def team_gather(value):
        evens = jnp.concatenate([value] + [swap(value, m) for m in range(2, team, 2)], axis=0)
        return jnp.concatenate([evens, swap(evens, 1)], axis=0)

    def team_reduce(make):
        theirs = swap(make(1), 1)
        evens = (make(0).astype(F32) + theirs.astype(F32)).astype(BF16).reshape(team // 2, chunk, width)
        total = evens[0].astype(F32)
        for m in range(2, team, 2):
            total = total + swap(evens[m // 2], m).astype(F32)
        return total

    def scatter_small(value):
        for bit in reversed(range(devices.bit_length() - 1)):
            mask = 1 << bit
            index = (f * cp_size + c) & mask
            half = value.shape[-1] // 2
            low, high = value[..., :half], value[..., half:]
            theirs = swap(jnp.where(index == 0, high, low), mask)
            value = jnp.where(index == 0, low, high) + theirs
        return value

    def collect(value):
        cols = value.shape[-1]
        blocks = value.reshape(fsdp_size, teams, -1, cols)
        theirs = swap(blocks[1], cp_size)
        blocks = (blocks[0].astype(F32) + theirs.astype(F32)).astype(BF16)
        theirs = swap(blocks[1], mirror)
        own = (blocks[0].astype(F32) + theirs.astype(F32)).astype(BF16)
        return to_team(own.reshape(team, -1, cols))

    def cut(weight):
        return weight.reshape(weight_rows, team, -1).transpose(1, 0, 2)

    def join(pieces):
        return pieces.transpose(1, 0, 2).reshape(pieces.shape[1], -1).astype(F32)

    def repeat_heads(weight):
        heads = weight.reshape(weight_rows, KV_HEADS, HEAD_DIM)
        return jnp.repeat(heads, copies, axis=1).reshape(weight_rows, -1)

    def sum_heads(pieces):
        grouped = pieces.astype(F32).reshape(KV_HEADS, copies, -1, HEAD_DIM).sum(axis=1)
        return grouped.transpose(1, 0, 2).reshape(grouped.shape[1], -1)

    inverse = ROPE_BASE ** (-(2.0 * jnp.arange(HALF, dtype=F32)) / HEAD_DIM)
    angle = jnp.arange(token_count, dtype=jnp.int32).astype(F32)[:, None] * inverse[None, :]
    cosine, sine = jnp.cos(angle), jnp.sin(angle)
    cos_table = jnp.concatenate([cosine] * 4, axis=-1)
    sin_table = jnp.concatenate([-sine, sine] * 2, axis=-1)

    qkv_cut = jnp.concatenate([cut(q_weight), cut(repeat_heads(k_weight)), cut(repeat_heads(v_weight))], axis=-1)
    o_cut = cut(o_weight)
    gains_in = jnp.pad(jnp.stack([attn_gain, ffn_gain]), ((0, 14), (0, 128 - weight_rows)))

    def hbm(*shape):
        return jax.ShapeDtypeStruct(shape, BF16)

    out_shape = (
        jax.ShapeDtypeStruct((chunk, width), F32),
        jax.ShapeDtypeStruct((8, width), F32),
        hbm(team, chunk, width),
        hbm(4, team, weight_rows, qkv_width),
        hbm(q_width, width),
        hbm(token_count, qkv_width),
        hbm(team, chunk, q_width),
        jax.ShapeDtypeStruct((chunk, width), F32),
        hbm(team, chunk, width),
        hbm(team, chunk, width),
        hbm(4, team, weight_rows, hidden_cols),
        hbm(4, team, weight_rows, hidden_cols),
        hbm(4, team, weight_rows, hidden_cols),
        hbm(4, team, weight_rows, width // team),
    )
    spaces = [vmem(), vmem(), anywhere(), anywhere(), vmem(), vmem(), vmem(), vmem()] + [anywhere()] * 6
    outs = pl.pallas_call(
        functools.partial(entry_kernel, fsdp_size, cp_size),
        out_shape=out_shape,
        in_specs=[vmem(), vmem(), vmem()] + [anywhere()] * 5 + [vmem()] * 2,
        out_specs=tuple(spaces),
        scratch_shapes=[
            pltpu.SemaphoreType.DMA((10 * team + 48,)),
            pltpu.SemaphoreType.DMA((10 * team + 48,)),
            pltpu.SemaphoreType.DMA((16,)),
            pltpu.VMEM((row_count, width), BF16),
            pltpu.VMEM((row_count, width), BF16),
            pltpu.VMEM((devices, 16, 128), BF16),
            pltpu.VMEM((chunk, width), BF16),
            pltpu.VMEM((chunk, width), BF16),
            pltpu.VMEM((team, chunk, width), BF16),
            pltpu.VMEM((4, team, weight_rows, qkv_width), BF16),
            pltpu.VMEM((token_count, q_width), BF16),
            pltpu.VMEM((team, q_width // weight_rows, weight_rows, width // team), BF16),
            pltpu.VMEM((team // 2, chunk, width), BF16),
            pltpu.VMEM((2, team // 4 - 1, chunk, width), BF16),
            pltpu.VMEM((chunk, width), BF16),
            pltpu.VMEM((chunk, width), F32),
        ],
        compiler_params=pltpu.CompilerParams(
            collective_id=0, has_side_effects=True, vmem_limit_bytes=VMEM_BYTES
        ),
        name="entry",
    )(tokens, cotangent, gains_in, qkv_cut, o_cut, gate_weight, up_weight, down_weight, cos_table, sin_table)
    x_float, gains, attn_in, qkv_team, o_team, rot, mix, resid, ffn_in, dy_team, gate_team, up_team, down_team = outs[:13]
    gain_one, gain_two = gains[0:1], gains[1:2]
    attn_in = attn_in.reshape(token_count, width)
    ffn_in = ffn_in.reshape(token_count, width)
    dy_low = dy_team[0]
    dy_team = dy_team.reshape(token_count, width)
    qkv_team = qkv_team.reshape(width, qkv_width)
    gate_team, up_team, down_team = (w.reshape(width, hidden_cols) for w in (gate_team, up_team, down_team))
    mix = mix.reshape(token_count, q_width)

    def f32(*shape):
        return jax.ShapeDtypeStruct(shape, F32)

    def buffers(cols):
        part = (team, weight_rows, cols)
        return hbm(4, *part), hbm(2, *part), hbm(*part), hbm(*part)

    def scratch(*shape, dtype=BF16):
        return pltpu.VMEM(shape, dtype)

    if 2 * hidden_cols == width and KV_HEADS == team:
        half = team // 2
        span = width // team
        sums = [scratch(half, chunk, width), scratch(2, team // 4 - 1, chunk, width), scratch(chunk, width)]
        results = pl.pallas_call(
            functools.partial(exit_kernel, cp_size),
            out_shape=(
                hbm(teams, row_count, width),
                hbm(teams, row_count, width),
                f32(8, 128),
                hbm(team, weight_rows, hidden_cols),
                hbm(team, weight_rows, hidden_cols),
                hbm(team, weight_rows, hidden_cols),
                hbm(team, weight_rows, qkv_width),
                hbm(team, weight_rows, span),
                hbm(team, chunk, width),
                *buffers(hidden_cols),
                *buffers(hidden_cols),
                *buffers(hidden_cols),
                *buffers(qkv_width),
            ),
            in_specs=[vmem()] * 8 + [anywhere()] * 7,
            out_specs=tuple([anywhere()] * 2 + [vmem()] + [anywhere()] * 22),
            scratch_shapes=[
                pltpu.SemaphoreType.DMA((10 * team + 48,)),
                pltpu.SemaphoreType.DMA((10 * team + 48,)),
                pltpu.SemaphoreType.DMA((32,)),
                pltpu.SemaphoreType.DMA((2, 2)),
                pltpu.SemaphoreType.DMA((2, 2)),
                scratch(token_count, width),
                scratch(token_count, width),
                scratch(width, hidden_cols),
                scratch(width, hidden_cols),
                scratch(width, hidden_cols),
                scratch(width, qkv_width),
                scratch(team, chunk, width),
                scratch(token_count, hidden_cols),
                scratch(token_count, 2 * hidden_cols),
                scratch(2, 2, half, weight_rows, hidden_cols),
                scratch(2, 2, half, weight_rows, hidden_cols),
                *sums,
                *sums,
                scratch(chunk, width, dtype=F32),
                scratch(chunk, width, dtype=F32),
                scratch(chunk, width, dtype=F32),
                scratch(chunk, width),
                scratch(chunk, width),
                scratch(token_count, q_width),
                scratch(token_count, q_width, dtype=F32),
                scratch(token_count, 2 * HEAD_DIM, dtype=F32),
                scratch(token_count, qkv_width),
                scratch(width // 2, span),
                scratch(width // 4, span),
                scratch(width // 4, span),
                scratch(width // 4, span),
                scratch(devices, 8, 128, dtype=F32),
                scratch(devices, 8, 128, dtype=F32),
            ],
            compiler_params=pltpu.CompilerParams(
                collective_id=1, has_side_effects=True, vmem_limit_bytes=63 << 20
            ),
            name="exit",
        )(
            x_float,
            resid,
            gains,
            rot,
            mix.reshape(team, chunk, q_width),
            o_team,
            cos_table,
            sin_table,
            attn_in,
            ffn_in,
            dy_team,
            gate_team,
            up_team,
            down_team,
            qkv_team,
        )
        block_out, input_grad, gain_grads, gate_parts, up_parts, down_parts, qkv_parts, o_parts = results[:8]
        return (
            block_out,
            input_grad,
            gain_grads[0, :weight_rows],
            join(qkv_parts[:, :, :q_width]),
            sum_heads(qkv_parts[:, :, q_width : q_width + HEAD_DIM]),
            sum_heads(qkv_parts[:, :, q_width + HEAD_DIM :]),
            join(o_parts),
            gain_grads[1, :weight_rows],
            join(gate_parts),
            join(up_parts),
            join(down_parts),
        )

    inv_one = lax.rsqrt(jnp.mean(x_float * x_float, axis=-1, keepdims=True) + NORM_EPS)
    normed_one = x_float * inv_one
    inv_two = lax.rsqrt(jnp.mean(resid * resid, axis=-1, keepdims=True) + NORM_EPS)
    normed_two = resid * inv_two

    gate = dot(ffn_in, gate_team)
    up_val = dot(ffn_in, up_team)
    sigma = jax.nn.sigmoid(gate)
    silu_val = gate * sigma
    hidden = (silu_val * up_val).astype(BF16)
    hidden_grad = dot(dy_team, down_team)
    gate_grad = (hidden_grad * up_val * (sigma + gate * sigma * (1.0 - sigma))).astype(BF16)
    up_grad = (hidden_grad * silu_val).astype(BF16)

    half = token_count // 2

    def half_of(value, odd):
        return value[half * odd : half * (odd + 1)]

    ffn_in_grad = team_reduce(
        lambda odd: (
            contract_cols(half_of(gate_grad, odd), gate_team) + contract_cols(half_of(up_grad, odd), up_team)
        ).astype(BF16)
    )
    down_sum = team_reduce(lambda odd: contract_cols(half_of(hidden, odd), down_team).astype(BF16))
    block_out = give_rows(restore((resid + down_sum).astype(BF16)))

    ffn_gain_grad = scatter_small(restore(jnp.sum(ffn_in_grad * normed_two, axis=0)))
    scaled_two = ffn_in_grad * gain_two
    resid_grad = dy_low.astype(F32) + inv_two * (
        scaled_two - normed_two * jnp.mean(scaled_two * normed_two, axis=-1, keepdims=True)
    )
    branch_grad = team_gather(resid_grad.astype(BF16))
    mix_grad = contract_cols(branch_grad, o_team).astype(BF16).reshape(team, chunk, q_width)

    down_weight_grad = join(collect(contract_rows(dy_team, hidden).astype(BF16)))
    gate_weight_grad = join(collect(contract_rows(ffn_in, gate_grad).astype(BF16)))
    up_weight_grad = join(collect(contract_rows(ffn_in, up_grad).astype(BF16)))

    proj_grad = pl.pallas_call(
        functools.partial(attention_backward, team, block_len, q_width),
        out_shape=jax.ShapeDtypeStruct((token_count, qkv_width), BF16),
        in_specs=[smem(), vmem(), vmem(), vmem(), vmem()],
        out_specs=vmem(),
        scratch_shapes=[
            pltpu.VMEM((token_count, q_width), BF16),
            pltpu.VMEM((token_count, q_width), F32),
            pltpu.VMEM((token_count, 2 * HEAD_DIM), F32),
        ],
        compiler_params=pltpu.CompilerParams(vmem_limit_bytes=VMEM_BYTES),
        name="attention_backward",
    )(t.astype(jnp.int32).reshape(1), rot, mix_grad, cos_table, sin_table)

    attn_in_grad = team_reduce(lambda odd: contract_cols(half_of(proj_grad, odd), qkv_team).astype(BF16))
    attn_gain_grad = scatter_small(restore(jnp.sum(attn_in_grad * normed_one, axis=0)))
    scaled_one = attn_in_grad * gain_one
    input_grad = resid_grad + inv_one * (
        scaled_one - normed_one * jnp.mean(scaled_one * normed_one, axis=-1, keepdims=True)
    )
    input_grad = give_rows(restore(input_grad.astype(BF16)))

    qkv_grad = collect(contract_rows(attn_in, proj_grad).astype(BF16))
    q_weight_grad = join(qkv_grad[:, :, :q_width])
    k_weight_grad = sum_heads(qkv_grad[:, :, q_width : q_width + HEAD_DIM])
    v_weight_grad = sum_heads(qkv_grad[:, :, q_width + HEAD_DIM :])

    o_grad = restore(contract_rows(mix, branch_grad)).astype(BF16)
    o_grad = to_team(o_grad.reshape(q_width, team, -1).transpose(1, 0, 2)).reshape(width, -1)
    o_weight_grad = join(collect(reorder_rows(o_grad)))

    return (
        block_out,
        input_grad,
        attn_gain_grad,
        q_weight_grad,
        k_weight_grad,
        v_weight_grad,
        o_weight_grad,
        ffn_gain_grad,
        gate_weight_grad,
        up_weight_grad,
        down_weight_grad,
    )


def solution(mesh):
    rows = P(BOTH, None)
    placed = P("fsdp", "cp", None)
    gain = P(BOTH)
    return jax.shard_map(
        body,
        mesh=mesh,
        in_specs=(placed, placed, gain, rows, rows, rows, rows, gain, rows, rows, rows),
        out_specs=(placed, placed, gain, rows, rows, rows, rows, gain, rows, rows, rows),
        check_vma=False,
    )
```

```python
import functools

import jax
import jax.numpy as jnp
import numpy as np
from jax import lax
from jax.experimental import pallas as pl
from jax.experimental.pallas import tpu as pltpu
from jax.sharding import PartitionSpec as P

HEADS = 32
KV_HEADS = 8
HEAD_DIM = 64
HALF = HEAD_DIM // 2
NORM_EPS = 1e-05
ROPE_BASE = 500000.0
BOTH = ("fsdp", "cp")
F32 = jnp.float32
BF16 = jnp.bfloat16
MESH = pl.DeviceIdType.MESH
VMEM_BYTES = 60 << 20


def dot(left, right):
    return jnp.dot(left, right, preferred_element_type=F32)


def contract_rows(left, right):
    return lax.dot_general(left, right, (((0,), (0,)), ((), ())), preferred_element_type=F32)


def contract_cols(left, right):
    return lax.dot_general(left, right, (((1,), (1,)), ((), ())), preferred_element_type=F32)


def flip(index, mask):
    bit = 1
    out = index
    while bit <= mask:
        if mask & bit:
            out = out + bit - 2 * bit * ((index // bit) % 2)
        bit *= 2
    return out


def spot_of(diff, team):
    return diff // 2 + (diff % 2) * (team // 2)


def chunk_blocks(member, team):
    second = team + flip(member, team // 2)
    last = 4 * team - 1
    return member, last - member, second, last - second


def natural_unit(mine, index):
    block = flip(mine, index // 2)
    turned = block % 2
    return block * 2 + (index % 2) + turned * (1 - 2 * (index % 2))


def swap_halves(wide):
    pieces = []
    for start in range(0, wide.shape[-1], HEAD_DIM):
        pieces.append(wide[:, start + HALF : start + HEAD_DIM])
        pieces.append(wide[:, start : start + HALF])
    return jnp.concatenate(pieces, axis=-1)


def over_row_blocks(token_count, most, step):
    quarter = token_count // 4
    rows = min(most, (1 << 18) // token_count)
    for first in range(0, token_count, quarter):
        if rows == quarter:
            step(first, first + quarter, first, rows)
        else:

            def block(index, carry, first=first):
                step(first, first + quarter, pl.multiple_of(first + index * rows, rows), rows)
                return carry

            lax.fori_loop(0, quarter // rows, block, 0)


def turn_by(wide, cosine, sine):
    swapped = swap_halves(wide)
    pieces = []
    for start in range(0, wide.shape[-1], 2 * HEAD_DIM):
        piece = slice(start, start + 2 * HEAD_DIM)
        span = wide[:, piece].shape[-1]
        pieces.append(wide[:, piece] * cosine[:, :span] + swapped[:, piece] * sine[:, :span])
    return jnp.concatenate(pieces, axis=-1)


def masked_scores(query, keys, first, start):
    rows, span = query.shape[0], keys.shape[0] - first
    scores = contract_cols(query, keys)
    row = lax.broadcasted_iota(jnp.int32, (rows, span), 0) + (start - first)
    col = lax.broadcasted_iota(jnp.int32, (rows, span), 1)
    last = jnp.where(row >= col, scores[:, first:], -1e30)
    return jnp.concatenate([scores[:, :first], last], axis=-1) if first else last


def differ(left, right, size):
    out = 0
    bit = 1
    while bit < size:
        out = out + ((left // bit + right // bit) % 2) * bit
        bit *= 2
    return out


class Links:
    def __init__(self, cp_size, send, recv, local):
        self.f, self.c = lax.axis_index("fsdp"), lax.axis_index("cp")
        self.cp_size, self.send, self.recv, self.local = cp_size, send, recv, local
        self.used = self.used_local = 0

    def device(self, mask):
        return (flip(self.f, mask // self.cp_size), flip(self.c, mask % self.cp_size))

    def barrier(self, masks):
        sem = pltpu.get_barrier_semaphore()
        for mask in masks:
            pl.semaphore_signal(sem, inc=1, device_id=self.device(mask), device_id_type=MESH)
        pl.semaphore_wait(sem, len(masks))

    def copy(self, src, dst, mask):
        index = self.used
        self.used += 1
        return pltpu.make_async_remote_copy(
            src_ref=src,
            dst_ref=dst,
            send_sem=self.send.at[index],
            recv_sem=self.recv.at[index],
            device_id=self.device(mask),
            device_id_type=MESH,
        )

    def inside(self, src, dst):
        index = self.used_local
        self.used_local += 1
        return pltpu.make_async_copy(src, dst, self.local.at[index])


class TeamGather:
    def __init__(self, links, team, src, dst):
        near = team // 2
        row = range(2, near, 2)

        def place(mask):
            return dst.at[spot_of(mask, team)]

        self.to_near = links.copy(src, place(near), near)
        self.to_row = [links.copy(src, place(m), m) for m in row]
        self.on = [links.copy(place(near), place(near + m), m) for m in row]
        self.to_core = links.copy(src, place(1), 1)
        self.near_core = links.copy(place(near), place(near + 1), 1)
        self.row_core = [links.copy(place(m), place(m + 1), 1) for m in row]
        self.on_core = [links.copy(place(near + m), place(near + m + 1), 1) for m in row]
        self.own = links.inside(src, dst.at[0])

    def start(self):
        self.to_near.start()
        for copy in self.to_row:
            copy.start()
        self.to_core.start()
        self.own.start()

    def pass_near(self):
        self.to_near.wait_recv()
        for copy in self.on:
            copy.start()
        self.near_core.start()

    def pass_row(self):
        for copy, core in zip(self.to_row, self.row_core):
            copy.wait_recv()
            core.start()

    def pass_on(self):
        for copy, core in zip(self.on, self.on_core):
            copy.wait_recv()
            core.start()

    def finish(self):
        core = [self.to_core, self.near_core] + self.row_core + self.on_core
        for copy in core:
            copy.wait_recv()
        for copy in [self.to_near] + self.to_row + self.on + core:
            copy.wait_send()
        self.own.wait()


class TeamSum:
    def __init__(self, links, team, parts, taken, row_in, near_in):
        self.team, self.parts, self.taken, self.row_in, self.near_in = team, parts, taken, row_in, near_in
        near = team // 2
        self.row = list(range(2, near, 2))
        half = team // 2
        self.cross = [links.copy(parts.at[half + e], taken.at[e], 1) for e in range(half)]
        self.far = [links.copy(parts.at[(near + m) // 2], row_in.at[0, i], m) for i, m in enumerate(self.row)]
        self.here = [links.copy(parts.at[m // 2], row_in.at[1, i], m) for i, m in enumerate(self.row)]
        self.last = links.copy(parts.at[near // 2], near_in, near)

    def start(self, make, near_sum, own_sum):
        half, rows, width = self.taken.shape
        pieces = [slice(start, start + 512) for start in range(0, width, 512)]
        for low in range(half - 2, -1, -2):
            for cols in pieces:
                value = make(pl.ds((half + low) * rows, 2 * rows), cols).astype(BF16)
                for k in range(2):
                    self.parts[half + low + k, :, cols] = value[k * rows : (k + 1) * rows]
            self.cross[low + 1].start()
            self.cross[low].start()
        for low in range(half - 2, -1, -2):
            self.cross[low + 1].wait_recv()
            self.cross[low].wait_recv()
            for cols in pieces:
                value = make(pl.ds(low * rows, 2 * rows), cols)
                for k in range(2):
                    spot = low + k
                    part = value[k * rows : (k + 1) * rows] + self.taken[spot, :, cols].astype(F32)
                    if spot == half // 2:
                        near_sum[:, cols] = part
                    elif spot == 0:
                        own_sum[:, cols] = part
                    else:
                        self.parts[spot, :, cols] = part.astype(BF16)
            for spot in (low + 1, low):
                if spot > half // 2:
                    self.far[spot - half // 2 - 1].start()
                elif 0 < spot < half // 2:
                    self.here[spot - 1].start()

    def pass_near(self, value):
        for index, copy in enumerate(self.far):
            copy.wait_recv()
            value = value + self.row_in[0, index].astype(F32)
        self.parts[self.team // 4] = value.astype(BF16)
        self.last.start()

    def total(self, value):
        for index, copy in enumerate(self.here):
            copy.wait_recv()
            value = value + self.row_in[1, index].astype(F32)
        self.last.wait_recv()
        return value + self.near_in[...].astype(F32)

    def finish(self):
        for copy in self.cross + self.far + self.here + [self.last]:
            copy.wait_send()


class Spread:
    def __init__(self, links, team, t, pieces, full):
        self.own = links.inside(pieces(0), full.at[0, t])
        self.cuts = [links.copy(pieces(m), full.at[0, t], m) for m in range(1, team)]
        self.far = [links.copy(full.at[b], full.at[b + 2], links.cp_size) for b in range(2)]
        self.side = links.copy(full.at[0], full.at[1], team + team // 2)
        self.outer = t // (team // 2) == 0

    def cut(self):
        self.own.start()
        for piece in self.cuts:
            piece.start()

    def leave(self):
        self.own.wait()
        for piece in self.cuts:
            piece.wait_recv()
        self.far[0].start()
        self.cross(False)

    def cross(self, outer):
        @pl.when(self.outer == outer)
        def _():
            self.side.start()

    def arrive(self):
        self.side.wait_recv()
        self.far[1].start()

    def finish(self):
        for copy in self.far:
            copy.wait_recv()
        for copy in self.cuts + self.far + [self.side]:
            copy.wait_send()


class Collect:
    def __init__(self, links, team, t, grad, far_in, side_in, final, out):
        self.grad, self.far_in, self.side_in, self.final = grad, far_in, side_in, final
        self.outer = t // (team // 2) == 0
        self.far = [links.copy(grad.at[b + 2], far_in.at[b], links.cp_size) for b in range(2)]
        self.side = links.copy(grad.at[1], side_in, team + team // 2)
        self.own = links.inside(final.at[t], out.at[t])
        self.cuts = [links.copy(final.at[flip(t, m)], out.at[t], m) for m in range(1, team)]

    def cut(self):
        self.own.start()
        for piece in self.cuts:
            piece.start()

    def cross(self, outer):
        @pl.when(self.outer == outer)
        def _():
            self.side.start()

    def finish(self):
        self.own.wait()
        for copy in self.far:
            copy.wait_send()
        self.side.wait_send()
        for piece in self.cuts:
            piece.wait()


def entry_kernel(
    fsdp_size,
    cp_size,
    tokens,
    cotangent,
    gains_in,
    q_cut,
    kv_cut,
    o_cut,
    gate_in,
    up_in,
    down_in,
    cos_ref,
    sin_ref,
    x_ref,
    gains_ref,
    attn_in_ref,
    q_full,
    kv_full,
    o_wide,
    rot_ref,
    mix_ref,
    resid_ref,
    ffn_in_ref,
    dy_ref,
    gate_full,
    up_full,
    down_full,
    o_full,
    send,
    recv,
    local,
    swapped,
    dy_swapped,
    slots,
    chunk_ref,
    dy_chunk,
    acts,
    q_w,
    kv_w,
    mixed,
    o_pieces,
    taken,
    row_in,
    near_in,
    near_sum,
):
    links = Links(cp_size, send, recv, local)
    f, c = links.f, links.c
    team = cp_size // 2
    near, mirror = team // 2, team + team // 2
    side = c // team
    t = c % team + side * (flip(c, near) - c)
    row_count, width = tokens.shape[1], tokens.shape[2]
    block_len = row_count // 2
    unit = width // 8
    token_count, q_width = mixed.shape
    heads = q_width // HEAD_DIM
    cols = gate_full.shape[-1]
    mine = f * 2 + side

    links.barrier(list(range(1, team)) + [mirror, cp_size])
    swap = links.copy(tokens.at[1 - side], swapped, mirror)
    swap.start()
    slots[0] = gains_in[...]
    stages = []
    size = 1
    for mask in [1 << k for k in range(team.bit_length() - 1)] + [mirror, cp_size]:
        stages.append(links.copy(slots.at[pl.ds(0, size)], slots.at[pl.ds(size, size)], mask))
        size *= 2

    def columns_of(weight):
        if len(weight.shape) == 3:
            return lambda m: weight.at[flip(t, m)]
        count = weight.shape[1] // team
        return lambda m: weight.at[:, pl.ds(pl.multiple_of(flip(t, m) * count, count), count)]

    def spread(pieces, full):
        return Spread(links, team, t, pieces, full)

    q_spread = spread(columns_of(q_cut), q_full)
    kv_spread = spread(columns_of(kv_cut), kv_full)
    o_spread = spread(columns_of(o_cut), o_full)
    gate_spread = spread(columns_of(gate_in), gate_full)
    up_spread = spread(columns_of(up_in), up_full)
    down_spread = spread(columns_of(down_in), down_full)

    stages[0].start()
    q_spread.cut()
    kv_spread.cut()
    o_spread.cut()
    for step in range(1, len(stages)):
        stages[step - 1].wait_recv()
        stages[step].start()
    gate_spread.cut()

    def fill(dst, source, theirs):
        here = pl.ds(pl.multiple_of(side * row_count, row_count), row_count)
        there = pl.ds(pl.multiple_of((1 - side) * row_count, row_count), row_count)
        for index in range(8):
            cols = slice(index * unit, (index + 1) * unit)
            natural = pl.ds(pl.multiple_of(natural_unit(mine, index) * unit, unit), unit)
            dst[here, cols] = source[side, :, natural].astype(dst.dtype)
            dst[there, cols] = theirs[:, natural].astype(dst.dtype)

    stages[-1].wait_recv()
    pieces = []
    for b in range(4):
        for member in range(team):
            pieces.append(slots[b * team + flip(t, member)][:8, : width // (4 * team)])
    gains = jnp.concatenate(pieces, axis=-1).astype(F32)
    gains_ref[...] = gains
    swap.wait_recv()
    fill(x_ref, tokens, swapped)
    x = x_ref[...]
    inv_one = lax.rsqrt(jnp.mean(x * x, axis=-1, keepdims=True) + NORM_EPS)
    chunk_ref[...] = (x * inv_one * gains[0:1]).astype(BF16)
    gather_one = TeamGather(links, team, chunk_ref, acts)
    gather_one.start()
    dy_swap = links.copy(cotangent.at[1 - side], dy_swapped, mirror)
    dy_swap.start()
    q_spread.leave()
    kv_spread.leave()
    q_spread.cross(True)
    kv_spread.cross(True)
    o_spread.leave()
    o_spread.cross(True)
    gather_one.pass_near()
    gather_one.pass_row()
    gate_spread.leave()
    gate_spread.cross(True)
    gather_one.pass_on()
    up_spread.cut()
    down_spread.cut()
    q_spread.arrive()
    kv_spread.arrive()
    o_spread.arrive()
    up_spread.leave()
    q_spread.finish()
    kv_spread.finish()
    weight_loads = [links.inside(q_full, q_w), links.inside(kv_full, kv_w)]
    for load in weight_loads:
        load.start()
    gather_one.finish()
    attn_out = links.inside(acts, attn_in_ref)
    attn_out.start()
    o_spread.finish()

    o_rows = o_full.shape[2]

    def o_source(m):
        count = q_width // o_rows
        first = flip(t, m) * count
        owners, start = first // team, first % team
        block = ((owners // 2 + mine // 2) % 2) * 2 + (owners + mine) % 2
        return o_full.at[block, pl.ds(start + (owners % 2) * (flip(start, near) - start), count)]

    o_own = links.inside(o_source(0), o_pieces.at[t])
    o_sends = [links.copy(o_source(m), o_pieces.at[t], m) for m in range(1, team)]
    o_own.start()
    for copy in o_sends:
        copy.start()

    for load in weight_loads:
        load.wait()
    q_weights = q_w[...].reshape(width, q_width)
    kv_weights = kv_w[...].reshape(width, 2 * HEAD_DIM)

    def project(m, carry):
        rows_in = acts[spot_of(m, team)]
        key_value = dot(rows_in, kv_weights)
        qk = jnp.concatenate([dot(rows_in, q_weights) * HEAD_DIM ** (-0.5), key_value[:, :HEAD_DIM]], axis=-1)
        blocks = chunk_blocks(differ(t, m, team), team)
        for slot in range(4):
            piece = slice(slot * block_len, (slot + 1) * block_len)
            rows = pl.ds(pl.multiple_of(blocks[slot] * block_len, block_len), block_len)
            turned = turn_by(qk[piece], cos_ref[rows, :], sin_ref[rows, :])
            rot_ref[rows, :] = jnp.concatenate([turned, key_value[piece, HEAD_DIM:]], axis=-1).astype(BF16)
        return carry

    lax.fori_loop(0, team, project, 0)

    dy_swap.wait_recv()
    fill(dy_chunk, cotangent, dy_swapped)
    gather_dy = TeamGather(links, team, dy_chunk, dy_ref)
    gather_dy.start()
    down_spread.leave()

    def attend(first, span, start, rows):
        keys = rot_ref[:span, q_width : q_width + HEAD_DIM]
        values = rot_ref[:span, q_width + HEAD_DIM :]
        outs = []
        for head in range(heads):
            query = rot_ref[pl.ds(start, rows), head * HEAD_DIM : (head + 1) * HEAD_DIM]
            scores = masked_scores(query, keys, first, start)
            peak = jnp.max(scores, axis=-1, keepdims=True)
            expo = jnp.exp(scores - peak)
            total = jnp.sum(expo, axis=-1, keepdims=True)
            outs.append(dot(expo.astype(BF16), values) / total)
        mixed[pl.ds(start, rows), :] = jnp.concatenate(outs, axis=-1).astype(BF16)

    over_row_blocks(token_count, 256, attend)
    gather_dy.pass_near()

    def collect_mix(m, carry):
        blocks = chunk_blocks(differ(t, m, team), team)
        for slot in range(4):
            where = pl.ds(pl.multiple_of(blocks[slot] * block_len, block_len), block_len)
            mix_ref[spot_of(m, team), slot * block_len : (slot + 1) * block_len, :] = mixed[where, :]
        return carry

    lax.fori_loop(0, team, collect_mix, 0)
    for copy in o_sends:
        copy.wait_recv()
    o_own.wait()
    span = width // team
    for index in range(8):
        for piece in range(team // 8):
            start = index * unit + piece * span
            source = natural_unit(mine, index) * (team // 8) + piece
            o_wide[:, start : start + span] = o_pieces[source].reshape(q_width, span)

    attn_out.wait()
    summed = TeamSum(links, team, acts, taken, row_in, near_in)
    row_pair = 2 * row_count
    gather_dy.pass_row()

    def mix_out(place, cols):
        spots = pl.ds(place.start // row_pair, 2)
        return dot(mix_ref[spots].reshape(2 * row_pair, q_width), o_wide[:, cols])

    summed.start(mix_out, near_sum, resid_ref)
    summed.pass_near(near_sum[...])
    up_spread.cross(True)
    gather_dy.pass_on()
    resid_ref[...] = x_ref[...] + summed.total(resid_ref[...])
    resid = resid_ref[...]
    inv_two = lax.rsqrt(jnp.mean(resid * resid, axis=-1, keepdims=True) + NORM_EPS)
    chunk_ref[...] = (resid * inv_two * gains_ref[1:2]).astype(BF16)
    gather_two = TeamGather(links, team, chunk_ref, ffn_in_ref)
    gather_two.start()
    down_spread.cross(True)
    gather_dy.finish()
    gate_spread.arrive()
    gather_two.pass_near()
    gather_two.pass_row()
    gather_two.pass_on()
    up_spread.arrive()
    gate_spread.finish()
    down_spread.arrive()
    gather_two.finish()
    up_spread.finish()
    down_spread.finish()
    swap.wait_send()
    dy_swap.wait_send()
    summed.finish()
    for copy in stages + o_sends:
        copy.wait_send()


def backward_heads(token_count, q_width, rot_ref, wide_ref, cos_ref, sin_ref, dq_ref, dkv_ref):
    heads = q_width // HEAD_DIM
    dkv_ref[...] = jnp.zeros_like(dkv_ref)

    def attend(first, span, start, count):
        rows = pl.ds(start, count)
        keys = rot_ref[:span, q_width : q_width + HEAD_DIM]
        values = rot_ref[:span, q_width + HEAD_DIM :]
        for head in range(heads):
            cols = slice(head * HEAD_DIM, (head + 1) * HEAD_DIM)
            query = rot_ref[rows, cols]
            grad = wide_ref[rows, cols]
            scores = masked_scores(query, keys, first, start)
            peak = jnp.max(scores, axis=-1, keepdims=True)
            expo = jnp.exp(scores - peak)
            probs = expo / jnp.sum(expo, axis=-1, keepdims=True)
            dprob = contract_cols(grad, values)
            delta = jnp.sum(probs * dprob, axis=-1, keepdims=True)
            score_grad = (probs * (dprob - delta)).astype(BF16)
            dq_ref[rows, cols] = dot(score_grad, keys)
            dk = contract_rows(score_grad, query)
            dv = contract_rows(probs.astype(BF16), grad)
            dkv_ref[:span, :] += jnp.concatenate([dk, dv], axis=-1)

    over_row_blocks(token_count, 128, attend)

    for start in range(0, token_count, token_count // 4):
        rows = slice(start, start + token_count // 4)
        qk = jnp.concatenate([dq_ref[rows, :], dkv_ref[rows, :HEAD_DIM]], axis=-1)
        turned = turn_by(qk, cos_ref[rows, :], -sin_ref[rows, :])
        dq_ref[rows, :] = turned[:, :q_width] * HEAD_DIM ** (-0.5)
        dkv_ref[rows, :] = jnp.concatenate([turned[:, q_width:], dkv_ref[rows, HEAD_DIM:]], axis=-1)


def scatter_chunk(t, m, team, block_len, wide_ref, value):
    blocks = chunk_blocks(differ(t, m, team), team)
    for slot in range(4):
        where = pl.ds(pl.multiple_of(blocks[slot] * block_len, block_len), block_len)
        wide_ref[where, :] = value[slot * block_len : (slot + 1) * block_len, :]


def gather_chunk(t, m, team, block_len, out_ref, *sources):
    blocks = chunk_blocks(differ(t, m, team), team)
    for slot in range(4):
        rows = pl.ds(pl.multiple_of(blocks[slot] * block_len, block_len), block_len)
        place = pl.ds(pl.multiple_of((spot_of(m, team) * 4 + slot) * block_len, block_len), block_len)
        piece = jnp.concatenate([source[rows, :] for source in sources], axis=-1)
        out_ref[place, :] = piece.astype(BF16)


def attention_backward(
    team, block_len, q_width, where_ref, rot_ref, grad_ref, cos_ref, sin_ref, out_ref, wide_ref, dq_ref, dkv_ref
):
    t = where_ref[0]

    def place_grad(m, carry):
        scatter_chunk(t, m, team, block_len, wide_ref, grad_ref[spot_of(m, team)])
        return carry

    lax.fori_loop(0, team, place_grad, 0)
    backward_heads(wide_ref.shape[0], q_width, rot_ref, wide_ref, cos_ref, sin_ref, dq_ref, dkv_ref)

    def give_chunk(m, carry):
        gather_chunk(t, m, team, block_len, out_ref, dq_ref, dkv_ref)
        return carry

    lax.fori_loop(0, team, give_chunk, 0)


def exit_kernel(
    cp_size,
    x_ref,
    resid_ref,
    gains_ref,
    rot_ref,
    mix_ref,
    o_wide,
    cos_ref,
    sin_ref,
    attn_in,
    ffn_in,
    dy,
    gate_in,
    up_in,
    down_in,
    q_in,
    kv_in,
    block_out,
    input_grad,
    gain_grads,
    gate_out,
    up_out,
    down_out,
    qkv_out,
    o_out,
    branch,
    gate_grad,
    gate_far,
    gate_side,
    gate_final,
    up_grad,
    up_far,
    up_side,
    up_final,
    down_grad,
    down_far,
    down_side,
    down_final,
    qkv_grad,
    qkv_far,
    qkv_side,
    qkv_final,
    send,
    recv,
    local,
    store_sem,
    load_sem,
    first,
    second,
    gate_w,
    up_w,
    down_w,
    qkv_w,
    parts,
    hidden,
    both,
    stage_out,
    stage_in,
    taken_one,
    row_one,
    near_one,
    taken_two,
    row_two,
    near_two,
    resid_grad,
    near_sum,
    own_sum,
    chunk_ref,
    grad_rows,
    wide,
    dq_ref,
    dkv_ref,
    proj_grad,
    o_far,
    o_two,
    o_side,
    o_final,
    gain_slots,
    gain_in,
):
    links = Links(cp_size, send, recv, local)
    f, c = links.f, links.c
    team = cp_size // 2
    near, mirror = team // 2, team + team // 2
    side = c // team
    t = c % team + side * (flip(c, near) - c)
    mine = f * 2 + side
    half = team // 2
    token_count, width = first.shape
    rows = token_count // team
    row_count = rows // 2
    block_len = row_count // 2
    unit = width // 8
    cols = hidden.shape[1]
    q_width = wide.shape[1]
    weight_rows = gate_grad.shape[2]

    links.barrier(list(range(1, team)) + [mirror, cp_size])
    loads = [
        links.inside(source, target)
        for source, target in (
            (ffn_in, first),
            (gate_in, gate_w),
            (up_in, up_w),
            (dy, second),
            (down_in, down_w),
            (q_in, qkv_w.at[:, pl.ds(0, q_in.shape[1])]),
            (kv_in, qkv_w.at[:, pl.ds(q_in.shape[1], kv_in.shape[1])]),
        )
    ]
    for load in loads:
        load.start()
    for load in loads[:3]:
        load.wait()

    steps = token_count // 256

    def forward(index, carry):
        place = pl.ds(pl.multiple_of(index * 256, 256), 256)
        spots = pl.ds(index * (256 // rows), 256 // rows)
        block = first[place, :]
        for start in range(0, cols, 256):
            cut = slice(start, start + 256)
            later = slice(cols + start, cols + start + 256)
            gate = dot(block, gate_w[:, cut])
            up_val = dot(block, up_w[:, cut])
            sigma = jax.nn.sigmoid(gate)
            silu_val = gate * sigma
            hidden[place, cut] = (silu_val * up_val).astype(BF16)
            factor = up_val * (sigma + silu_val * (1.0 - sigma))
            parts[spots, :, cut] = silu_val.astype(BF16).reshape(256 // rows, rows, 256)
            parts[spots, :, later] = factor.astype(BF16).reshape(256 // rows, rows, 256)
        return carry

    lax.fori_loop(0, steps, forward, 0)

    def produce(left, right, offset, widths, start, count, targets, adds):
        def one(index, carry):
            place = start + index
            slot = index % 2
            block, part = place // 2, pl.ds((place % 2) * half, half)
            waits = []
            for a, sources in enumerate(adds):
                for k, source in enumerate(sources):
                    load = pltpu.make_async_copy(
                        source(block, part), stage_in.at[a, k, :, :, : widths[k]], load_sem.at[a, k]
                    )
                    load.start()
                    waits.append(load)
            stores = [
                pltpu.make_async_copy(
                    stage_out.at[slot, k, :, :, : widths[k]], target(block, part), store_sem.at[slot, k]
                )
                for k, target in enumerate(targets)
            ]

            @pl.when(index >= 2)
            def _():
                for store in stores:
                    store.wait()

            turned = left[:, pl.ds(pl.multiple_of(place * unit, unit), unit)].T
            first_col = offset
            for k, span in enumerate(widths):
                value = dot(turned, right[:, first_col : first_col + span]).reshape(half, weight_rows, span)
                for a in range(len(adds)):
                    waits[a * len(widths) + k].wait()
                    value = value + stage_in[a, k, :, :, :span].astype(F32)
                stage_out[slot, k, :, :, :span] = value.astype(BF16)
                stores[k].start()
                first_col += span
            return carry

        lax.fori_loop(0, count, one, 0)
        for index in range(max(0, count - 2), count):
            for k, target in enumerate(targets):
                pltpu.make_async_copy(
                    stage_out.at[index % 2, k, :, :, : widths[k]], target(0, pl.ds(0, half)), store_sem.at[index % 2, k]
                ).wait()

    def in_block(ref):
        return lambda block, part: ref.at[block, part]

    def in_side(ref):
        return lambda block, part: ref.at[part]

    def give_far(block, left, right, offset, widths, collects):
        produce(left, right, offset, widths, 4 + 2 * block, 2, [in_block(k.grad) for k in collects], [])
        for collect in collects:
            collect.far[block].start()

    def give_side(left, right, offset, widths, collects):
        for collect in collects:
            collect.far[1].wait_recv()
        sources = [in_block(k.far_in) for k in collects]
        produce(left, right, offset, widths, 2, 2, [in_block(k.grad) for k in collects], [sources])
        for collect in collects:
            collect.cross(False)

    def give_final(left, right, offset, widths, collects):
        for collect in collects:
            collect.far[0].wait_recv()
            collect.side.wait_recv()
        sources = [[in_block(k.far_in) for k in collects], [in_side(k.side_in) for k in collects]]
        produce(left, right, offset, widths, 0, 2, [in_side(k.final) for k in collects], sources)
        for collect in collects:
            collect.cut()

    gate_sum = Collect(links, team, t, gate_grad, gate_far, gate_side, gate_final, gate_out)
    up_sum = Collect(links, team, t, up_grad, up_far, up_side, up_final, up_out)
    down_sum = Collect(links, team, t, down_grad, down_far, down_side, down_final, down_out)
    qkv_sum = Collect(links, team, t, qkv_grad, qkv_far, qkv_side, qkv_final, qkv_out)

    loads[3].wait()
    give_far(1, second, hidden, 0, [cols], [down_sum])
    loads[4].wait()

    def backward(index, carry):
        place = pl.ds(pl.multiple_of(index * 256, 256), 256)
        spots = pl.ds(index * (256 // rows), 256 // rows)
        block = second[place, :]
        for start in range(0, cols, 256):
            cut = slice(start, start + 256)
            later = slice(cols + start, cols + start + 256)
            hidden_grad = dot(block, down_w[:, cut])
            silu_val = parts[spots, :, cut].reshape(256, 256).astype(F32)
            factor = parts[spots, :, later].reshape(256, 256).astype(F32)
            both[place, cut] = (hidden_grad * factor).astype(BF16)
            both[place, later] = (hidden_grad * silu_val).astype(BF16)
        return carry

    lax.fori_loop(0, steps, backward, 0)

    def team_sum(taken, row_in, near_in, make):
        summed = TeamSum(links, team, parts, taken, row_in, near_in)
        summed.start(make, near_sum, own_sum)
        return summed

    def finish_sum(summed):
        summed.pass_near(near_sum[...])
        value = summed.total(own_sum[...])
        summed.finish()
        return value

    ffn_sum = team_sum(
        taken_one,
        row_one,
        near_one,
        lambda place, cut: contract_cols(both[place, :cols], gate_w[cut, :]) + contract_cols(both[place, cols:], up_w[cut, :]),
    )
    ffn_sum.pass_near(near_sum[...])
    give_far(1, first, both, 0, [cols, cols], [gate_sum, up_sum])
    give_far(0, second, hidden, 0, [cols], [down_sum])
    give_side(second, hidden, 0, [cols], [down_sum])
    give_far(0, first, both, 0, [cols, cols], [gate_sum, up_sum])
    ffn_in_grad = ffn_sum.total(own_sum[...])
    ffn_sum.finish()

    def place_gain(row, value):
        share = width // (4 * team)
        for b in range(4):
            for member in range(team):
                start = (b * team + member) * share
                gain_slots[b * team + flip(t, member), row : row + 1, :share] = value[:, start : start + share]

    gain_slots[...] = jnp.zeros_like(gain_slots)
    resid = resid_ref[...]
    inv_two = lax.rsqrt(jnp.mean(resid * resid, axis=-1, keepdims=True) + NORM_EPS)
    normed = resid * inv_two
    place_gain(1, jnp.sum(ffn_in_grad * normed, axis=0, keepdims=True))
    scaled = ffn_in_grad * gains_ref[1:2]
    value = second[:rows, :].astype(F32) + inv_two * (
        scaled - normed * jnp.mean(scaled * normed, axis=-1, keepdims=True)
    )
    resid_grad[...] = value
    chunk_ref[...] = value.astype(BF16)
    gather = TeamGather(links, team, chunk_ref, branch)
    gather.start()
    down_sum.cross(True)
    give_side(first, both, 0, [cols], [gate_sum])
    gather.pass_near()
    gather.pass_row()
    gather.pass_on()
    give_side(first, both, cols, [cols], [up_sum])
    gather.finish()
    load = links.inside(branch, parts)
    load.start()
    load.wait()

    for low in range(0, team, 2):
        value = contract_cols(parts[low : low + 2].reshape(2 * rows, width), o_wide[...]).astype(BF16)
        for spot in range(2):
            m = 2 * (low + spot) if low + spot < half else 2 * (low + spot - half) + 1
            scatter_chunk(t, m, team, block_len, wide, value[spot * rows : (spot + 1) * rows])

    def head_rows(member):
        return pl.ds(pl.multiple_of(member * q_width, q_width), q_width)

    span = width // team
    turned = mix_ref[...].reshape(token_count, q_width).T
    for index in range(8):
        value = dot(turned, parts[:, :, index * unit : (index + 1) * unit].reshape(token_count, unit)).astype(BF16)
        for piece in range(team // 8):
            target = natural_unit(mine, index) * (team // 8) + piece
            gate_w[head_rows(target), span : 2 * span] = value[:, piece * span : (piece + 1) * span]
    quarter = width // 4
    o_place = gate_w.at[head_rows(t), pl.ds(0, span)]

    def o_part(member):
        return gate_w.at[head_rows(member), pl.ds(span, span)]

    def o_land(block):
        return gate_w[pl.ds(pl.multiple_of(block * quarter, quarter), quarter), :span].astype(F32)

    o_own = links.inside(o_part(t), o_place)
    o_sends = [links.copy(o_part(flip(t, m)), o_place, m) for m in range(1, team)]
    o_own.start()
    for copy in o_sends:
        copy.start()

    out_sum = team_sum(taken_two, row_two, near_two, lambda place, cut: contract_cols(hidden[place, :], down_w[cut, :]))
    gate_sum.cross(True)
    up_sum.cross(True)
    backward_heads(token_count, q_width, rot_ref, wide, cos_ref, sin_ref, dq_ref, dkv_ref)

    def give_chunk(m, carry):
        gather_chunk(t, m, team, block_len, proj_grad, dq_ref, dkv_ref)
        return carry

    lax.fori_loop(0, team, give_chunk, 0)

    def give_rows(value, target, out):
        for index in range(8):
            natural = pl.ds(pl.multiple_of(natural_unit(mine, index) * unit, unit), unit)
            target[:, natural] = value[:, index * unit : (index + 1) * unit].astype(BF16)
        here = pl.ds(pl.multiple_of(side * row_count, row_count), row_count)
        there = pl.ds(pl.multiple_of((1 - side) * row_count, row_count), row_count)
        own = links.inside(target.at[here], out.at[side])
        other = links.copy(target.at[there], out.at[side], mirror)
        own.start()
        other.start()
        return own, other

    out_copies = give_rows(resid_ref[...] + finish_sum(out_sum), chunk_ref, block_out)
    qkv_width = q_width + 2 * HEAD_DIM
    loads[5].wait()
    loads[6].wait()
    attn_sum = team_sum(
        taken_one,
        row_one,
        near_one,
        lambda place, cut: contract_cols(proj_grad[place, :], qkv_w[cut, :]),
    )
    attn_load = links.inside(attn_in, second)
    give_final(second, hidden, 0, [cols], [down_sum])
    attn_load.start()
    for copy in o_sends:
        copy.wait_recv()
    o_own.wait()
    other_half = pl.ds(pl.multiple_of((1 - f) * 2 * quarter, 2 * quarter), 2 * quarter)
    o_across = links.copy(gate_w.at[other_half, pl.ds(0, span)], o_far, cp_size)
    o_across.start()
    attn_load.wait()
    attn_in_grad = finish_sum(attn_sum)

    x = x_ref[...]
    inv_one = lax.rsqrt(jnp.mean(x * x, axis=-1, keepdims=True) + NORM_EPS)
    normed = x * inv_one
    place_gain(0, jnp.sum(attn_in_grad * normed, axis=0, keepdims=True))
    size = 2 * team
    gain_steps = []
    for mask in [cp_size, mirror] + [1 << k for k in reversed(range(team.bit_length() - 1))]:
        gain_steps.append(links.copy(gain_slots.at[pl.ds(size, size)], gain_in.at[pl.ds(size, size)], mask))
        size //= 2
    gain_steps[0].start()
    scaled = attn_in_grad * gains_ref[0:1]
    value = resid_grad[...] + inv_one * (scaled - normed * jnp.mean(scaled * normed, axis=-1, keepdims=True))
    grad_copies = give_rows(value, grad_rows, input_grad)

    give_far(1, second, proj_grad, 0, [qkv_width], [qkv_sum])
    give_far(0, second, proj_grad, 0, [qkv_width], [qkv_sum])
    give_final(first, both, 0, [cols], [gate_sum])
    o_across.wait_recv()

    def o_came(block):
        return o_far[pl.ds(pl.multiple_of(block * quarter, quarter), quarter), :].astype(F32)

    o_two[...] = (o_land(f * 2 + 1 - side) + o_came(1 - side)).astype(BF16)
    o_cross = links.copy(o_two, o_side, mirror)
    o_cross.start()
    size = 2 * team
    for index, step in enumerate(gain_steps):
        step.wait_recv()
        gain_slots[:size] += gain_in[size : 2 * size]
        size //= 2
        if index + 1 < len(gain_steps):
            gain_steps[index + 1].start()
    gain_grads[...] = gain_slots[0]
    give_side(second, proj_grad, 0, [qkv_width], [qkv_sum])
    qkv_sum.cross(True)
    o_cross.wait_recv()
    o_final[...] = (o_land(f * 2 + side) + o_came(side) + o_side[...].astype(F32)).astype(BF16)

    def o_rows(member):
        place = member + side * (flip(member, near) - member)
        return o_final.at[pl.ds(pl.multiple_of(place * weight_rows, weight_rows), weight_rows)]

    o_last = links.inside(o_rows(t), o_out.at[t])
    o_gives = [links.copy(o_rows(flip(t, m)), o_out.at[t], m) for m in range(1, team)]
    o_last.start()
    for copy in o_gives:
        copy.start()
    give_final(first, both, cols, [cols], [up_sum])
    give_final(second, proj_grad, 0, [qkv_width], [qkv_sum])
    for own, other in (out_copies, grad_copies):
        own.wait()
        other.wait()
    for copy in o_sends + [o_across, o_cross] + gain_steps:
        copy.wait_send()
    for copy in o_gives:
        copy.wait()
    o_last.wait()
    for collect in (down_sum, gate_sum, up_sum, qkv_sum):
        collect.finish()


def join_kernel(team, q_width, qkv, o_part, gate_part, up_part, down_part, q_out, o_out, gate_out, up_out, down_out, k_out, v_out):
    member = pl.program_id(0)
    q_out[...] = qkv[member, :, :q_width].astype(F32)
    for part, out in ((o_part, o_out), (gate_part, gate_out), (up_part, up_out), (down_part, down_out)):
        out[...] = part[0].astype(F32)

    @pl.when(member == 0)
    def _():
        keys, values = slice(q_width, q_width + HEAD_DIM), slice(q_width + HEAD_DIM, q_width + 2 * HEAD_DIM)
        k_out[...] = jnp.concatenate([qkv[k, :, keys] for k in range(team)], axis=-1).astype(F32)
        v_out[...] = jnp.concatenate([qkv[k, :, values] for k in range(team)], axis=-1).astype(F32)


def vmem():
    return pl.BlockSpec(memory_space=pltpu.VMEM)


def smem():
    return pl.BlockSpec(memory_space=pltpu.SMEM)


def anywhere():
    return pl.BlockSpec(memory_space=pl.ANY)


def body(
    tokens,
    cotangent,
    attn_gain,
    q_weight,
    k_weight,
    v_weight,
    o_weight,
    ffn_gain,
    gate_weight,
    up_weight,
    down_weight,
):
    fsdp_size, cp_size = lax.axis_size("fsdp"), lax.axis_size("cp")
    devices = fsdp_size * cp_size
    teams, row_count, width = tokens.shape
    team = cp_size // teams
    mirror = team + team // 2
    block_len = row_count // 2
    chunk = teams * row_count
    token_count = team * chunk
    f = lax.axis_index("fsdp")
    c = lax.axis_index("cp")
    side = c // team
    t = c % team ^ (team // 2 * side)
    q_width = HEADS // team * HEAD_DIM
    copies = team // KV_HEADS
    qkv_width = q_width + 2 * HEAD_DIM
    weight_rows = q_weight.shape[0]
    hidden_cols = gate_weight.shape[1] // team
    team_groups = [[k * team + i for i in range(team)] for k in range(teams)]

    def swap(value, mask):
        return lax.ppermute(value, BOTH, [(i, i ^ mask) for i in range(devices)])

    def turn(value):
        half = team // 2
        return jnp.where(side == 1, jnp.concatenate([value[half:], value[:half]], axis=0), value)

    def to_team(value):
        return turn(lax.all_to_all(turn(value), "cp", 0, 0, axis_index_groups=team_groups, tiled=True))

    def swap_blocks(blocks):
        blocks = jnp.where(f == 1, blocks[:, ::-1], blocks)
        return jnp.where(side == 1, blocks[:, :, ::-1], blocks)

    def turn_second(blocks):
        return jnp.concatenate([blocks[:, :, :1], blocks[:, :, 1:, ::-1]], axis=2)

    def reorder_rows(value):
        blocks = value.reshape(1, 2, 2, 2, width // 8, -1)
        return swap_blocks(turn_second(blocks)).reshape(value.shape)

    def restore(value):
        blocks = value.reshape(-1, 2, 2, 2, width // 8)
        return turn_second(swap_blocks(blocks)).reshape(value.shape)

    def give_rows(value):
        first, second = value[:row_count], value[row_count:]
        mine = jnp.where(side == 0, first, second)
        theirs = swap(jnp.where(side == 0, second, first), mirror)
        return jnp.stack([jnp.where(side == 0, mine, theirs), jnp.where(side == 0, theirs, mine)], axis=0)

    def team_gather(value):
        evens = jnp.concatenate([value] + [swap(value, m) for m in range(2, team, 2)], axis=0)
        return jnp.concatenate([evens, swap(evens, 1)], axis=0)

    def team_reduce(make):
        theirs = swap(make(1), 1)
        evens = (make(0).astype(F32) + theirs.astype(F32)).astype(BF16).reshape(team // 2, chunk, width)
        total = evens[0].astype(F32)
        for m in range(2, team, 2):
            total = total + swap(evens[m // 2], m).astype(F32)
        return total

    def scatter_small(value):
        for bit in reversed(range(devices.bit_length() - 1)):
            mask = 1 << bit
            index = (f * cp_size + c) & mask
            half = value.shape[-1] // 2
            low, high = value[..., :half], value[..., half:]
            theirs = swap(jnp.where(index == 0, high, low), mask)
            value = jnp.where(index == 0, low, high) + theirs
        return value

    def collect(value):
        cols = value.shape[-1]
        blocks = value.reshape(fsdp_size, teams, -1, cols)
        theirs = swap(blocks[1], cp_size)
        blocks = (blocks[0].astype(F32) + theirs.astype(F32)).astype(BF16)
        theirs = swap(blocks[1], mirror)
        own = (blocks[0].astype(F32) + theirs.astype(F32)).astype(BF16)
        return to_team(own.reshape(team, -1, cols))

    def cut(weight):
        return weight.reshape(weight_rows, team, -1).transpose(1, 0, 2)

    def join(pieces):
        return pieces.transpose(1, 0, 2).reshape(pieces.shape[1], -1).astype(F32)

    def sum_heads(pieces):
        grouped = pieces.astype(F32).reshape(KV_HEADS, copies, -1, HEAD_DIM).sum(axis=1)
        return grouped.transpose(1, 0, 2).reshape(grouped.shape[1], -1)

    inverse = np.float32(ROPE_BASE) ** (-(2.0 * np.arange(HALF, dtype=np.float32)) / HEAD_DIM)
    angle = np.arange(token_count).astype(np.float32)[:, None] * inverse.astype(np.float32)[None, :]
    cosine, sine = np.cos(angle), np.sin(angle)
    cos_table = jnp.asarray(np.concatenate([cosine] * 4, axis=-1), F32)
    sin_table = jnp.asarray(np.concatenate([-sine, sine] * 2, axis=-1), F32)

    q_cut, o_cut = (
        weight if weight.shape[1] // team % 128 == 0 else cut(weight) for weight in (q_weight, o_weight)
    )
    heads_of = [weight.reshape(weight_rows, KV_HEADS, HEAD_DIM) for weight in (k_weight, v_weight)]
    kv_cut = jnp.repeat(jnp.concatenate(heads_of, axis=-1).transpose(1, 0, 2), copies, axis=0)
    gains_in = jnp.pad(jnp.stack([attn_gain, ffn_gain]), ((0, 14), (0, 128 - weight_rows)))

    def hbm(*shape):
        return jax.ShapeDtypeStruct(shape, BF16)

    out_shape = (
        jax.ShapeDtypeStruct((chunk, width), F32),
        jax.ShapeDtypeStruct((8, width), F32),
        hbm(team, chunk, width),
        hbm(4, team, weight_rows, q_width),
        hbm(4, team, weight_rows, 2 * HEAD_DIM),
        hbm(q_width, width),
        hbm(token_count, qkv_width),
        hbm(team, chunk, q_width),
        jax.ShapeDtypeStruct((chunk, width), F32),
        hbm(team, chunk, width),
        hbm(team, chunk, width),
        hbm(4, team, weight_rows, hidden_cols),
        hbm(4, team, weight_rows, hidden_cols),
        hbm(4, team, weight_rows, hidden_cols),
        hbm(4, team, weight_rows, width // team),
    )
    spaces = [vmem(), vmem()] + [anywhere()] * 3 + [vmem()] * 4 + [anywhere()] * 6
    outs = pl.pallas_call(
        functools.partial(entry_kernel, fsdp_size, cp_size),
        out_shape=out_shape,
        in_specs=[vmem(), vmem(), vmem()] + [anywhere()] * 6 + [vmem()] * 2,
        out_specs=tuple(spaces),
        scratch_shapes=[
            pltpu.SemaphoreType.DMA((11 * team + 48,)),
            pltpu.SemaphoreType.DMA((11 * team + 48,)),
            pltpu.SemaphoreType.DMA((24,)),
            pltpu.VMEM((row_count, width), BF16),
            pltpu.VMEM((row_count, width), BF16),
            pltpu.VMEM((devices, 16, 128), BF16),
            pltpu.VMEM((chunk, width), BF16),
            pltpu.VMEM((chunk, width), BF16),
            pltpu.VMEM((team, chunk, width), BF16),
            pltpu.VMEM((4, team, weight_rows, q_width), BF16),
            pltpu.VMEM((4, team, weight_rows, 2 * HEAD_DIM), BF16),
            pltpu.VMEM((token_count, q_width), BF16),
            pltpu.VMEM((team, q_width // weight_rows, weight_rows, width // team), BF16),
            pltpu.VMEM((team // 2, chunk, width), BF16),
            pltpu.VMEM((2, team // 4 - 1, chunk, width), BF16),
            pltpu.VMEM((chunk, width), BF16),
            pltpu.VMEM((chunk, width), F32),
        ],
        compiler_params=pltpu.CompilerParams(
            collective_id=0, has_side_effects=True, vmem_limit_bytes=VMEM_BYTES
        ),
        name="entry",
    )(tokens, cotangent, gains_in, q_cut, kv_cut, o_cut, gate_weight, up_weight, down_weight, cos_table, sin_table)
    x_float, gains, attn_in, q_team, kv_team, o_team, rot, mix, resid = outs[:9]
    ffn_in, dy_team, gate_team, up_team, down_team = outs[9:14]
    gain_one, gain_two = gains[0:1], gains[1:2]
    attn_in = attn_in.reshape(token_count, width)
    ffn_in = ffn_in.reshape(token_count, width)
    dy_low = dy_team[0]
    dy_team = dy_team.reshape(token_count, width)
    q_team, kv_team = q_team.reshape(width, q_width), kv_team.reshape(width, 2 * HEAD_DIM)
    gate_team, up_team, down_team = (w.reshape(width, hidden_cols) for w in (gate_team, up_team, down_team))
    mix = mix.reshape(token_count, q_width)

    def f32(*shape):
        return jax.ShapeDtypeStruct(shape, F32)

    def buffers(cols):
        part = (team, weight_rows, cols)
        return hbm(4, *part), hbm(2, *part), hbm(*part), hbm(*part)

    def scratch(*shape, dtype=BF16):
        return pltpu.VMEM(shape, dtype)

    if 2 * hidden_cols == width and KV_HEADS == team:
        half = team // 2
        span = width // team
        sums = [scratch(half, chunk, width), scratch(2, team // 4 - 1, chunk, width), scratch(chunk, width)]
        results = pl.pallas_call(
            functools.partial(exit_kernel, cp_size),
            out_shape=(
                hbm(teams, row_count, width),
                hbm(teams, row_count, width),
                f32(8, 128),
                hbm(team, weight_rows, hidden_cols),
                hbm(team, weight_rows, hidden_cols),
                hbm(team, weight_rows, hidden_cols),
                hbm(team, weight_rows, qkv_width),
                hbm(team, weight_rows, span),
                hbm(team, chunk, width),
                *buffers(hidden_cols),
                *buffers(hidden_cols),
                *buffers(hidden_cols),
                *buffers(qkv_width),
            ),
            in_specs=[vmem()] * 8 + [anywhere()] * 8,
            out_specs=tuple([anywhere()] * 2 + [vmem()] + [anywhere()] * 22),
            scratch_shapes=[
                pltpu.SemaphoreType.DMA((10 * team + 48,)),
                pltpu.SemaphoreType.DMA((10 * team + 48,)),
                pltpu.SemaphoreType.DMA((32,)),
                pltpu.SemaphoreType.DMA((2, 2)),
                pltpu.SemaphoreType.DMA((2, 2)),
                scratch(token_count, width),
                scratch(token_count, width),
                scratch(width, hidden_cols),
                scratch(width, hidden_cols),
                scratch(width, hidden_cols),
                scratch(width, qkv_width),
                scratch(team, chunk, width),
                scratch(token_count, hidden_cols),
                scratch(token_count, 2 * hidden_cols),
                scratch(2, 2, half, weight_rows, hidden_cols),
                scratch(2, 2, half, weight_rows, hidden_cols),
                *sums,
                *sums,
                scratch(chunk, width, dtype=F32),
                scratch(chunk, width, dtype=F32),
                scratch(chunk, width, dtype=F32),
                scratch(chunk, width),
                scratch(chunk, width),
                scratch(token_count, q_width),
                scratch(token_count, q_width, dtype=F32),
                scratch(token_count, 2 * HEAD_DIM, dtype=F32),
                scratch(token_count, qkv_width),
                scratch(width // 2, span),
                scratch(width // 4, span),
                scratch(width // 4, span),
                scratch(width // 4, span),
                scratch(devices, 8, 128, dtype=F32),
                scratch(devices, 8, 128, dtype=F32),
            ],
            compiler_params=pltpu.CompilerParams(
                collective_id=1, has_side_effects=True, vmem_limit_bytes=63 << 20
            ),
            name="exit",
        )(
            x_float,
            resid,
            gains,
            rot,
            mix.reshape(team, chunk, q_width),
            o_team,
            cos_table,
            sin_table,
            attn_in,
            ffn_in,
            dy_team,
            gate_team,
            up_team,
            down_team,
            q_team,
            kv_team,
        )
        block_out, input_grad, gain_grads, gate_parts, up_parts, down_parts, qkv_parts, o_parts = results[:8]
        def part_spec(cols):
            return pl.BlockSpec((1, weight_rows, cols), lambda member: (member, 0, 0))

        def row_spec(cols):
            return pl.BlockSpec((weight_rows, cols), lambda member: (0, member))

        def fixed_spec(*shape):
            return pl.BlockSpec(shape, lambda member: (0,) * len(shape))

        kv_width = team * HEAD_DIM
        wide_cols = [q_width, span, hidden_cols, hidden_cols, hidden_cols]
        joined = pl.pallas_call(
            functools.partial(join_kernel, team, q_width),
            grid=(team,),
            out_shape=tuple(f32(weight_rows, team * cols) for cols in wide_cols)
            + (f32(weight_rows, kv_width), f32(weight_rows, kv_width)),
            in_specs=[fixed_spec(team, weight_rows, qkv_width)] + [part_spec(cols) for cols in wide_cols[1:]],
            out_specs=tuple(row_spec(cols) for cols in wide_cols)
            + (fixed_spec(weight_rows, kv_width), fixed_spec(weight_rows, kv_width)),
            compiler_params=pltpu.CompilerParams(vmem_limit_bytes=VMEM_BYTES),
            name="join",
        )(qkv_parts, o_parts, gate_parts, up_parts, down_parts)
        q_out, o_out, gate_out, up_out, down_out, k_out, v_out = joined
        return (
            block_out,
            input_grad,
            gain_grads[0, :weight_rows],
            q_out,
            k_out,
            v_out,
            o_out,
            gain_grads[1, :weight_rows],
            gate_out,
            up_out,
            down_out,
        )

    inv_one = lax.rsqrt(jnp.mean(x_float * x_float, axis=-1, keepdims=True) + NORM_EPS)
    normed_one = x_float * inv_one
    inv_two = lax.rsqrt(jnp.mean(resid * resid, axis=-1, keepdims=True) + NORM_EPS)
    normed_two = resid * inv_two

    gate = dot(ffn_in, gate_team)
    up_val = dot(ffn_in, up_team)
    sigma = jax.nn.sigmoid(gate)
    silu_val = gate * sigma
    hidden = (silu_val * up_val).astype(BF16)
    hidden_grad = dot(dy_team, down_team)
    gate_grad = (hidden_grad * up_val * (sigma + gate * sigma * (1.0 - sigma))).astype(BF16)
    up_grad = (hidden_grad * silu_val).astype(BF16)

    half = token_count // 2

    def half_of(value, odd):
        return value[half * odd : half * (odd + 1)]

    ffn_in_grad = team_reduce(
        lambda odd: (
            contract_cols(half_of(gate_grad, odd), gate_team) + contract_cols(half_of(up_grad, odd), up_team)
        ).astype(BF16)
    )
    down_sum = team_reduce(lambda odd: contract_cols(half_of(hidden, odd), down_team).astype(BF16))
    block_out = give_rows(restore((resid + down_sum).astype(BF16)))

    ffn_gain_grad = scatter_small(restore(jnp.sum(ffn_in_grad * normed_two, axis=0)))
    scaled_two = ffn_in_grad * gain_two
    resid_grad = dy_low.astype(F32) + inv_two * (
        scaled_two - normed_two * jnp.mean(scaled_two * normed_two, axis=-1, keepdims=True)
    )
    branch_grad = team_gather(resid_grad.astype(BF16))
    mix_grad = contract_cols(branch_grad, o_team).astype(BF16).reshape(team, chunk, q_width)

    down_weight_grad = join(collect(contract_rows(dy_team, hidden).astype(BF16)))
    gate_weight_grad = join(collect(contract_rows(ffn_in, gate_grad).astype(BF16)))
    up_weight_grad = join(collect(contract_rows(ffn_in, up_grad).astype(BF16)))

    proj_grad = pl.pallas_call(
        functools.partial(attention_backward, team, block_len, q_width),
        out_shape=jax.ShapeDtypeStruct((token_count, qkv_width), BF16),
        in_specs=[smem(), vmem(), vmem(), vmem(), vmem()],
        out_specs=vmem(),
        scratch_shapes=[
            pltpu.VMEM((token_count, q_width), BF16),
            pltpu.VMEM((token_count, q_width), F32),
            pltpu.VMEM((token_count, 2 * HEAD_DIM), F32),
        ],
        compiler_params=pltpu.CompilerParams(vmem_limit_bytes=VMEM_BYTES),
        name="attention_backward",
    )(t.astype(jnp.int32).reshape(1), rot, mix_grad, cos_table, sin_table)

    qkv_team = jnp.concatenate([q_team, kv_team], axis=-1)
    attn_in_grad = team_reduce(lambda odd: contract_cols(half_of(proj_grad, odd), qkv_team).astype(BF16))
    attn_gain_grad = scatter_small(restore(jnp.sum(attn_in_grad * normed_one, axis=0)))
    scaled_one = attn_in_grad * gain_one
    input_grad = resid_grad + inv_one * (
        scaled_one - normed_one * jnp.mean(scaled_one * normed_one, axis=-1, keepdims=True)
    )
    input_grad = give_rows(restore(input_grad.astype(BF16)))

    qkv_grad = collect(contract_rows(attn_in, proj_grad).astype(BF16))
    q_weight_grad = join(qkv_grad[:, :, :q_width])
    k_weight_grad = sum_heads(qkv_grad[:, :, q_width : q_width + HEAD_DIM])
    v_weight_grad = sum_heads(qkv_grad[:, :, q_width + HEAD_DIM :])

    o_grad = restore(contract_rows(mix, branch_grad)).astype(BF16)
    o_grad = to_team(o_grad.reshape(q_width, team, -1).transpose(1, 0, 2)).reshape(width, -1)
    o_weight_grad = join(collect(reorder_rows(o_grad)))

    return (
        block_out,
        input_grad,
        attn_gain_grad,
        q_weight_grad,
        k_weight_grad,
        v_weight_grad,
        o_weight_grad,
        ffn_gain_grad,
        gate_weight_grad,
        up_weight_grad,
        down_weight_grad,
    )


def solution(mesh):
    rows = P(BOTH, None)
    placed = P("fsdp", "cp", None)
    gain = P(BOTH)
    return jax.shard_map(
        body,
        mesh=mesh,
        in_specs=(placed, placed, gain, rows, rows, rows, rows, gain, rows, rows, rows),
        out_specs=(placed, placed, gain, rows, rows, rows, rows, gain, rows, rows, rows),
        check_vma=False,
    )
```

```python
import functools

import jax
import jax.numpy as jnp
import numpy as np
from jax import lax
from jax.experimental import pallas as pl
from jax.experimental.pallas import tpu as pltpu
from jax.sharding import PartitionSpec as P

HEADS = 32
KV_HEADS = 8
HEAD_DIM = 64
HALF = HEAD_DIM // 2
NORM_EPS = 1e-05
ROPE_BASE = 500000.0
BOTH = ("fsdp", "cp")
F32 = jnp.float32
BF16 = jnp.bfloat16
MESH = pl.DeviceIdType.MESH
VMEM_BYTES = 60 << 20


def dot(left, right):
    return jnp.dot(left, right, preferred_element_type=F32)


def contract_rows(left, right):
    return lax.dot_general(left, right, (((0,), (0,)), ((), ())), preferred_element_type=F32)


def contract_cols(left, right):
    return lax.dot_general(left, right, (((1,), (1,)), ((), ())), preferred_element_type=F32)


def flip(index, mask):
    bit = 1
    out = index
    while bit <= mask:
        if mask & bit:
            out = out + bit - 2 * bit * ((index // bit) % 2)
        bit *= 2
    return out


def spot_of(diff, team):
    return diff // 2 + (diff % 2) * (team // 2)


def chunk_blocks(member, team):
    second = team + flip(member, team // 2)
    last = 4 * team - 1
    return member, last - member, second, last - second


def natural_unit(mine, index):
    block = flip(mine, index // 2)
    turned = block % 2
    return block * 2 + (index % 2) + turned * (1 - 2 * (index % 2))


def swap_halves(wide):
    pieces = []
    for start in range(0, wide.shape[-1], HEAD_DIM):
        pieces.append(wide[:, start + HALF : start + HEAD_DIM])
        pieces.append(wide[:, start : start + HALF])
    return jnp.concatenate(pieces, axis=-1)


def over_row_blocks(token_count, most, step):
    quarter = token_count // 4
    rows = min(most, (1 << 18) // token_count)
    for first in range(0, token_count, quarter):
        if rows == quarter:
            step(first, first + quarter, first, rows)
        else:

            def block(index, carry, first=first):
                step(first, first + quarter, pl.multiple_of(first + index * rows, rows), rows)
                return carry

            lax.fori_loop(0, quarter // rows, block, 0)


def turn_by(wide, cosine, sine):
    swapped = swap_halves(wide)
    pieces = []
    for start in range(0, wide.shape[-1], 2 * HEAD_DIM):
        piece = slice(start, start + 2 * HEAD_DIM)
        span = wide[:, piece].shape[-1]
        pieces.append(wide[:, piece] * cosine[:, :span] + swapped[:, piece] * sine[:, :span])
    return jnp.concatenate(pieces, axis=-1)


def masked_scores(query, keys, first, start):
    rows, span = query.shape[0], keys.shape[0] - first
    scores = contract_cols(query, keys)
    row = lax.broadcasted_iota(jnp.int32, (rows, span), 0) + (start - first)
    col = lax.broadcasted_iota(jnp.int32, (rows, span), 1)
    last = jnp.where(row >= col, scores[:, first:], -1e30)
    return jnp.concatenate([scores[:, :first], last], axis=-1) if first else last


def differ(left, right, size):
    out = 0
    bit = 1
    while bit < size:
        out = out + ((left // bit + right // bit) % 2) * bit
        bit *= 2
    return out


class Links:
    def __init__(self, cp_size, send, recv, local):
        self.f, self.c = lax.axis_index("fsdp"), lax.axis_index("cp")
        self.cp_size, self.send, self.recv, self.local = cp_size, send, recv, local
        self.used = self.used_local = 0

    def device(self, mask):
        return (flip(self.f, mask // self.cp_size), flip(self.c, mask % self.cp_size))

    def barrier(self, masks):
        sem = pltpu.get_barrier_semaphore()
        for mask in masks:
            pl.semaphore_signal(sem, inc=1, device_id=self.device(mask), device_id_type=MESH)
        pl.semaphore_wait(sem, len(masks))

    def copy(self, src, dst, mask):
        index = self.used
        self.used += 1
        return pltpu.make_async_remote_copy(
            src_ref=src,
            dst_ref=dst,
            send_sem=self.send.at[index],
            recv_sem=self.recv.at[index],
            device_id=self.device(mask),
            device_id_type=MESH,
        )

    def inside(self, src, dst):
        index = self.used_local
        self.used_local += 1
        return pltpu.make_async_copy(src, dst, self.local.at[index])


class TeamGather:
    def __init__(self, links, team, src, dst):
        near = team // 2
        row = range(2, near, 2)

        def place(mask):
            return dst.at[spot_of(mask, team)]

        self.to_near = links.copy(src, place(near), near)
        self.to_row = [links.copy(src, place(m), m) for m in row]
        self.on = [links.copy(place(near), place(near + m), m) for m in row]
        self.to_core = links.copy(src, place(1), 1)
        self.near_core = links.copy(place(near), place(near + 1), 1)
        self.row_core = [links.copy(place(m), place(m + 1), 1) for m in row]
        self.on_core = [links.copy(place(near + m), place(near + m + 1), 1) for m in row]
        self.own = links.inside(src, dst.at[0])

    def start(self):
        self.to_near.start()
        for copy in self.to_row:
            copy.start()
        self.to_core.start()
        self.own.start()

    def pass_near(self):
        self.to_near.wait_recv()
        for copy in self.on:
            copy.start()
        self.near_core.start()

    def pass_row(self):
        for copy, core in zip(self.to_row, self.row_core):
            copy.wait_recv()
            core.start()

    def pass_on(self):
        for copy, core in zip(self.on, self.on_core):
            copy.wait_recv()
            core.start()

    def finish(self):
        core = [self.to_core, self.near_core] + self.row_core + self.on_core
        for copy in core:
            copy.wait_recv()
        for copy in [self.to_near] + self.to_row + self.on + core:
            copy.wait_send()
        self.own.wait()


class TeamSum:
    def __init__(self, links, team, parts, taken, row_in, near_in):
        self.team, self.parts, self.taken, self.row_in, self.near_in = team, parts, taken, row_in, near_in
        near = team // 2
        self.row = list(range(2, near, 2))
        half = team // 2
        self.cross = [links.copy(parts.at[half + e], taken.at[e], 1) for e in range(half)]
        self.far = [links.copy(parts.at[(near + m) // 2], row_in.at[0, i], m) for i, m in enumerate(self.row)]
        self.here = [links.copy(parts.at[m // 2], row_in.at[1, i], m) for i, m in enumerate(self.row)]
        self.last = links.copy(parts.at[near // 2], near_in, near)

    def start(self, make, near_sum, own_sum):
        half, rows, width = self.taken.shape
        pieces = [slice(start, start + 512) for start in range(0, width, 512)]
        for low in range(half - 2, -1, -2):
            for cols in pieces:
                value = make(pl.ds((half + low) * rows, 2 * rows), cols).astype(BF16)
                for k in range(2):
                    self.parts[half + low + k, :, cols] = value[k * rows : (k + 1) * rows]
            self.cross[low + 1].start()
            self.cross[low].start()
        for low in range(half - 2, -1, -2):
            self.cross[low + 1].wait_recv()
            self.cross[low].wait_recv()
            for cols in pieces:
                value = make(pl.ds(low * rows, 2 * rows), cols)
                for k in range(2):
                    spot = low + k
                    part = value[k * rows : (k + 1) * rows] + self.taken[spot, :, cols].astype(F32)
                    if spot == half // 2:
                        near_sum[:, cols] = part
                    elif spot == 0:
                        own_sum[:, cols] = part
                    else:
                        self.parts[spot, :, cols] = part.astype(BF16)
            for spot in (low + 1, low):
                if spot > half // 2:
                    self.far[spot - half // 2 - 1].start()
                elif 0 < spot < half // 2:
                    self.here[spot - 1].start()

    def pass_near(self, value):
        for index, copy in enumerate(self.far):
            copy.wait_recv()
            value = value + self.row_in[0, index].astype(F32)
        self.parts[self.team // 4] = value.astype(BF16)
        self.last.start()

    def total(self, value):
        for index, copy in enumerate(self.here):
            copy.wait_recv()
            value = value + self.row_in[1, index].astype(F32)
        self.last.wait_recv()
        return value + self.near_in[...].astype(F32)

    def finish(self):
        for copy in self.cross + self.far + self.here + [self.last]:
            copy.wait_send()


class Spread:
    def __init__(self, links, team, t, pieces, full):
        self.own = links.inside(pieces(0), full.at[0, t])
        self.cuts = [links.copy(pieces(m), full.at[0, t], m) for m in range(1, team)]
        parts = [pl.ds(start, team // 2) for start in (0, team // 2)]
        self.far = [links.copy(full.at[0], full.at[2], links.cp_size)]
        self.far += [links.copy(full.at[1, part], full.at[3, part], links.cp_size) for part in parts]
        self.side = [links.copy(full.at[0, part], full.at[1, part], team + team // 2) for part in parts]
        self.outer = t // (team // 2) == 0

    def cut(self):
        self.own.start()
        for piece in self.cuts:
            piece.start()

    def leave(self):
        self.own.wait()
        for piece in self.cuts:
            piece.wait_recv()
        self.far[0].start()
        self.cross(False)

    def cross(self, outer):
        @pl.when(self.outer == outer)
        def _():
            for copy in self.side:
                copy.start()

    def arrive(self):
        for copy, far in zip(self.side, self.far[1:]):
            copy.wait_recv()
            far.start()

    def finish(self):
        for copy in self.far:
            copy.wait_recv()
        for copy in self.cuts + self.far + self.side:
            copy.wait_send()


class Collect:
    def __init__(self, links, team, t, grad, far_in, side_in, final, out):
        self.grad, self.far_in, self.side_in, self.final = grad, far_in, side_in, final
        self.outer = t // (team // 2) == 0
        parts = [pl.ds(start, team // 2) for start in (0, team // 2)]
        self.far = [[links.copy(grad.at[b + 2, part], far_in.at[b, part], links.cp_size) for part in parts] for b in range(2)]
        self.side = [links.copy(grad.at[1, part], side_in.at[part], team + team // 2) for part in parts]
        self.own = links.inside(final.at[t], out.at[t])
        self.cuts = [links.copy(final.at[flip(t, m)], out.at[t], m) for m in range(1, team)]

    def cut(self):
        self.own.start()
        for piece in self.cuts:
            piece.start()

    def finish(self):
        self.own.wait()
        for copy in self.far[0] + self.far[1] + self.side:
            copy.wait_send()
        for piece in self.cuts:
            piece.wait()


def entry_kernel(
    fsdp_size,
    cp_size,
    tokens,
    cotangent,
    gains_in,
    q_cut,
    kv_cut,
    o_cut,
    gate_in,
    up_in,
    down_in,
    cos_ref,
    sin_ref,
    x_ref,
    gains_ref,
    attn_in_ref,
    q_full,
    kv_full,
    o_wide,
    rot_ref,
    mix_ref,
    resid_ref,
    ffn_in_ref,
    dy_ref,
    gate_full,
    up_full,
    down_full,
    o_full,
    send,
    recv,
    local,
    swapped,
    dy_swapped,
    slots,
    chunk_ref,
    dy_chunk,
    acts,
    q_w,
    kv_w,
    mixed,
    o_pieces,
    taken,
    row_in,
    near_in,
    near_sum,
):
    links = Links(cp_size, send, recv, local)
    f, c = links.f, links.c
    team = cp_size // 2
    near, mirror = team // 2, team + team // 2
    side = c // team
    t = c % team + side * (flip(c, near) - c)
    row_count, width = tokens.shape[1], tokens.shape[2]
    block_len = row_count // 2
    unit = width // 8
    token_count, q_width = mixed.shape
    heads = q_width // HEAD_DIM
    cols = gate_full.shape[-1]
    mine = f * 2 + side

    links.barrier(list(range(1, team)) + [mirror, cp_size])
    swap = links.copy(tokens.at[1 - side], swapped, mirror)
    swap.start()
    slots[0] = gains_in[...]
    stages = []
    size = 1
    for mask in [1 << k for k in range(team.bit_length() - 1)] + [mirror, cp_size]:
        stages.append(links.copy(slots.at[pl.ds(0, size)], slots.at[pl.ds(size, size)], mask))
        size *= 2

    def columns_of(weight):
        if len(weight.shape) == 3:
            return lambda m: weight.at[flip(t, m)]
        count = weight.shape[1] // team
        return lambda m: weight.at[:, pl.ds(pl.multiple_of(flip(t, m) * count, count), count)]

    def spread(pieces, full):
        return Spread(links, team, t, pieces, full)

    q_spread = spread(columns_of(q_cut), q_full)
    kv_spread = spread(columns_of(kv_cut), kv_full)
    o_spread = spread(columns_of(o_cut), o_full)
    gate_spread = spread(columns_of(gate_in), gate_full)
    up_spread = spread(columns_of(up_in), up_full)
    down_spread = spread(columns_of(down_in), down_full)

    stages[0].start()
    q_spread.cut()
    kv_spread.cut()
    o_spread.cut()
    for step in range(1, len(stages)):
        stages[step - 1].wait_recv()
        stages[step].start()
    gate_spread.cut()

    def fill(dst, source, theirs):
        here = pl.ds(pl.multiple_of(side * row_count, row_count), row_count)
        there = pl.ds(pl.multiple_of((1 - side) * row_count, row_count), row_count)
        for index in range(8):
            cols = slice(index * unit, (index + 1) * unit)
            natural = pl.ds(pl.multiple_of(natural_unit(mine, index) * unit, unit), unit)
            dst[here, cols] = source[side, :, natural].astype(dst.dtype)
            dst[there, cols] = theirs[:, natural].astype(dst.dtype)

    stages[-1].wait_recv()
    pieces = []
    for b in range(4):
        for member in range(team):
            pieces.append(slots[b * team + flip(t, member)][:8, : width // (4 * team)])
    gains = jnp.concatenate(pieces, axis=-1).astype(F32)
    gains_ref[...] = gains
    swap.wait_recv()
    fill(x_ref, tokens, swapped)
    x = x_ref[...]
    inv_one = lax.rsqrt(jnp.mean(x * x, axis=-1, keepdims=True) + NORM_EPS)
    chunk_ref[...] = (x * inv_one * gains[0:1]).astype(BF16)
    gather_one = TeamGather(links, team, chunk_ref, acts)
    gather_one.start()
    dy_swap = links.copy(cotangent.at[1 - side], dy_swapped, mirror)
    dy_swap.start()
    q_spread.leave()
    kv_spread.leave()
    q_spread.cross(True)
    kv_spread.cross(True)
    o_spread.leave()
    o_spread.cross(True)
    gather_one.pass_near()
    gather_one.pass_row()
    gate_spread.leave()
    gate_spread.cross(True)
    gather_one.pass_on()
    up_spread.cut()
    down_spread.cut()
    q_spread.arrive()
    kv_spread.arrive()
    o_spread.arrive()
    up_spread.leave()
    q_spread.finish()
    kv_spread.finish()
    weight_loads = [links.inside(q_full, q_w), links.inside(kv_full, kv_w)]
    for load in weight_loads:
        load.start()
    gather_one.finish()
    attn_out = links.inside(acts, attn_in_ref)
    attn_out.start()
    o_spread.finish()

    o_rows = o_full.shape[2]

    def o_source(m):
        count = q_width // o_rows
        first = flip(t, m) * count
        owners, start = first // team, first % team
        block = ((owners // 2 + mine // 2) % 2) * 2 + (owners + mine) % 2
        return o_full.at[block, pl.ds(start + (owners % 2) * (flip(start, near) - start), count)]

    o_own = links.inside(o_source(0), o_pieces.at[t])
    o_sends = [links.copy(o_source(m), o_pieces.at[t], m) for m in range(1, team)]
    o_own.start()
    for copy in o_sends:
        copy.start()

    for load in weight_loads:
        load.wait()
    q_weights = q_w[...].reshape(width, q_width)
    kv_weights = kv_w[...].reshape(width, 2 * HEAD_DIM)

    def project(m, carry):
        rows_in = acts[spot_of(m, team)]
        key_value = dot(rows_in, kv_weights)
        qk = jnp.concatenate([dot(rows_in, q_weights) * HEAD_DIM ** (-0.5), key_value[:, :HEAD_DIM]], axis=-1)
        blocks = chunk_blocks(differ(t, m, team), team)
        for slot in range(4):
            piece = slice(slot * block_len, (slot + 1) * block_len)
            rows = pl.ds(pl.multiple_of(blocks[slot] * block_len, block_len), block_len)
            turned = turn_by(qk[piece], cos_ref[rows, :], sin_ref[rows, :])
            rot_ref[rows, :] = jnp.concatenate([turned, key_value[piece, HEAD_DIM:]], axis=-1).astype(BF16)
        return carry

    lax.fori_loop(0, team, project, 0)

    dy_swap.wait_recv()
    fill(dy_chunk, cotangent, dy_swapped)
    gather_dy = TeamGather(links, team, dy_chunk, dy_ref)
    down_spread.leave()

    def attend(first, span, start, rows):
        keys = rot_ref[:span, q_width : q_width + HEAD_DIM]
        values = rot_ref[:span, q_width + HEAD_DIM :]
        outs = []
        for head in range(heads):
            query = rot_ref[pl.ds(start, rows), head * HEAD_DIM : (head + 1) * HEAD_DIM]
            scores = masked_scores(query, keys, first, start)
            peak = jnp.max(scores, axis=-1, keepdims=True)
            expo = jnp.exp(scores - peak)
            total = jnp.sum(expo, axis=-1, keepdims=True)
            outs.append(dot(expo.astype(BF16), values) / total)
        mixed[pl.ds(start, rows), :] = jnp.concatenate(outs, axis=-1).astype(BF16)

    over_row_blocks(token_count, 256, attend)

    def collect_mix(m, carry):
        blocks = chunk_blocks(differ(t, m, team), team)
        for slot in range(4):
            where = pl.ds(pl.multiple_of(blocks[slot] * block_len, block_len), block_len)
            mix_ref[spot_of(m, team), slot * block_len : (slot + 1) * block_len, :] = mixed[where, :]
        return carry

    lax.fori_loop(0, team, collect_mix, 0)
    for copy in o_sends:
        copy.wait_recv()
    o_own.wait()
    span = width // team
    for index in range(8):
        for piece in range(team // 8):
            start = index * unit + piece * span
            source = natural_unit(mine, index) * (team // 8) + piece
            o_wide[:, start : start + span] = o_pieces[source].reshape(q_width, span)

    attn_out.wait()
    summed = TeamSum(links, team, acts, taken, row_in, near_in)
    row_pair = 2 * row_count

    def mix_out(place, cols):
        spots = pl.ds(place.start // row_pair, 2)
        return dot(mix_ref[spots].reshape(2 * row_pair, q_width), o_wide[:, cols])

    summed.start(mix_out, near_sum, resid_ref)
    summed.pass_near(near_sum[...])
    up_spread.cross(True)
    resid_ref[...] = x_ref[...] + summed.total(resid_ref[...])
    resid = resid_ref[...]
    inv_two = lax.rsqrt(jnp.mean(resid * resid, axis=-1, keepdims=True) + NORM_EPS)
    chunk_ref[...] = (resid * inv_two * gains_ref[1:2]).astype(BF16)
    gather_two = TeamGather(links, team, chunk_ref, ffn_in_ref)
    gather_two.start()
    down_spread.cross(True)
    gate_spread.arrive()
    gather_two.pass_near()
    gather_two.pass_row()
    gather_two.pass_on()
    gather_dy.start()
    up_spread.arrive()
    gate_spread.finish()
    down_spread.arrive()
    gather_two.finish()
    gather_dy.pass_near()
    gather_dy.pass_row()
    gather_dy.pass_on()
    gather_dy.finish()
    up_spread.finish()
    down_spread.finish()
    swap.wait_send()
    dy_swap.wait_send()
    summed.finish()
    for copy in stages + o_sends:
        copy.wait_send()


def backward_heads(token_count, q_width, rot_ref, wide_ref, cos_ref, sin_ref, dq_ref, dkv_ref):
    heads = q_width // HEAD_DIM
    dkv_ref[...] = jnp.zeros_like(dkv_ref)

    def attend(first, span, start, count):
        rows = pl.ds(start, count)
        keys = rot_ref[:span, q_width : q_width + HEAD_DIM]
        values = rot_ref[:span, q_width + HEAD_DIM :]
        for head in range(heads):
            cols = slice(head * HEAD_DIM, (head + 1) * HEAD_DIM)
            query = rot_ref[rows, cols]
            grad = wide_ref[rows, cols]
            scores = masked_scores(query, keys, first, start)
            peak = jnp.max(scores, axis=-1, keepdims=True)
            expo = jnp.exp(scores - peak)
            probs = expo / jnp.sum(expo, axis=-1, keepdims=True)
            dprob = contract_cols(grad, values)
            delta = jnp.sum(probs * dprob, axis=-1, keepdims=True)
            score_grad = (probs * (dprob - delta)).astype(BF16)
            dq_ref[rows, cols] = dot(score_grad, keys)
            dk = contract_rows(score_grad, query)
            dv = contract_rows(probs.astype(BF16), grad)
            dkv_ref[:span, :] += jnp.concatenate([dk, dv], axis=-1)

    over_row_blocks(token_count, 128, attend)

    for start in range(0, token_count, token_count // 4):
        rows = slice(start, start + token_count // 4)
        qk = jnp.concatenate([dq_ref[rows, :], dkv_ref[rows, :HEAD_DIM]], axis=-1)
        turned = turn_by(qk, cos_ref[rows, :], -sin_ref[rows, :])
        dq_ref[rows, :] = turned[:, :q_width] * HEAD_DIM ** (-0.5)
        dkv_ref[rows, :] = jnp.concatenate([turned[:, q_width:], dkv_ref[rows, HEAD_DIM:]], axis=-1)


def scatter_chunk(t, m, team, block_len, wide_ref, value):
    blocks = chunk_blocks(differ(t, m, team), team)
    for slot in range(4):
        where = pl.ds(pl.multiple_of(blocks[slot] * block_len, block_len), block_len)
        wide_ref[where, :] = value[slot * block_len : (slot + 1) * block_len, :]


def gather_chunk(t, m, team, block_len, out_ref, *sources):
    blocks = chunk_blocks(differ(t, m, team), team)
    for slot in range(4):
        rows = pl.ds(pl.multiple_of(blocks[slot] * block_len, block_len), block_len)
        place = pl.ds(pl.multiple_of((spot_of(m, team) * 4 + slot) * block_len, block_len), block_len)
        piece = jnp.concatenate([source[rows, :] for source in sources], axis=-1)
        out_ref[place, :] = piece.astype(BF16)


def attention_backward(
    team, block_len, q_width, where_ref, rot_ref, grad_ref, cos_ref, sin_ref, out_ref, wide_ref, dq_ref, dkv_ref
):
    t = where_ref[0]

    def place_grad(m, carry):
        scatter_chunk(t, m, team, block_len, wide_ref, grad_ref[spot_of(m, team)])
        return carry

    lax.fori_loop(0, team, place_grad, 0)
    backward_heads(wide_ref.shape[0], q_width, rot_ref, wide_ref, cos_ref, sin_ref, dq_ref, dkv_ref)

    def give_chunk(m, carry):
        gather_chunk(t, m, team, block_len, out_ref, dq_ref, dkv_ref)
        return carry

    lax.fori_loop(0, team, give_chunk, 0)


def exit_kernel(
    cp_size,
    x_ref,
    resid_ref,
    gains_ref,
    rot_ref,
    mix_ref,
    o_wide,
    cos_ref,
    sin_ref,
    attn_in,
    ffn_in,
    dy,
    gate_in,
    up_in,
    down_in,
    q_in,
    kv_in,
    block_out,
    input_grad,
    gain_grads,
    gate_out,
    up_out,
    down_out,
    qkv_out,
    o_out,
    branch,
    gate_grad,
    gate_far,
    gate_side,
    gate_final,
    up_grad,
    up_far,
    up_side,
    up_final,
    down_grad,
    down_far,
    down_side,
    down_final,
    qkv_grad,
    qkv_far,
    qkv_side,
    qkv_final,
    send,
    recv,
    local,
    store_sem,
    load_sem,
    first,
    second,
    gate_w,
    up_w,
    down_w,
    qkv_w,
    parts,
    hidden,
    both,
    stage_out,
    stage_in,
    taken_one,
    row_one,
    near_one,
    taken_two,
    row_two,
    near_two,
    resid_grad,
    near_sum,
    own_sum,
    chunk_ref,
    grad_rows,
    wide,
    dq_ref,
    dkv_ref,
    proj_grad,
    o_far,
    o_two,
    o_side,
    o_final,
    gain_slots,
    gain_in,
):
    links = Links(cp_size, send, recv, local)
    f, c = links.f, links.c
    team = cp_size // 2
    near, mirror = team // 2, team + team // 2
    side = c // team
    t = c % team + side * (flip(c, near) - c)
    mine = f * 2 + side
    half = team // 2
    token_count, width = first.shape
    rows = token_count // team
    row_count = rows // 2
    block_len = row_count // 2
    unit = width // 8
    cols = hidden.shape[1]
    q_width = wide.shape[1]
    weight_rows = gate_grad.shape[2]

    links.barrier(list(range(1, team)) + [mirror, cp_size])
    loads = [
        links.inside(source, target)
        for source, target in (
            (ffn_in, first),
            (gate_in, gate_w),
            (up_in, up_w),
            (dy, second),
            (down_in, down_w),
            (q_in, qkv_w.at[:, pl.ds(0, q_in.shape[1])]),
            (kv_in, qkv_w.at[:, pl.ds(q_in.shape[1], kv_in.shape[1])]),
        )
    ]
    for load in loads:
        load.start()
    for load in loads[:3]:
        load.wait()

    steps = token_count // 256

    def forward(index, carry):
        place = pl.ds(pl.multiple_of(index * 256, 256), 256)
        spots = pl.ds(index * (256 // rows), 256 // rows)
        block = first[place, :]
        for start in range(0, cols, 256):
            cut = slice(start, start + 256)
            later = slice(cols + start, cols + start + 256)
            gate = dot(block, gate_w[:, cut])
            up_val = dot(block, up_w[:, cut])
            sigma = jax.nn.sigmoid(gate)
            silu_val = gate * sigma
            hidden[place, cut] = (silu_val * up_val).astype(BF16)
            factor = up_val * (sigma + silu_val * (1.0 - sigma))
            parts[spots, :, cut] = silu_val.astype(BF16).reshape(256 // rows, rows, 256)
            parts[spots, :, later] = factor.astype(BF16).reshape(256 // rows, rows, 256)
        return carry

    lax.fori_loop(0, steps, forward, 0)

    def produce(left, right, offset, widths, place, targets, adds):
        block, part = place // 2, pl.ds((place % 2) * half, half)
        waits = []
        for a, sources in enumerate(adds):
            for k, source in enumerate(sources):
                load = pltpu.make_async_copy(source(block, part), stage_in.at[a, k, :, :, : widths[k]], load_sem.at[a, k])
                load.start()
                waits.append(load)
        turned = left[:, place * unit : (place + 1) * unit].T
        stores = []
        for k, span in enumerate(widths):
            value = dot(turned, right[:, offset : offset + span]).reshape(half, weight_rows, span)
            for a in range(len(adds)):
                waits[a * len(widths) + k].wait()
                value = value + stage_in[a, k, :, :, :span].astype(F32)
            stage_out[k, :, :, :span] = value.astype(BF16)
            store = pltpu.make_async_copy(stage_out.at[k, :, :, :span], targets[k](block, part), store_sem.at[k])
            store.start()
            stores.append(store)
            offset += span
        for store in stores:
            store.wait()

    def in_block(ref):
        return lambda block, part: ref.at[block, part]

    def in_side(ref):
        return lambda block, part: ref.at[part]

    def give_far(block, left, right, offset, widths, collects):
        for h in range(2):
            produce(left, right, offset, widths, 4 + 2 * block + h, [in_block(k.grad) for k in collects], [])
            for collect in collects:
                collect.far[block][h].start()

    def give_side(left, right, offset, widths, collects):
        sources = [in_block(k.far_in) for k in collects]
        for h in range(2):
            for collect in collects:
                collect.far[1][h].wait_recv()
            produce(left, right, offset, widths, 2 + h, [in_block(k.grad) for k in collects], [sources])
            for collect in collects:
                collect.side[h].start()

    def give_final(left, right, offset, widths, collects):
        sources = [[in_block(k.far_in) for k in collects], [in_side(k.side_in) for k in collects]]
        for h in range(2):
            for collect in collects:
                collect.far[0][h].wait_recv()
                collect.side[h].wait_recv()
            produce(left, right, offset, widths, h, [in_side(k.final) for k in collects], sources)
        for collect in collects:
            collect.cut()

    gate_sum = Collect(links, team, t, gate_grad, gate_far, gate_side, gate_final, gate_out)
    up_sum = Collect(links, team, t, up_grad, up_far, up_side, up_final, up_out)
    down_sum = Collect(links, team, t, down_grad, down_far, down_side, down_final, down_out)
    qkv_sum = Collect(links, team, t, qkv_grad, qkv_far, qkv_side, qkv_final, qkv_out)

    loads[3].wait()
    give_far(1, second, hidden, 0, [cols], [down_sum])
    loads[4].wait()

    def backward(index, carry):
        place = pl.ds(pl.multiple_of(index * 256, 256), 256)
        spots = pl.ds(index * (256 // rows), 256 // rows)
        block = second[place, :]
        for start in range(0, cols, 256):
            cut = slice(start, start + 256)
            later = slice(cols + start, cols + start + 256)
            hidden_grad = dot(block, down_w[:, cut])
            silu_val = parts[spots, :, cut].reshape(256, 256).astype(F32)
            factor = parts[spots, :, later].reshape(256, 256).astype(F32)
            both[place, cut] = (hidden_grad * factor).astype(BF16)
            both[place, later] = (hidden_grad * silu_val).astype(BF16)
        return carry

    lax.fori_loop(0, steps, backward, 0)

    def team_sum(taken, row_in, near_in, make):
        summed = TeamSum(links, team, parts, taken, row_in, near_in)
        summed.start(make, near_sum, own_sum)
        return summed

    def finish_sum(summed):
        value = summed.total(own_sum[...])
        summed.finish()
        return value

    ffn_sum = team_sum(
        taken_one,
        row_one,
        near_one,
        lambda place, cut: contract_cols(both[place, :cols], gate_w[cut, :]) + contract_cols(both[place, cols:], up_w[cut, :]),
    )
    ffn_sum.pass_near(near_sum[...])
    give_far(1, first, both, 0, [cols, cols], [gate_sum, up_sum])
    give_far(0, second, hidden, 0, [cols], [down_sum])
    give_side(second, hidden, 0, [cols], [down_sum])
    give_far(0, first, both, 0, [cols, cols], [gate_sum, up_sum])
    ffn_in_grad = ffn_sum.total(own_sum[...])
    ffn_sum.finish()

    def place_gain(row, value):
        share = width // (4 * team)
        for b in range(4):
            for member in range(team):
                start = (b * team + member) * share
                gain_slots[b * team + flip(t, member), row : row + 1, :share] = value[:, start : start + share]

    gain_slots[...] = jnp.zeros_like(gain_slots)
    resid = resid_ref[...]
    inv_two = lax.rsqrt(jnp.mean(resid * resid, axis=-1, keepdims=True) + NORM_EPS)
    normed = resid * inv_two
    place_gain(1, jnp.sum(ffn_in_grad * normed, axis=0, keepdims=True))
    scaled = ffn_in_grad * gains_ref[1:2]
    value = second[:rows, :].astype(F32) + inv_two * (
        scaled - normed * jnp.mean(scaled * normed, axis=-1, keepdims=True)
    )
    resid_grad[...] = value
    chunk_ref[...] = value.astype(BF16)
    gather = TeamGather(links, team, chunk_ref, branch)
    gather.start()
    give_side(first, both, 0, [cols], [gate_sum])
    gather.pass_near()
    gather.pass_row()
    out_sum = team_sum(taken_two, row_two, near_two, lambda place, cut: contract_cols(hidden[place, :], down_w[cut, :]))
    gather.pass_on()
    give_side(first, both, cols, [cols], [up_sum])
    gather.finish()

    branch_loads = []
    for h in range(2):
        for spot in range(team):
            target = gate_w.at[pl.ds(h * token_count + spot * rows, rows)]
            branch_loads.append(links.inside(branch.at[spot, :, pl.ds(h * cols, cols)], target))
    for load in branch_loads:
        load.start()
    for load in branch_loads:
        load.wait()

    for low in range(0, team, 2):
        left, right = (pl.ds(h * token_count + low * rows, 2 * rows) for h in range(2))
        value = contract_cols(gate_w[left, :], o_wide[:, :cols]) + contract_cols(gate_w[right, :], o_wide[:, cols:])
        value = value.astype(BF16)
        for spot in range(2):
            m = 2 * (low + spot) if low + spot < half else 2 * (low + spot - half) + 1
            scatter_chunk(t, m, team, block_len, wide, value[spot * rows : (spot + 1) * rows])

    def head_rows(member):
        return pl.ds(pl.multiple_of(member * q_width, q_width), q_width)

    span = width // team
    turned = mix_ref[...].reshape(token_count, q_width).T
    for index in range(8):
        above = index * unit // cols * token_count
        start = index * unit % cols
        value = dot(turned, gate_w[above : above + token_count, start : start + unit]).astype(BF16)
        for piece in range(team // 8):
            target = natural_unit(mine, index) * (team // 8) + piece
            up_w[head_rows(target), span : 2 * span] = value[:, piece * span : (piece + 1) * span]
    quarter = width // 4
    o_place = up_w.at[head_rows(t), pl.ds(0, span)]

    def o_part(member):
        return up_w.at[head_rows(member), pl.ds(span, span)]

    def o_land(block):
        return up_w[pl.ds(pl.multiple_of(block * quarter, quarter), quarter), :span].astype(F32)

    o_own = links.inside(o_part(t), o_place)
    o_sends = [links.copy(o_part(flip(t, m)), o_place, m) for m in range(1, team)]
    o_own.start()
    for copy in o_sends:
        copy.start()

    out_sum.pass_near(near_sum[...])
    backward_heads(token_count, q_width, rot_ref, wide, cos_ref, sin_ref, dq_ref, dkv_ref)

    def give_chunk(m, carry):
        gather_chunk(t, m, team, block_len, proj_grad, dq_ref, dkv_ref)
        return carry

    lax.fori_loop(0, team, give_chunk, 0)
    for copy in o_sends:
        copy.wait_recv()
    o_own.wait()
    other_half = pl.ds(pl.multiple_of((1 - f) * 2 * quarter, 2 * quarter), 2 * quarter)
    o_across = links.copy(up_w.at[other_half, pl.ds(0, span)], o_far, cp_size)
    o_across.start()
    o_cross = links.copy(o_two, o_side, mirror)

    def o_came(block):
        return o_far[pl.ds(pl.multiple_of(block * quarter, quarter), quarter), :].astype(F32)

    def give_rows(value, target, out):
        for index in range(8):
            natural = pl.ds(pl.multiple_of(natural_unit(mine, index) * unit, unit), unit)
            target[:, natural] = value[:, index * unit : (index + 1) * unit].astype(BF16)
        here = pl.ds(pl.multiple_of(side * row_count, row_count), row_count)
        there = pl.ds(pl.multiple_of((1 - side) * row_count, row_count), row_count)
        own = links.inside(target.at[here], out.at[side])
        other = links.copy(target.at[there], out.at[side], mirror)
        own.start()
        other.start()
        return own, other

    out_copies = give_rows(resid_ref[...] + finish_sum(out_sum), chunk_ref, block_out)
    qkv_width = q_width + 2 * HEAD_DIM
    loads[5].wait()
    loads[6].wait()
    attn_sum = team_sum(
        taken_one,
        row_one,
        near_one,
        lambda place, cut: contract_cols(proj_grad[place, :], qkv_w[cut, :]),
    )
    attn_sum.pass_near(near_sum[...])
    attn_load = links.inside(attn_in, second)
    give_final(second, hidden, 0, [cols], [down_sum])
    attn_load.start()
    attn_load.wait()
    give_far(1, second, proj_grad, 0, [qkv_width], [qkv_sum])
    give_far(0, second, proj_grad, 0, [qkv_width], [qkv_sum])
    o_across.wait_recv()
    o_two[...] = (o_land(f * 2 + 1 - side) + o_came(1 - side)).astype(BF16)
    o_cross.start()
    attn_in_grad = finish_sum(attn_sum)

    x = x_ref[...]
    inv_one = lax.rsqrt(jnp.mean(x * x, axis=-1, keepdims=True) + NORM_EPS)
    normed = x * inv_one
    place_gain(0, jnp.sum(attn_in_grad * normed, axis=0, keepdims=True))
    size = 2 * team
    gain_steps = []
    for mask in [cp_size, mirror] + [1 << k for k in reversed(range(team.bit_length() - 1))]:
        gain_steps.append(links.copy(gain_slots.at[pl.ds(size, size)], gain_in.at[pl.ds(size, size)], mask))
        size //= 2
    gain_steps[0].start()
    scaled = attn_in_grad * gains_ref[0:1]
    value = resid_grad[...] + inv_one * (scaled - normed * jnp.mean(scaled * normed, axis=-1, keepdims=True))
    grad_copies = give_rows(value, grad_rows, input_grad)

    give_side(second, proj_grad, 0, [qkv_width], [qkv_sum])
    give_final(first, both, 0, [cols], [gate_sum])
    size = 2 * team
    for index, step in enumerate(gain_steps):
        step.wait_recv()
        gain_slots[:size] += gain_in[size : 2 * size]
        size //= 2
        if index + 1 < len(gain_steps):
            gain_steps[index + 1].start()
    gain_grads[...] = gain_slots[0]
    o_cross.wait_recv()
    o_final[...] = (o_land(f * 2 + side) + o_came(side) + o_side[...].astype(F32)).astype(BF16)

    def o_rows(member):
        place = member + side * (flip(member, near) - member)
        return o_final.at[pl.ds(pl.multiple_of(place * weight_rows, weight_rows), weight_rows)]

    o_last = links.inside(o_rows(t), o_out.at[t])
    o_gives = [links.copy(o_rows(flip(t, m)), o_out.at[t], m) for m in range(1, team)]
    o_last.start()
    for copy in o_gives:
        copy.start()
    give_final(first, both, cols, [cols], [up_sum])
    give_final(second, proj_grad, 0, [qkv_width], [qkv_sum])
    for own, other in (out_copies, grad_copies):
        own.wait()
        other.wait()
    for copy in o_sends + [o_across, o_cross] + gain_steps:
        copy.wait_send()
    for copy in o_gives:
        copy.wait()
    o_last.wait()
    for collect in (down_sum, gate_sum, up_sum, qkv_sum):
        collect.finish()


def join_kernel(
    team,
    q_width,
    qkv,
    block_in,
    grad_in,
    o_part,
    gate_part,
    up_part,
    down_part,
    q_out,
    o_out,
    gate_out,
    up_out,
    down_out,
    k_out,
    v_out,
    block_out,
    grad_out,
):
    step = pl.program_id(0)
    for k in range(2):
        q_out[:, k * q_width : (k + 1) * q_width] = qkv[2 * step + k, :, :q_width].astype(F32)
        for part, out in ((o_part, o_out), (gate_part, gate_out), (up_part, up_out), (down_part, down_out)):
            cols = part.shape[2]
            out[:, k * cols : (k + 1) * cols] = part[k].astype(F32)

    @pl.when(step == 0)
    def _():
        keys, values = slice(q_width, q_width + HEAD_DIM), slice(q_width + HEAD_DIM, q_width + 2 * HEAD_DIM)
        k_out[...] = jnp.concatenate([qkv[k, :, keys] for k in range(team)], axis=-1).astype(F32)
        v_out[...] = jnp.concatenate([qkv[k, :, values] for k in range(team)], axis=-1).astype(F32)
        block_out[...] = block_in[...]
        grad_out[...] = grad_in[...]


def vmem():
    return pl.BlockSpec(memory_space=pltpu.VMEM)


def smem():
    return pl.BlockSpec(memory_space=pltpu.SMEM)


def anywhere():
    return pl.BlockSpec(memory_space=pl.ANY)


def body(
    tokens,
    cotangent,
    attn_gain,
    q_weight,
    k_weight,
    v_weight,
    o_weight,
    ffn_gain,
    gate_weight,
    up_weight,
    down_weight,
):
    fsdp_size, cp_size = lax.axis_size("fsdp"), lax.axis_size("cp")
    devices = fsdp_size * cp_size
    teams, row_count, width = tokens.shape
    team = cp_size // teams
    mirror = team + team // 2
    block_len = row_count // 2
    chunk = teams * row_count
    token_count = team * chunk
    f = lax.axis_index("fsdp")
    c = lax.axis_index("cp")
    side = c // team
    t = c % team ^ (team // 2 * side)
    q_width = HEADS // team * HEAD_DIM
    copies = team // KV_HEADS
    qkv_width = q_width + 2 * HEAD_DIM
    weight_rows = q_weight.shape[0]
    hidden_cols = gate_weight.shape[1] // team
    team_groups = [[k * team + i for i in range(team)] for k in range(teams)]

    def swap(value, mask):
        return lax.ppermute(value, BOTH, [(i, i ^ mask) for i in range(devices)])

    def turn(value):
        half = team // 2
        return jnp.where(side == 1, jnp.concatenate([value[half:], value[:half]], axis=0), value)

    def to_team(value):
        return turn(lax.all_to_all(turn(value), "cp", 0, 0, axis_index_groups=team_groups, tiled=True))

    def swap_blocks(blocks):
        blocks = jnp.where(f == 1, blocks[:, ::-1], blocks)
        return jnp.where(side == 1, blocks[:, :, ::-1], blocks)

    def turn_second(blocks):
        return jnp.concatenate([blocks[:, :, :1], blocks[:, :, 1:, ::-1]], axis=2)

    def reorder_rows(value):
        blocks = value.reshape(1, 2, 2, 2, width // 8, -1)
        return swap_blocks(turn_second(blocks)).reshape(value.shape)

    def restore(value):
        blocks = value.reshape(-1, 2, 2, 2, width // 8)
        return turn_second(swap_blocks(blocks)).reshape(value.shape)

    def give_rows(value):
        first, second = value[:row_count], value[row_count:]
        mine = jnp.where(side == 0, first, second)
        theirs = swap(jnp.where(side == 0, second, first), mirror)
        return jnp.stack([jnp.where(side == 0, mine, theirs), jnp.where(side == 0, theirs, mine)], axis=0)

    def team_gather(value):
        evens = jnp.concatenate([value] + [swap(value, m) for m in range(2, team, 2)], axis=0)
        return jnp.concatenate([evens, swap(evens, 1)], axis=0)

    def team_reduce(make):
        theirs = swap(make(1), 1)
        evens = (make(0).astype(F32) + theirs.astype(F32)).astype(BF16).reshape(team // 2, chunk, width)
        total = evens[0].astype(F32)
        for m in range(2, team, 2):
            total = total + swap(evens[m // 2], m).astype(F32)
        return total

    def scatter_small(value):
        for bit in reversed(range(devices.bit_length() - 1)):
            mask = 1 << bit
            index = (f * cp_size + c) & mask
            half = value.shape[-1] // 2
            low, high = value[..., :half], value[..., half:]
            theirs = swap(jnp.where(index == 0, high, low), mask)
            value = jnp.where(index == 0, low, high) + theirs
        return value

    def collect(value):
        cols = value.shape[-1]
        blocks = value.reshape(fsdp_size, teams, -1, cols)
        theirs = swap(blocks[1], cp_size)
        blocks = (blocks[0].astype(F32) + theirs.astype(F32)).astype(BF16)
        theirs = swap(blocks[1], mirror)
        own = (blocks[0].astype(F32) + theirs.astype(F32)).astype(BF16)
        return to_team(own.reshape(team, -1, cols))

    def cut(weight):
        return weight.reshape(weight_rows, team, -1).transpose(1, 0, 2)

    def join(pieces):
        return pieces.transpose(1, 0, 2).reshape(pieces.shape[1], -1).astype(F32)

    def sum_heads(pieces):
        grouped = pieces.astype(F32).reshape(KV_HEADS, copies, -1, HEAD_DIM).sum(axis=1)
        return grouped.transpose(1, 0, 2).reshape(grouped.shape[1], -1)

    inverse = np.float32(ROPE_BASE) ** (-(2.0 * np.arange(HALF, dtype=np.float32)) / HEAD_DIM)
    angle = np.arange(token_count).astype(np.float32)[:, None] * inverse.astype(np.float32)[None, :]
    cosine, sine = np.cos(angle), np.sin(angle)
    cos_table = jnp.asarray(np.concatenate([cosine] * 4, axis=-1), F32)
    sin_table = jnp.asarray(np.concatenate([-sine, sine] * 2, axis=-1), F32)

    q_cut, o_cut = (
        weight if weight.shape[1] // team % 128 == 0 else cut(weight) for weight in (q_weight, o_weight)
    )
    heads_of = [weight.reshape(weight_rows, KV_HEADS, HEAD_DIM) for weight in (k_weight, v_weight)]
    kv_cut = jnp.repeat(jnp.concatenate(heads_of, axis=-1).transpose(1, 0, 2), copies, axis=0)
    gains_in = jnp.pad(jnp.stack([attn_gain, ffn_gain]), ((0, 14), (0, 128 - weight_rows)))

    def hbm(*shape):
        return jax.ShapeDtypeStruct(shape, BF16)

    out_shape = (
        jax.ShapeDtypeStruct((chunk, width), F32),
        jax.ShapeDtypeStruct((8, width), F32),
        hbm(team, chunk, width),
        hbm(4, team, weight_rows, q_width),
        hbm(4, team, weight_rows, 2 * HEAD_DIM),
        hbm(q_width, width),
        hbm(token_count, qkv_width),
        hbm(team, chunk, q_width),
        jax.ShapeDtypeStruct((chunk, width), F32),
        hbm(team, chunk, width),
        hbm(team, chunk, width),
        hbm(4, team, weight_rows, hidden_cols),
        hbm(4, team, weight_rows, hidden_cols),
        hbm(4, team, weight_rows, hidden_cols),
        hbm(4, team, weight_rows, width // team),
    )
    spaces = [vmem(), vmem()] + [anywhere()] * 3 + [vmem()] * 4 + [anywhere()] * 6
    outs = pl.pallas_call(
        functools.partial(entry_kernel, fsdp_size, cp_size),
        out_shape=out_shape,
        in_specs=[vmem(), vmem(), vmem()] + [anywhere()] * 6 + [vmem()] * 2,
        out_specs=tuple(spaces),
        scratch_shapes=[
            pltpu.SemaphoreType.DMA((11 * team + 64,)),
            pltpu.SemaphoreType.DMA((11 * team + 64,)),
            pltpu.SemaphoreType.DMA((24,)),
            pltpu.VMEM((row_count, width), BF16),
            pltpu.VMEM((row_count, width), BF16),
            pltpu.VMEM((devices, 16, 128), BF16),
            pltpu.VMEM((chunk, width), BF16),
            pltpu.VMEM((chunk, width), BF16),
            pltpu.VMEM((team, chunk, width), BF16),
            pltpu.VMEM((4, team, weight_rows, q_width), BF16),
            pltpu.VMEM((4, team, weight_rows, 2 * HEAD_DIM), BF16),
            pltpu.VMEM((token_count, q_width), BF16),
            pltpu.VMEM((team, q_width // weight_rows, weight_rows, width // team), BF16),
            pltpu.VMEM((team // 2, chunk, width), BF16),
            pltpu.VMEM((2, team // 4 - 1, chunk, width), BF16),
            pltpu.VMEM((chunk, width), BF16),
            pltpu.VMEM((chunk, width), F32),
        ],
        compiler_params=pltpu.CompilerParams(
            collective_id=0, has_side_effects=True, vmem_limit_bytes=VMEM_BYTES
        ),
        name="entry",
    )(tokens, cotangent, gains_in, q_cut, kv_cut, o_cut, gate_weight, up_weight, down_weight, cos_table, sin_table)
    x_float, gains, attn_in, q_team, kv_team, o_team, rot, mix, resid = outs[:9]
    ffn_in, dy_team, gate_team, up_team, down_team = outs[9:14]
    gain_one, gain_two = gains[0:1], gains[1:2]
    attn_in = attn_in.reshape(token_count, width)
    ffn_in = ffn_in.reshape(token_count, width)
    dy_low = dy_team[0]
    dy_team = dy_team.reshape(token_count, width)
    q_team, kv_team = q_team.reshape(width, q_width), kv_team.reshape(width, 2 * HEAD_DIM)
    gate_team, up_team, down_team = (w.reshape(width, hidden_cols) for w in (gate_team, up_team, down_team))
    mix = mix.reshape(token_count, q_width)

    def f32(*shape):
        return jax.ShapeDtypeStruct(shape, F32)

    def buffers(cols):
        part = (team, weight_rows, cols)
        return hbm(4, *part), hbm(2, *part), hbm(*part), hbm(*part)

    def scratch(*shape, dtype=BF16):
        return pltpu.VMEM(shape, dtype)

    if 2 * hidden_cols == width and KV_HEADS == team:
        half = team // 2
        span = width // team
        sums = [scratch(half, chunk, width), scratch(2, team // 4 - 1, chunk, width), scratch(chunk, width)]
        results = pl.pallas_call(
            functools.partial(exit_kernel, cp_size),
            out_shape=(
                hbm(teams, row_count, width),
                hbm(teams, row_count, width),
                f32(8, 128),
                hbm(team, weight_rows, hidden_cols),
                hbm(team, weight_rows, hidden_cols),
                hbm(team, weight_rows, hidden_cols),
                hbm(team, weight_rows, qkv_width),
                hbm(team, weight_rows, span),
                hbm(team, chunk, width),
                *buffers(hidden_cols),
                *buffers(hidden_cols),
                *buffers(hidden_cols),
                *buffers(qkv_width),
            ),
            in_specs=[vmem()] * 8 + [anywhere()] * 8,
            out_specs=tuple([anywhere()] * 2 + [vmem()] + [anywhere()] * 22),
            scratch_shapes=[
                pltpu.SemaphoreType.DMA((10 * team + 48,)),
                pltpu.SemaphoreType.DMA((10 * team + 48,)),
                pltpu.SemaphoreType.DMA((2 * team + 32,)),
                pltpu.SemaphoreType.DMA((2,)),
                pltpu.SemaphoreType.DMA((2, 2)),
                scratch(token_count, width),
                scratch(token_count, width),
                scratch(width, hidden_cols),
                scratch(width, hidden_cols),
                scratch(width, hidden_cols),
                scratch(width, qkv_width),
                scratch(team, chunk, width),
                scratch(token_count, hidden_cols),
                scratch(token_count, 2 * hidden_cols),
                scratch(2, half, weight_rows, hidden_cols),
                scratch(2, 2, half, weight_rows, hidden_cols),
                *sums,
                *sums,
                scratch(chunk, width, dtype=F32),
                scratch(chunk, width, dtype=F32),
                scratch(chunk, width, dtype=F32),
                scratch(chunk, width),
                scratch(chunk, width),
                scratch(token_count, q_width),
                scratch(token_count, q_width, dtype=F32),
                scratch(token_count, 2 * HEAD_DIM, dtype=F32),
                scratch(token_count, qkv_width),
                scratch(width // 2, span),
                scratch(width // 4, span),
                scratch(width // 4, span),
                scratch(width // 4, span),
                scratch(devices, 8, 128, dtype=F32),
                scratch(devices, 8, 128, dtype=F32),
            ],
            compiler_params=pltpu.CompilerParams(
                collective_id=1, has_side_effects=True, vmem_limit_bytes=63 << 20
            ),
            name="exit",
        )(
            x_float,
            resid,
            gains,
            rot,
            mix.reshape(team, chunk, q_width),
            o_team,
            cos_table,
            sin_table,
            attn_in,
            ffn_in,
            dy_team,
            gate_team,
            up_team,
            down_team,
            q_team,
            kv_team,
        )
        block_out, input_grad, gain_grads, gate_parts, up_parts, down_parts, qkv_parts, o_parts = results[:8]
        def part_spec(cols):
            return pl.BlockSpec((2, weight_rows, cols), lambda step: (step, 0, 0))

        def row_spec(cols):
            return pl.BlockSpec((weight_rows, 2 * cols), lambda step: (0, step))

        def fixed_spec(*shape):
            return pl.BlockSpec(shape, lambda step: (0,) * len(shape))

        kv_width = team * HEAD_DIM
        wide_cols = [q_width, span, hidden_cols, hidden_cols, hidden_cols]
        row_specs = [fixed_spec(teams, row_count, width)] * 2
        joined = pl.pallas_call(
            functools.partial(join_kernel, team, q_width),
            grid=(team // 2,),
            out_shape=tuple(f32(weight_rows, team * cols) for cols in wide_cols)
            + (f32(weight_rows, kv_width), f32(weight_rows, kv_width))
            + (hbm(teams, row_count, width), hbm(teams, row_count, width)),
            in_specs=[fixed_spec(team, weight_rows, qkv_width)]
            + row_specs
            + [part_spec(cols) for cols in wide_cols[1:]],
            out_specs=tuple(row_spec(cols) for cols in wide_cols)
            + (fixed_spec(weight_rows, kv_width), fixed_spec(weight_rows, kv_width))
            + tuple(row_specs),
            compiler_params=pltpu.CompilerParams(vmem_limit_bytes=VMEM_BYTES),
            name="join",
        )(qkv_parts, block_out, input_grad, o_parts, gate_parts, up_parts, down_parts)
        q_out, o_out, gate_out, up_out, down_out, k_out, v_out, block_out, input_grad = joined
        return (
            block_out,
            input_grad,
            gain_grads[0, :weight_rows],
            q_out,
            k_out,
            v_out,
            o_out,
            gain_grads[1, :weight_rows],
            gate_out,
            up_out,
            down_out,
        )

    inv_one = lax.rsqrt(jnp.mean(x_float * x_float, axis=-1, keepdims=True) + NORM_EPS)
    normed_one = x_float * inv_one
    inv_two = lax.rsqrt(jnp.mean(resid * resid, axis=-1, keepdims=True) + NORM_EPS)
    normed_two = resid * inv_two

    gate = dot(ffn_in, gate_team)
    up_val = dot(ffn_in, up_team)
    sigma = jax.nn.sigmoid(gate)
    silu_val = gate * sigma
    hidden = (silu_val * up_val).astype(BF16)
    hidden_grad = dot(dy_team, down_team)
    gate_grad = (hidden_grad * up_val * (sigma + gate * sigma * (1.0 - sigma))).astype(BF16)
    up_grad = (hidden_grad * silu_val).astype(BF16)

    half = token_count // 2

    def half_of(value, odd):
        return value[half * odd : half * (odd + 1)]

    ffn_in_grad = team_reduce(
        lambda odd: (
            contract_cols(half_of(gate_grad, odd), gate_team) + contract_cols(half_of(up_grad, odd), up_team)
        ).astype(BF16)
    )
    down_sum = team_reduce(lambda odd: contract_cols(half_of(hidden, odd), down_team).astype(BF16))
    block_out = give_rows(restore((resid + down_sum).astype(BF16)))

    ffn_gain_grad = scatter_small(restore(jnp.sum(ffn_in_grad * normed_two, axis=0)))
    scaled_two = ffn_in_grad * gain_two
    resid_grad = dy_low.astype(F32) + inv_two * (
        scaled_two - normed_two * jnp.mean(scaled_two * normed_two, axis=-1, keepdims=True)
    )
    branch_grad = team_gather(resid_grad.astype(BF16))
    mix_grad = contract_cols(branch_grad, o_team).astype(BF16).reshape(team, chunk, q_width)

    down_weight_grad = join(collect(contract_rows(dy_team, hidden).astype(BF16)))
    gate_weight_grad = join(collect(contract_rows(ffn_in, gate_grad).astype(BF16)))
    up_weight_grad = join(collect(contract_rows(ffn_in, up_grad).astype(BF16)))

    proj_grad = pl.pallas_call(
        functools.partial(attention_backward, team, block_len, q_width),
        out_shape=jax.ShapeDtypeStruct((token_count, qkv_width), BF16),
        in_specs=[smem(), vmem(), vmem(), vmem(), vmem()],
        out_specs=vmem(),
        scratch_shapes=[
            pltpu.VMEM((token_count, q_width), BF16),
            pltpu.VMEM((token_count, q_width), F32),
            pltpu.VMEM((token_count, 2 * HEAD_DIM), F32),
        ],
        compiler_params=pltpu.CompilerParams(vmem_limit_bytes=VMEM_BYTES),
        name="attention_backward",
    )(t.astype(jnp.int32).reshape(1), rot, mix_grad, cos_table, sin_table)

    qkv_team = jnp.concatenate([q_team, kv_team], axis=-1)
    attn_in_grad = team_reduce(lambda odd: contract_cols(half_of(proj_grad, odd), qkv_team).astype(BF16))
    attn_gain_grad = scatter_small(restore(jnp.sum(attn_in_grad * normed_one, axis=0)))
    scaled_one = attn_in_grad * gain_one
    input_grad = resid_grad + inv_one * (
        scaled_one - normed_one * jnp.mean(scaled_one * normed_one, axis=-1, keepdims=True)
    )
    input_grad = give_rows(restore(input_grad.astype(BF16)))

    qkv_grad = collect(contract_rows(attn_in, proj_grad).astype(BF16))
    q_weight_grad = join(qkv_grad[:, :, :q_width])
    k_weight_grad = sum_heads(qkv_grad[:, :, q_width : q_width + HEAD_DIM])
    v_weight_grad = sum_heads(qkv_grad[:, :, q_width + HEAD_DIM :])

    o_grad = restore(contract_rows(mix, branch_grad)).astype(BF16)
    o_grad = to_team(o_grad.reshape(q_width, team, -1).transpose(1, 0, 2)).reshape(width, -1)
    o_weight_grad = join(collect(reorder_rows(o_grad)))

    return (
        block_out,
        input_grad,
        attn_gain_grad,
        q_weight_grad,
        k_weight_grad,
        v_weight_grad,
        o_weight_grad,
        ffn_gain_grad,
        gate_weight_grad,
        up_weight_grad,
        down_weight_grad,
    )


def solution(mesh):
    rows = P(BOTH, None)
    placed = P("fsdp", "cp", None)
    gain = P(BOTH)
    return jax.shard_map(
        body,
        mesh=mesh,
        in_specs=(placed, placed, gain, rows, rows, rows, rows, gain, rows, rows, rows),
        out_specs=(placed, placed, gain, rows, rows, rows, rows, gain, rows, rows, rows),
        check_vma=False,
    )
```
